32 devices in a mesh: img: 8 (over y, x, core), patch: 4 (over z).
Axes of the slice: x: 2, y: 2, z: 4, core: 2. Of those that a mesh axis runs over, the one named last changes fastest.
Arguments:
- tokens: bfloat16 [4, 8, 324, 512], P(None, 'img', 'patch')
- cotangent: bfloat16 [4, 8, 324, 512], P(None, 'img', 'patch'), may hold values from -6 to 6
- patch_count: int32 [4, 8], P(None, 'img'), may hold values from 100 to 324, as said below
- crop_index: int32 [4, 8, 324], P(None, 'img'), may hold values from 0 to 323, as said below
- in_weight: float32 [512, 3072], P('patch'), may hold values from -0.25 to 0.25
- in_moment: float32 [512, 3072], P('patch'), may hold values from -320 to 320
- in_average: float32 [512, 3072], P('patch'), may hold values from -0.25 to 0.25
- out_weight: float32 [1536, 512], P('patch'), may hold values from -0.3125 to 0.3125
- out_moment: float32 [1536, 512], P('patch'), may hold values from -256 to 256
- out_average: float32 [1536, 512], P('patch'), may hold values from -0.3125 to 0.3125
- spatial_weight: float32 [324, 324], P('patch'), may hold values from -0.3125 to 0.3125
- spatial_moment: float32 [324, 324], P('patch'), may hold values from -640 to 640
- spatial_average: float32 [324, 324], P('patch'), may hold values from -0.3125 to 0.3125
- vectors: float32 [8004], replicated
- vector_moment: float32 [8004], replicated, may hold values from -512 to 512
- vector_average: float32 [8004], replicated
Outputs:
- out_tokens: bfloat16 [4, 8, 324, 512], P(None, 'img', 'patch')
- in_grad: float32 [4, 8, 324, 512], P(None, 'img', 'patch')
- in_weight_new: float32 [512, 3072], P('patch')
- in_moment_new: float32 [512, 3072], P('patch')
- in_average_new: float32 [512, 3072], P('patch')
- out_weight_new: float32 [1536, 512], P('patch')
- out_moment_new: float32 [1536, 512], P('patch')
- out_average_new: float32 [1536, 512], P('patch')
- spatial_weight_new: float32 [324, 324], P('patch')
- spatial_moment_new: float32 [324, 324], P('patch')
- spatial_average_new: float32 [324, 324], P('patch')
- vectors_new: float32 [8004], replicated
- vector_moment_new: float32 [8004], replicated
- vector_average_new: float32 [8004], replicated
The draws below stay inside these ranges and needn't reach their ends.
Inputs may be any that keep to these rules, and one draw needn't show every extreme that they name: `patch_count`: each image has 100, 196 or 324 patches, a square grid of side 10, 14 or 18; every micro-batch holds an image of 324 patches. `crop_index`: for an image of n patches, entries 0 to n - 1 are the cells of a square window of the 18 x 18 grid, row by row, as row * 18 + column; later entries are unused.
All inputs are finite; a program needn't handle non-finite values.
Results may differ from the reference program's by a relative error of at most 0.008.
Values may be sent and summed in bfloat16 or wider, within the bound.
No kernel may reach another device: no remote copies, remote signals or barrier semaphores. Data moves between devices by JAX's collectives and lax.ppermute only.
A program may use at most 192 MiB of HBM per device.

```python
import math
import jax
import jax.numpy as jnp
from jax import lax

D = 512
FF = 3072
GH = 1536
GRID = 18
PMAX = 324
MICRO = 4
SLOTS = 8
VEC = 8004
N_PATCH = 4


def side_law(key):
    keys = jax.random.split(jax.random.fold_in(key, 11), 2)
    kinds = jax.random.randint(keys[0], (MICRO, SLOTS), 0, 3)
    spots = jax.random.randint(keys[1], (MICRO,), 0, SLOTS)
    kinds = jnp.where(jnp.arange(SLOTS)[None, :] == spots[:, None], 2, kinds)
    return 10 + 4 * kinds


def draw_patch_count(key, part):
    sides = side_law(key)
    return (sides * sides).astype(jnp.int32)


def draw_crop_index(key, part):
    sides = side_law(key)
    keys = jax.random.split(jax.random.fold_in(key, 23), 3)
    top_row = jax.random.randint(keys[0], (MICRO, SLOTS), 0, GRID - sides + 1)
    left_col = jax.random.randint(keys[1], (MICRO, SLOTS), 0, GRID - sides + 1)
    spare = jax.random.randint(keys[2], (MICRO, SLOTS, PMAX), 0, PMAX)
    cell_ids = jnp.arange(PMAX)[None, None, :]
    side_cols = sides[:, :, None]
    window = (top_row[:, :, None] + cell_ids // side_cols) * GRID + left_col[:, :, None] + cell_ids % side_cols
    return jnp.where(cell_ids < side_cols * side_cols, window, spare).astype(jnp.int32)


def draw_tokens(key, part):
    keys = jax.random.split(jax.random.fold_in(key, 31), 3)
    row_scale = jnp.exp(jax.random.uniform(keys[0], (MICRO, SLOTS, PMAX, 1), jnp.float32, -1.15, 1.15))
    col_scale = jnp.exp(jax.random.uniform(keys[1], (D,), jnp.float32, -1.15, 1.15))
    base = jax.random.normal(keys[2], (MICRO, SLOTS, PMAX, D), jnp.float32)
    return (base * row_scale * col_scale).astype(jnp.bfloat16)


def vector_law(key, salt):
    keys = jax.random.split(jax.random.fold_in(key, salt), 7)
    gain_one = 1.0 + jax.random.uniform(keys[0], (D,), jnp.float32, -0.3, 0.3)
    shift_one = 0.2 * jax.random.normal(keys[1], (D,), jnp.float32)
    bias_in = 0.2 * jax.random.normal(keys[2], (FF,), jnp.float32)
    gain_two = 1.0 + jax.random.uniform(keys[3], (GH,), jnp.float32, -0.3, 0.3)
    shift_two = 0.2 * jax.random.normal(keys[4], (GH,), jnp.float32)
    bias_mix = 0.3 * jax.random.normal(keys[5], (PMAX,), jnp.float32)
    bias_out = 0.2 * jax.random.normal(keys[6], (D,), jnp.float32)
    return jnp.concatenate([gain_one, shift_one, bias_in, gain_two, shift_two, bias_mix, bias_out])


def draw_vectors(key, part):
    return vector_law(key, 5)


def draw_vector_average(key, part):
    return vector_law(key, 9)


def block_levels(own_key, shape, cuts, low, top_value):
    def one(dim, blocks):
        heights = jax.random.uniform(jax.random.fold_in(jax.random.fold_in(own_key, 6), dim), (blocks,), jnp.float32, low / len(cuts), top_value / len(cuts))
        return jnp.repeat(jnp.exp(heights), shape[dim] // blocks).reshape((-1,) + (1,) * (len(shape) - dim - 1))

    loudness = one(*cuts[0])
    for cut in cuts[1:]:
        loudness = loudness * one(*cut)
    return loudness


def bell_draw(own_key, extent, spread, reach, cuts=(), kind=jnp.bfloat16):
    entries = jax.random.normal(own_key, extent, jnp.float32) * spread
    if len(cuts) > 0:
        entries = block_levels(own_key, extent, cuts, -0.22, 0.18) * entries
    return jnp.clip(entries, min=-reach, max=reach).astype(kind)


def setup_inputs(seed: int = 0) -> dict:
    seeds = jax.random.split(jax.random.key(seed), 17)
    tokens = draw_tokens(jax.random.fold_in(seeds[16], 71), 0)
    cotangent = bell_draw(seeds[1], (MICRO, SLOTS, PMAX, D), 1.0, 6.0, ((1, 8), (2, 4)))
    patch_count = draw_patch_count(jax.random.fold_in(seeds[16], 71), 0)
    crop_index = draw_crop_index(jax.random.fold_in(seeds[16], 71), 0)
    in_weight = bell_draw(seeds[4], (D, FF), D ** -0.5, 0.25, ((0, 4),), jnp.float32)
    in_moment = bell_draw(seeds[5], (D, FF), (0.7 * (207 * MICRO * SLOTS) ** 0.5), 320.0, ((0, 4),), jnp.float32)
    in_average = bell_draw(seeds[6], (D, FF), D ** -0.5, 0.25, ((0, 4),), jnp.float32)
    out_weight = bell_draw(seeds[7], (GH, D), (GH // 4) ** -0.5, 0.3125, ((0, 4),), jnp.float32)
    out_moment = bell_draw(seeds[8], (GH, D), (0.6 * (207 * MICRO * SLOTS) ** 0.5), 256.0, ((0, 4),), jnp.float32)
    out_average = bell_draw(seeds[9], (GH, D), (GH // 4) ** -0.5, 0.3125, ((0, 4),), jnp.float32)
    spatial_weight = bell_draw(seeds[10], (PMAX, PMAX), PMAX ** -0.5, 0.3125, ((0, 4),), jnp.float32)
    spatial_moment = bell_draw(seeds[11], (PMAX, PMAX), (0.75 * (GH * MICRO * SLOTS // 2) ** 0.5), 640.0, ((0, 4),), jnp.float32)
    spatial_average = bell_draw(seeds[12], (PMAX, PMAX), PMAX ** -0.5, 0.3125, ((0, 4),), jnp.float32)
    vectors = draw_vectors(jax.random.fold_in(seeds[16], 71), 0)
    vector_moment = bell_draw(seeds[14], (VEC,), ((207 * MICRO * SLOTS) ** 0.5), 512.0, (), jnp.float32)
    vector_average = draw_vector_average(jax.random.fold_in(seeds[16], 71), 0)
    return dict(tokens=tokens, cotangent=cotangent, patch_count=patch_count, crop_index=crop_index, in_weight=in_weight, in_moment=in_moment, in_average=in_average, out_weight=out_weight, out_moment=out_moment, out_average=out_average, spatial_weight=spatial_weight, spatial_moment=spatial_moment, spatial_average=spatial_average, vectors=vectors, vector_moment=vector_moment, vector_average=vector_average)


EPS = 1e-05
MOMENTUM = 0.9
AVG_DECAY = 0.8

@jax.custom_vjp
def low(v):
    return lax.optimization_barrier(v.astype(jnp.bfloat16)).astype(jnp.float32)

@jax.custom_vjp
def low_back(v):
    return v

def low_keep(v):
    return (low(v), None)

def low_pass(kept, grad):
    return (grad,)

def back_keep(v):
    return (v, None)

def back_low(kept, grad):
    return (low(grad),)
low.defvjp(low_keep, low_pass)
low_back.defvjp(back_keep, back_low)

def layer_norm(values, gain_vec, shift_vec):
    row_mean = lax.optimization_barrier(jnp.mean(values, axis=-1, keepdims=True))
    centered = values - row_mean
    variance = lax.optimization_barrier(jnp.mean(centered * centered, axis=-1, keepdims=True))
    return centered * lax.rsqrt(variance + EPS) * gain_vec + shift_vec

def exact_gelu(values):
    return jax.nn.gelu(values, approximate=False)

def split_vectors(vectors, model_width, hidden_width, gate_width, cell_count):
    bounds = [model_width, model_width, hidden_width, gate_width, gate_width, cell_count, model_width]
    pieces = []
    offset = 0
    for length in bounds:
        pieces.append(vectors[offset:offset + length])
        offset = offset + length
    return pieces

def step_rates(images, model_width, gate_width, cell_count):
    live_rows = 207.0 * images
    rate_in = 1.0 / (math.sqrt(model_width) * 1.4 * math.sqrt(live_rows))
    rate_out = 1.0 / (math.sqrt(gate_width / 4.0) * 1.2 * math.sqrt(live_rows))
    rate_mix = 1.0 / (math.sqrt(cell_count) * 1.5 * math.sqrt(gate_width * images / 2.0))
    rate_vec = 0.1 / (2.0 * math.sqrt(live_rows))
    return (rate_in, rate_out, rate_mix, rate_vec)

def nesterov(weight, grads, moment, average, rate):
    moment_new = MOMENTUM * moment + grads
    weight_new = weight - rate * (grads + MOMENTUM * moment_new)
    average_new = AVG_DECAY * average + (1.0 - AVG_DECAY) * weight_new
    return (weight_new, moment_new, average_new)

def image_layout(count, crop_row):
    row_count = PMAX // N_PATCH
    per_shard = count // N_PATCH
    slot_ids = jnp.arange(PMAX, dtype=jnp.int32)
    within = slot_ids % row_count
    live_mask = within < per_shard
    order_ids = jnp.clip(slot_ids // row_count * per_shard + within, 0, PMAX - 1).astype(jnp.int32)
    positions = jnp.where(live_mask, crop_row[order_ids], 0).astype(jnp.int32)
    return (live_mask, positions)

def forward(params, tokens, counts, crops):
    in_weight, out_weight, mix_weight, vectors = params
    gain_one, shift_one, bias_in, gain_two, shift_two, bias_mix, bias_out = split_vectors(vectors, D, FF, GH, PMAX)
    live_mask, positions = jax.vmap(image_layout)(counts, crops)
    high = lax.Precision.HIGHEST
    normed = layer_norm(tokens, gain_one, shift_one)
    pre_act = low_back(jnp.einsum('gsd,df->gsf', low(normed), low(in_weight), precision=high) + bias_in)
    activated = exact_gelu(pre_act)
    left_half = activated[..., :GH]
    right_low = low(layer_norm(activated[..., GH:], gain_two, shift_two))
    mix_low = low(mix_weight)
    col_mask = live_mask.astype(jnp.float32)
    mixing = mix_low[positions[:, :, None], positions[:, None, :]] * col_mask[:, None, :]
    spatial = low_back(jnp.einsum('gst,gtc->gsc', mixing, right_low, precision=high) + bias_mix[positions][:, :, None])
    gated = low(left_half * spatial)
    branch = jnp.einsum('gsc,cd->gsd', gated, low(out_weight), precision=high) + bias_out
    return jnp.where(live_mask[:, :, None], tokens + branch, 0.0)

def reference(tokens, cotangent, patch_count, crop_index, in_weight, in_moment, in_average, out_weight, out_moment, out_average, spatial_weight, spatial_moment, spatial_average, vectors, vector_moment, vector_average):
    images = MICRO * SLOTS
    group_size = math.gcd(images, 8)
    group_count = images // group_size
    tok_groups = tokens.reshape(group_count, group_size, PMAX, D)
    cot_groups = cotangent.reshape(group_count, group_size, PMAX, D)
    count_groups = patch_count.reshape(group_count, group_size)
    crop_groups = crop_index.reshape(group_count, group_size, PMAX)
    params = (in_weight, out_weight, spatial_weight, vectors)
    zero_grads = tuple((jnp.zeros_like(item) for item in params))

    def one_group(carry, block):
        tok_block, cot_block, count_block, crop_block = block

        def local_fn(prm, tok_vals):
            return forward(prm, tok_vals, count_block, crop_block)
        result, pullback = jax.vjp(local_fn, params, tok_block.astype(jnp.float32))
        param_grads, token_grad = pullback(cot_block.astype(jnp.float32))
        carry = tuple((left_val + right_val for left_val, right_val in zip(carry, param_grads)))
        return (carry, (result.astype(jnp.bfloat16), token_grad))
    grads, outputs = lax.scan(one_group, zero_grads, (tok_groups, cot_groups, count_groups, crop_groups))
    out_tokens = outputs[0].reshape(MICRO, SLOTS, PMAX, D)
    in_grad = outputs[1].reshape(MICRO, SLOTS, PMAX, D)
    rate_in, rate_out, rate_mix, rate_vec = step_rates(images, D, GH, PMAX)
    in_new = nesterov(in_weight, grads[0], in_moment, in_average, rate_in)
    out_new = nesterov(out_weight, grads[1], out_moment, out_average, rate_out)
    mix_new = nesterov(spatial_weight, grads[2], spatial_moment, spatial_average, rate_mix)
    vec_new = nesterov(vectors, grads[3], vector_moment, vector_average, rate_vec)
    return (out_tokens, in_grad, in_new[0], in_new[1], in_new[2], out_new[0], out_new[1], out_new[2], mix_new[0], mix_new[1], mix_new[2], vec_new[0], vec_new[1], vec_new[2])
```

```python
import math

import jax
import jax.numpy as jnp
from jax import lax
from jax.sharding import PartitionSpec as P

EPS = 1e-05
MOMENTUM = 0.9
AVG_DECAY = 0.8
BF = jnp.bfloat16
F32 = jnp.float32


def step_rates(images, model_width, gate_width, cell_count):
    live_rows = 207.0 * images
    rate_in = 1.0 / (math.sqrt(model_width) * 1.4 * math.sqrt(live_rows))
    rate_out = 1.0 / (math.sqrt(gate_width / 4.0) * 1.2 * math.sqrt(live_rows))
    rate_mix = 1.0 / (math.sqrt(cell_count) * 1.5 * math.sqrt(gate_width * images / 2.0))
    rate_vec = 0.1 / (2.0 * math.sqrt(live_rows))
    return (rate_in, rate_out, rate_mix, rate_vec)


def nesterov(weight, grads, moment, average, rate):
    moment_new = MOMENTUM * moment + grads
    weight_new = weight - rate * (grads + MOMENTUM * moment_new)
    average_new = AVG_DECAY * average + (1.0 - AVG_DECAY) * weight_new
    return (weight_new, moment_new, average_new)


def xor_pairs(n, mask):
    return [(k, k ^ mask) for k in range(n)]


def turn(arr, r):
    n = lax.axis_size("patch")
    if r % n == 0:
        return arr
    return lax.ppermute(arr, "patch", [(s, (s + r) % n) for s in range(n)])


def swap(arr, mask):
    return lax.ppermute(arr, "img", xor_pairs(lax.axis_size("img"), mask))


def own_bit(mask):
    return (lax.axis_index("img") & mask) != 0


def join(arr, mask, axis):
    other = swap(arr, mask)
    bit = own_bit(mask)
    return jnp.concatenate([jnp.where(bit, other, arr), jnp.where(bit, arr, other)], axis)


def halve(arr, mask, axis):
    half = arr.shape[axis] // 2
    low = lax.slice_in_dim(arr, 0, half, axis=axis)
    high = lax.slice_in_dim(arr, half, 2 * half, axis=axis)
    bit = own_bit(mask)
    keep = jnp.where(bit, high, low).astype(F32)
    got = swap(jnp.where(bit, low, high).astype(BF), mask)
    return keep + got.astype(F32)


CORE, XBIT, YBIT = 1, 2, 4


def gather_shards(shard):
    rows, cols = shard.shape
    unit = rows // 8
    u = lax.axis_index("img") % 8
    piece = lax.dynamic_slice_in_dim(shard, u * unit, unit, 0)
    got = jnp.stack([turn(piece, r) for r in (1, 2, 3)]).reshape(3, 1, 1, 1, unit, cols)
    half = cols // 2
    left, right = got[..., :half], got[..., half:]
    left = join(left, XBIT, 2)
    right = join(right, YBIT, 1)
    left = join(left, YBIT, 1)
    right = join(right, XBIT, 2)
    both = jnp.concatenate([left, right], axis=-1)
    both = join(both, CORE, 3)
    return jnp.concatenate([shard[None], both.reshape(3, rows, cols)])


def to_absolute(rel):
    p = lax.axis_index("patch")
    flipped = rel[::-1]
    twice = jnp.concatenate([flipped, flipped])
    return lax.dynamic_slice_in_dim(twice, (3 - p) % 4, 4, 0)


def reduce_shards(grad):
    n, rows, cols = grad.shape
    unit = rows // 8
    p = lax.axis_index("patch")
    g = grad.reshape(n, 2, 2, 2, unit, cols)
    g = halve(g, CORE, 3).astype(BF)
    half = cols // 2
    left, right = g[..., :half], g[..., half:]
    left = halve(left, XBIT, 2).astype(BF)
    right = halve(right, YBIT, 1).astype(BF)
    left = halve(left, YBIT, 1)
    right = halve(right, XBIT, 2)
    g = jnp.concatenate([left, right], axis=-1)
    mask = 8
    while mask < lax.axis_size("img"):
        g = g + swap(g, mask)
        mask = mask * 2
    mine = lax.dynamic_slice_in_dim(g, p, 1, 0)
    for r in (1, 2, 3):
        away = lax.dynamic_slice_in_dim(g, (p + r) % 4, 1, 0).astype(BF)
        mine = mine + turn(away, r).astype(F32)
    mine = mine.astype(BF)
    left, right = mine[..., :half], mine[..., half:]
    left = join(left, YBIT, 1)
    right = join(right, XBIT, 2)
    left = join(left, XBIT, 2)
    right = join(right, YBIT, 1)
    whole = join(jnp.concatenate([left, right], axis=-1), CORE, 3)
    return whole.reshape(rows, cols).astype(F32)


def all_sum(arr):
    mask = 1
    while mask < lax.axis_size("img"):
        arr = arr + swap(arr, mask)
        mask = mask * 2
    for mask in (1, 2):
        arr = arr + lax.ppermute(arr, "patch", xor_pairs(4, mask))
    return arr


def dot(a, b, ca, cb):
    return lax.dot_general(a, b, (((ca,), (cb,)), ((), ())), preferred_element_type=F32)


def shards(
    tokens,
    cotangent,
    patch_count,
    crop_index,
    in_weight,
    in_moment,
    in_average,
    out_weight,
    out_moment,
    out_average,
    spatial_weight,
    spatial_moment,
    spatial_average,
    vectors,
    vector_moment,
    vector_average,
):
    p = lax.axis_index("patch")
    nz = lax.axis_size("patch")
    micro_count, slot_count, row_count, width = tokens.shape
    assert micro_count == nz == 4 and slot_count == 1
    hidden = in_weight.shape[1]
    gate = hidden // 2
    cells = spatial_weight.shape[1]
    grid = math.isqrt(cells)

    in_low = to_absolute(gather_shards(in_weight.astype(BF))).reshape(width, hidden)
    mix_rows = spatial_weight.shape[0]
    mix_pad = 128
    mixed = jnp.pad(spatial_weight.astype(BF), ((0, mix_pad - mix_rows), (0, width - cells)))
    out_rows = out_weight.shape[0]
    second = jnp.concatenate(
        [out_weight.astype(BF).reshape(8, out_rows // 8, width), mixed.reshape(8, mix_pad // 8, width)], axis=1
    ).reshape(out_rows + mix_pad, width)
    second = to_absolute(gather_shards(second)).reshape(4, 8, (out_rows + mix_pad) // 8, width)
    out_low = second[:, :, : out_rows // 8].reshape(gate, width)
    mix_low = second[:, :, out_rows // 8 :].reshape(4, mix_pad, width)[:, :mix_rows, :cells].reshape(cells, cells)

    def collect(arr):
        return jnp.concatenate(
            [turn(lax.dynamic_index_in_dim(arr, (p + r) % 4, 0, keepdims=False)[0], r) for r in range(4)]
        )

    count = lax.dynamic_index_in_dim(patch_count, p, 0, keepdims=False)[0]
    first = lax.dynamic_index_in_dim(crop_index, p, 0, keepdims=False)[0, 0]
    quarter = count // 4
    side = jnp.round(jnp.sqrt(count.astype(F32))).astype(jnp.int32)
    place = jnp.arange(cells, dtype=jnp.int32)
    drow = place // grid - first // grid
    dcol = place % grid - first % grid
    inside = (drow >= 0) & (drow < side) & (dcol >= 0) & (dcol < side)
    order = drow * side + dcol
    block = (
        (order >= quarter).astype(jnp.int32)
        + (order >= 2 * quarter).astype(jnp.int32)
        + (order >= 3 * quarter).astype(jnp.int32)
    )
    slot = ((p - block) % 4) * row_count + order - block * quarter
    slot = jnp.where(inside, slot, -1)
    onehot = (slot[:, None] == jnp.arange(cells, dtype=jnp.int32)[None, :]).astype(BF)
    live = inside[:, None]

    tok_low = dot(onehot, collect(tokens), 1, 0).astype(BF)
    cot_low = dot(onehot, collect(cotangent), 1, 0).astype(BF)

    bounds = [width, width, hidden, gate, gate, cells, width]
    pieces = []
    offset = 0
    for length in bounds:
        pieces.append(vectors[offset : offset + length])
        offset += length
    gain_one, shift_one, bias_in, gain_two, shift_two, bias_mix, bias_out = pieces

    x = tok_low.astype(F32)
    mean1 = jnp.mean(x, -1, keepdims=True)
    cen1 = x - mean1
    rstd1 = lax.rsqrt(jnp.mean(cen1 * cen1, -1, keepdims=True) + EPS)
    xhat = cen1 * rstd1
    xn = (xhat * gain_one + shift_one).astype(BF)
    pre = dot(xn, in_low, 1, 0) + bias_in
    phi = 0.5 * (1.0 + lax.erf(pre * math.sqrt(0.5)))
    slope = phi + pre * jnp.exp(-0.5 * pre * pre) * (1.0 / math.sqrt(2.0 * math.pi))
    act = pre * phi
    u = act[:, :gate]
    v = act[:, gate:]
    mean2 = jnp.mean(v, -1, keepdims=True)
    cen2 = v - mean2
    rstd2 = lax.rsqrt(jnp.mean(cen2 * cen2, -1, keepdims=True) + EPS)
    vhat = cen2 * rstd2
    vn = jnp.where(live, vhat * gain_two + shift_two, 0.0).astype(BF)
    spatial = dot(mix_low, vn, 1, 0) + bias_mix[:, None]
    gated = (u * spatial).astype(BF)
    branch = dot(gated, out_low, 1, 0) + bias_out
    out_pos = jnp.where(live, x + branch, 0.0).astype(BF)

    grad_out = dot(gated, cot_low, 0, 0)
    gated_grad = dot(cot_low, out_low, 1, 1)
    spatial_grad = (gated_grad * u).astype(BF)
    u_grad = gated_grad * spatial
    grad_mix = dot(spatial_grad, vn, 1, 1)
    vn_grad = jnp.where(live, dot(mix_low, spatial_grad, 0, 0), 0.0)
    h = vn_grad * gain_two
    v_grad = rstd2 * (h - jnp.mean(h, -1, keepdims=True) - vhat * jnp.mean(h * vhat, -1, keepdims=True))
    pre_grad = (jnp.concatenate([u_grad, v_grad], axis=1) * slope).astype(BF)
    grad_in = dot(xn, pre_grad, 0, 0)
    xn_grad = dot(pre_grad, in_low, 1, 1)
    h1 = xn_grad * gain_one
    x_grad = rstd1 * (h1 - jnp.mean(h1, -1, keepdims=True) - xhat * jnp.mean(h1 * xhat, -1, keepdims=True))
    in_pos = jnp.where(live, cot_low.astype(F32) + x_grad, 0.0).astype(BF)

    grad_vec = jnp.concatenate(
        [
            jnp.sum(xn_grad * xhat, 0),
            jnp.sum(xn_grad, 0),
            jnp.sum(pre_grad.astype(F32), 0),
            jnp.sum(vn_grad * vhat, 0),
            jnp.sum(vn_grad, 0),
            jnp.sum(spatial_grad.astype(F32), 1),
            jnp.sum(cot_low.astype(F32), 0),
        ]
    )

    def spread(pos, kind):
        slots = dot(onehot, pos, 0, 0).astype(BF).reshape(4, row_count, width)
        back = jnp.stack([turn(slots[r], -r) for r in range(4)])
        twice = jnp.concatenate([back, back])
        return lax.dynamic_slice_in_dim(twice, (4 - p) % 4, 4, 0).astype(kind).reshape(tokens.shape)

    out_tokens = spread(out_pos, BF)
    in_grad = spread(in_pos, F32)

    mix_part = jnp.pad(
        grad_mix.reshape(4, mix_rows, cells), ((0, 0), (0, mix_pad - mix_rows), (0, width - cells))
    )
    packed = jnp.concatenate(
        [grad_out.astype(BF).reshape(4, 8, out_rows // 8, width), mix_part.astype(BF).reshape(4, 8, mix_pad // 8, width)],
        axis=2,
    ).reshape(4, out_rows + mix_pad, width)
    second_sum = reduce_shards(packed).reshape(8, (out_rows + mix_pad) // 8, width)
    out_share = second_sum[:, : out_rows // 8].reshape(out_rows, width)
    mix_share = second_sum[:, out_rows // 8 :].reshape(mix_pad, width)[:mix_rows, :cells]
    in_share = reduce_shards(grad_in.astype(BF).reshape(4, width // 4, hidden))
    vec_sum = all_sum(grad_vec)

    images = micro_count * slot_count * lax.axis_size("img")
    rate_in, rate_out, rate_mix, rate_vec = step_rates(images, width, gate, cells)
    in_new = nesterov(in_weight, in_share, in_moment, in_average, rate_in)
    out_new = nesterov(out_weight, out_share, out_moment, out_average, rate_out)
    mix_new = nesterov(spatial_weight, mix_share, spatial_moment, spatial_average, rate_mix)
    vec_new = nesterov(vectors, vec_sum, vector_moment, vector_average, rate_vec)
    return (out_tokens, in_grad, *in_new, *out_new, *mix_new, *vec_new)


def solution(mesh):
    rows = P("patch", None)
    act = P(None, "img", "patch", None)
    return jax.shard_map(
        shards,
        mesh=mesh,
        in_specs=(act, act, P(None, "img"), P(None, "img", None), *([rows] * 9), P(), P(), P()),
        out_specs=(act, act, *([rows] * 9), P(), P(), P()),
        check_vma=False,
    )
```

```python
import functools
import math

import jax
import jax.numpy as jnp
from jax import lax
from jax.experimental import pallas as pl
from jax.experimental.pallas import tpu as pltpu
from jax.sharding import PartitionSpec as P

EPS = 1e-05
MOMENTUM = 0.9
AVG_DECAY = 0.8
BF = jnp.bfloat16
F32 = jnp.float32
I32 = jnp.int32
CORE, XBIT, YBIT = 1, 2, 4
LANE = 512
STEP = 16


def step_rates(images, model_width, gate_width, cell_count):
    live_rows = 207.0 * images
    rate_in = 1.0 / (math.sqrt(model_width) * 1.4 * math.sqrt(live_rows))
    rate_out = 1.0 / (math.sqrt(gate_width / 4.0) * 1.2 * math.sqrt(live_rows))
    rate_mix = 1.0 / (math.sqrt(cell_count) * 1.5 * math.sqrt(gate_width * images / 2.0))
    rate_vec = 0.1 / (2.0 * math.sqrt(live_rows))
    return (rate_in, rate_out, rate_mix, rate_vec)


def nesterov(weight, grads, moment, average, rate):
    moment_new = MOMENTUM * moment + grads
    weight_new = weight - rate * (grads + MOMENTUM * moment_new)
    average_new = AVG_DECAY * average + (1.0 - AVG_DECAY) * weight_new
    return (weight_new, moment_new, average_new)


def turn(arr, r):
    n = lax.axis_size("patch")
    return lax.ppermute(arr, "patch", [(s, (s + r) % n) for s in range(n)])


def swap(arr, mask):
    n = lax.axis_size("img")
    return lax.ppermute(arr, "img", [(k, k ^ mask) for k in range(n)])


def dot(a, b, ca=1, cb=0):
    return lax.dot_general(a, b, (((ca,), (cb,)), ((), ())), preferred_element_type=F32)


def aligned(v, by):
    return pl.multiple_of(v, by)


def rows_of(i):
    return pl.ds(aligned(i * STEP, STEP), STEP)


def each_tile(n):
    steps = n // STEP
    return pl.loop(0, steps, unroll=7 if steps % 7 == 0 else 1)


def gelu_parts(pre):
    phi = 0.5 * (1.0 + lax.erf(pre * math.sqrt(0.5)))
    slope = phi + pre * (jnp.exp(-0.5 * pre * pre) * (1.0 / math.sqrt(2.0 * math.pi)))
    return pre * phi, slope


def mean_rows(v):
    return jnp.sum(v, axis=-1, keepdims=True) * (1.0 / v.shape[-1])


def onehot(slot, lanes, base):
    lane = lax.broadcasted_iota(I32, (slot.shape[0], lanes), 1) + base
    return jnp.where(slot == lane, 1.0, 0.0).astype(BF)


def prep_kernel(scal, tok, cot, weight, mix, m1, m2, m3, tok_own, c1, c2, c3, cot_own, wo_own, mx_own):
    own, unit = scal[0], scal[1]
    rows = weight.shape[0] // 8
    wo_own[...] = weight[...].astype(BF)
    mx_own[...] = jnp.zeros_like(mx_own)
    mx_own[0 : mix.shape[0], 0 : mix.shape[1]] = mix[...].astype(BF)
    piece = weight[pl.ds(aligned(unit * rows, STEP), rows), :].astype(BF)
    strip = mx_own[pl.ds(aligned(unit * STEP, STEP), STEP), :]
    for r, (msg, out) in enumerate(((m1, c1), (m2, c2), (m3, c3)), 1):
        to = lax.rem(own + r, 4)
        msg[0:rows, :] = piece
        msg[rows : rows + STEP, :] = strip
        msg[rows + STEP :, :] = tok[to]
        out[...] = cot[to]
    tok_own[...] = tok[own]
    cot_own[...] = cot[own]


def place_kernel(slot_ref, b0, b1, b2, b3, pos_ref):
    slot = slot_ref[...]
    lanes = b0.shape[0]
    total = None
    for r, blk in enumerate((b0, b1, b2, b3)):
        part = dot(onehot(slot, lanes, r * lanes), blk[blk.shape[0] - lanes :, :])
        total = part if total is None else total + part
    pos_ref[...] = total.astype(BF)


ORDER = [(c, y, x, r) for c in (0, 1) for y in (0, 1) for x in (0, 1) for r in range(4)]


def norm_kernel(scal, slot_ref, b0, b1, b2, b3, gain, shift, pos_ref, xn_ref, xt_ref, turned):
    place_kernel(slot_ref, b0, b1, b2, b3, pos_ref)
    own, unit = scal[0], scal[1]

    @each_tile(pos_ref.shape[0])
    def _(i):
        x = pos_ref[rows_of(i), :].astype(F32)
        cen = x - mean_rows(x)
        rstd = lax.rsqrt(mean_rows(cen * cen) + EPS)
        xn_ref[rows_of(i), :] = (cen * rstd * gain[...] + shift[...]).astype(BF)

    turned[...] = xn_ref[...].T
    for k, (c, y, x, r) in enumerate(ORDER):
        who = lax.rem(own + r, 4)
        e = c + 2 * x + 4 * y
        src = who * 128 + (unit ^ e) * STEP
        xt_ref[k * STEP : (k + 1) * STEP, :] = turned[pl.ds(aligned(src, STEP), STEP), :]


class Copies:
    def __init__(self, sems):
        self.sems, self.all = sems, []

    def bring(self, src, dst):
        copy = pltpu.make_async_copy(src, dst, self.sems.at[len(self.all)])
        copy.start()
        self.all.append(copy)

    def wait(self):
        for copy in self.all:
            copy.wait()


def gate_kernel(scal, slot_ref, xn_ref, b_in, g_two, s_two, wi_own, *rest):
    wi, rest = rest[:8], rest[8:]
    win, u_ref, slope_u, vhat_ref, rstd_ref, slope_v, vn_ref, pre, sems = rest
    own, unit = scal[0], scal[1]
    n, gate = vhat_ref.shape
    tiles = gate // LANE
    copies = Copies(sems)
    copies.bring(wi_own, win.at[pl.ds(aligned(own * 128, 128), 128), :])
    for e in range(8):
        for r in (1, 2, 3):
            who = lax.rem(own + (4 - r), 4)
            at = who * 128 + (unit ^ e) * STEP
            copies.bring(wi[e].at[r - 1], win.at[pl.ds(aligned(at, STEP), STEP), :])
    copies.wait()

    xn = xn_ref[...]
    for k in range(tiles):
        cols = slice(k * LANE, (k + 1) * LANE)
        wide = slice(gate + k * LANE, gate + (k + 1) * LANE)
        pre[:, cols] = dot(xn, win[:, wide]) + b_in[:, wide]

    @each_tile(n)
    def _(i):
        rows = rows_of(i)
        v, slope = gelu_parts(pre[rows, :])
        slope_v[rows, :] = slope
        cen = v - mean_rows(v)
        rstd = lax.rsqrt(mean_rows(cen * cen) + EPS)
        vhat = cen * rstd
        vhat_ref[rows, :] = vhat
        rstd_ref[rows, :] = rstd
        vn = jnp.where(slot_ref[rows, :] >= 0, vhat * g_two[...] + s_two[...], 0.0)
        vn_ref[rows, :] = vn.astype(BF)

    for k in range(tiles):
        cols = slice(k * LANE, (k + 1) * LANE)
        pre[:, cols] = dot(xn, win[:, cols]) + b_in[:, cols]

    @each_tile(n)
    def _(i):
        rows = rows_of(i)
        u, slope = gelu_parts(pre[rows, :])
        u_ref[rows, :] = u
        slope_u[rows, :] = slope


def spatial_kernel(scal, slot_ref, pos_ref, xt_ref, cot_ref, u_ref, slope_u, vn_ref, b_mix, b_out, wo_own, mx_own, *rest):
    wo, rest = rest[:8], rest[8:]
    out_ref, mix_ref, pre_u, sg_ref, keep, send, *rest = rest
    wout, mixp, spat, gated, gtmp, sems = rest
    own, unit = scal[0], scal[1]
    n, gate = u_ref.shape
    tiles = gate // LANE
    out_unit = wout.shape[0] // 32
    copies = Copies(sems)
    copies.bring(wo_own, wout.at[pl.ds(aligned(own * 8 * out_unit, STEP), 8 * out_unit), :])
    copies.bring(mx_own, mixp.at[pl.ds(aligned(own * 128, 128), 128), :])
    for e in range(8):
        for r in (1, 2, 3):
            who = lax.rem(own + (4 - r), 4)
            at = (who * 8 + (unit ^ e)) * out_unit
            copies.bring(wo[e].at[r - 1, pl.ds(0, out_unit)], wout.at[pl.ds(aligned(at, STEP), out_unit), :])
            at = who * 128 + (unit ^ e) * STEP
            copies.bring(wo[e].at[r - 1, pl.ds(out_unit, STEP)], mixp.at[pl.ds(aligned(at, STEP), STEP), :])
    copies.wait()
    per = 81
    cell = lax.broadcasted_iota(I32, (n, mixp.shape[0]), 0)
    lane = lax.broadcasted_iota(I32, (n, mixp.shape[0]), 1)
    part = jnp.where(cell >= per, 1, 0) + jnp.where(cell >= 2 * per, 1, 0) + jnp.where(cell >= 3 * per, 1, 0)
    pick = jnp.where(lane == cell + part * (128 - per), 1.0, 0.0).astype(BF)
    mix_ref[...] = dot(pick, mixp[:, :n]).astype(BF)
    mix = mix_ref[...]
    for k in range(tiles):
        cols = slice(k * LANE, (k + 1) * LANE)
        sp = dot(mix, vn_ref[:, cols]) + b_mix[...]
        spat[:, cols] = sp
        gated[:, cols] = (u_ref[:, cols] * sp).astype(BF)

    cot = cot_ref[...]
    for k in range(tiles):
        cols = slice(k * LANE, (k + 1) * LANE)
        gg = dot(cot, wout[cols, :], 1, 1)
        sg_ref[:, cols] = (gg * u_ref[:, cols]).astype(BF)
        pre_u[:, cols] = (gg * spat[:, cols] * slope_u[:, cols]).astype(BF)

    low = out_unit + STEP
    for k in range(tiles):
        rows = slice(k * LANE, (k + 1) * LANE)
        gtmp[rows, :] = dot(gated[:, rows], cot, 0, 0).astype(BF)
    height = keep.shape[1] // 4
    for c, dst in ((0, keep), (1, send)):
        for e in range(4):
            for r in range(4):
                at = (lax.rem(own + r, 4) * 8 + (unit ^ (c + 2 * e))) * out_unit
                dst[e, r * height : r * height + out_unit, :] = gtmp[pl.ds(aligned(at, STEP), out_unit), :]
    gmix = dot(sg_ref[...], vn_ref[...], 1, 1).astype(BF)
    big = lax.broadcasted_iota(I32, (512, n), 0)
    lane = lax.broadcasted_iota(I32, (512, n), 1)
    within = ((big >> 6) ^ unit) * STEP + (big & 15)
    a = (((big >> 4) + own) & 3) * per + within
    pick = jnp.where((lane == a) & (within < per), 1.0, 0.0).astype(BF)
    padded = dot(pick, gmix).astype(BF)
    for c, dst in ((0, keep), (1, send)):
        for e in range(4):
            for r in range(4):
                at = (c + 2 * e) * 64 + r * STEP
                to = r * height + out_unit
                dst[e, to : to + STEP, :] = jnp.zeros((STEP, LANE), BF)
                dst[e, to : to + STEP, 0:n] = padded[at : at + STEP, :]
    for k in range(tiles):
        cols = slice(k * LANE, (k + 1) * LANE)
        part = dot(xt_ref[...], pre_u[:, cols]).astype(BF)
        for j, (c, y, x, r) in enumerate(ORDER):
            to = r * height + low + k * STEP
            (send if c else keep)[x + 2 * y, to : to + STEP, :] = part[j * STEP : (j + 1) * STEP, :]
    branch = dot(gated[...], wout[...]) + b_out[...]
    live = slot_ref[...] >= 0
    out_ref[...] = jnp.where(live, pos_ref[...].astype(F32) + branch, 0.0).astype(BF)


def back_kernel(slot_ref, xt_ref, mix_ref, sg_ref, vhat_ref, rstd_ref, slope_v, g_two, pre_v, keep, send, rows_ref, vng, gain, shift):
    n, gate = vhat_ref.shape
    tiles = gate // LANE
    mix = mix_ref[...]
    for k in range(tiles):
        cols = slice(k * LANE, (k + 1) * LANE)
        vng[:, cols] = dot(mix, sg_ref[:, cols], 0, 0)
    gain[...] = jnp.zeros_like(gain)
    shift[...] = jnp.zeros_like(shift)

    @each_tile(n)
    def _(i):
        rows = rows_of(i)
        vg = jnp.where(slot_ref[rows, :] >= 0, vng[rows, :], 0.0)
        vhat = vhat_ref[rows, :]
        gain[...] += jnp.sum((vg * vhat).reshape(2, 8, gate), 0)
        shift[...] += jnp.sum(vg.reshape(2, 8, gate), 0)
        h = vg * g_two[...]
        v_grad = rstd_ref[rows, :] * (h - mean_rows(h) - vhat * mean_rows(h * vhat))
        pre_v[rows, :] = (v_grad * slope_v[rows, :]).astype(BF)

    height = keep.shape[1] // 4
    for k in range(tiles):
        cols = slice(k * LANE, (k + 1) * LANE)
        part = dot(xt_ref[...], pre_v[:, cols]).astype(BF)
        for j, (c, y, x, r) in enumerate(ORDER):
            to = r * height + k * STEP
            (send if c else keep)[x + 2 * y, to : to + STEP, :] = part[j * STEP : (j + 1) * STEP, :]
        rows_ref[k : k + 1, :] = jnp.sum(gain[:, cols], 0, keepdims=True)
        rows_ref[tiles + k : tiles + k + 1, :] = jnp.sum(shift[:, cols], 0, keepdims=True)


def token_kernel(slot_ref, slot_row, pos_ref, cot_ref, win, pre_u, pre_v, sg_ref, out_ref, g_one, rows_ref, *rest):
    _, o0, o1, o2, o3, vec, xg, in_ref, gain, shift = rest
    n, gate = pre_u.shape
    xg[...] = dot(pre_u[...], win[:, :gate], 1, 1) + dot(pre_v[...], win[:, gate:], 1, 1)
    gain[...] = jnp.zeros_like(gain)
    shift[...] = jnp.zeros_like(shift)
    width = xg.shape[1]

    @each_tile(n)
    def _(i):
        rows = rows_of(i)
        x = pos_ref[rows, :].astype(F32)
        cen = x - mean_rows(x)
        rstd = lax.rsqrt(mean_rows(cen * cen) + EPS)
        xhat = cen * rstd
        g = xg[rows, :]
        gain[...] += jnp.sum((g * xhat).reshape(2, 8, width), 0)
        shift[...] += jnp.sum(g.reshape(2, 8, width), 0)
        h = g * g_one[...]
        x_grad = rstd * (h - mean_rows(h) - xhat * mean_rows(h * xhat))
        total = cot_ref[rows, :].astype(F32) + x_grad
        in_ref[rows, :] = jnp.where(slot_ref[rows, :] >= 0, total, 0.0).astype(BF)

    count = o0.shape[1]
    for r, dst in enumerate((o0, o1, o2, o3)):
        spot = lax.broadcasted_iota(I32, (count, n), 0) + r * count
        pick = jnp.where(slot_row[...] == spot, 1.0, 0.0).astype(BF)
        dst[0] = dot(pick, out_ref[...]).astype(BF)
        dst[1] = dot(pick, in_ref[...]).astype(BF)

    ones = jnp.ones((8, n), BF)
    tiles = gate // LANE
    vec[0:1, :] = jnp.sum(gain[...], 0, keepdims=True)
    vec[1:2, :] = jnp.sum(shift[...], 0, keepdims=True)
    for k in range(tiles):
        cols = slice(k * LANE, (k + 1) * LANE)
        vec[2 + k : 3 + k, :] = dot(ones, pre_u[:, cols])[0:1]
        vec[2 + tiles + k : 3 + tiles + k, :] = dot(ones, pre_v[:, cols])[0:1]
    at = 2 + 2 * tiles
    vec[at : at + 2 * tiles, :] = rows_ref[...]
    at += 2 * tiles
    vec[at : at + 1, :] = dot(ones, cot_ref[...])[0:1]
    vec[at + 1 : at + 2, :] = jnp.zeros((1, LANE), F32)
    vec[at + 1 : at + 2, 0:n] = dot(jnp.ones((8, gate), BF), sg_ref[...], 1, 1)[0:1]


def split_low(v):
    high = v.astype(BF)
    return high, (v - high.astype(F32)).astype(BF)


def put_vec(ref, at, v):
    high, low = split_low(v)
    ref[at : at + STEP, :] = high
    ref[at + STEP : at + 2 * STEP, :] = low


def get_vec(ref, at):
    return ref[at : at + STEP, :].astype(F32) + ref[at + STEP : at + 2 * STEP, :].astype(F32)


def core_kernel(keep, got, own, s1, s2, s3):
    for e, dst in enumerate((own, s1, s2, s3)):
        dst[...] = (keep[e].astype(F32) + got[e].astype(F32)).astype(dst.dtype)


def core_vec_kernel(keep, got, vec, vec_got, own, s1, s2, s3, vec_own):
    rows = own.shape[0]
    total = vec[...] + vec_got[...]
    put_vec(vec_own, 0, total)
    for e, dst in enumerate((own, s1, s2, s3)):
        dst[0:rows, :] = (keep[e].astype(F32) + got[e].astype(F32)).astype(dst.dtype)
        if e:
            put_vec(dst, rows, total)


def plane_kernel(own, g1, g2, g3, z0, z1, z2, z3):
    rows = z0.shape[0]
    for r, dst in enumerate((z0, z1, z2, z3)):
        at = slice(r * rows, (r + 1) * rows)
        total = (own[at, :] + g1[at, :].astype(F32)) + (g2[at, :].astype(F32) + g3[at, :].astype(F32))
        dst[...] = total.astype(dst.dtype)


def plane_vec_kernel(own, vec_own, g1, g2, g3, z0, z1, z2, z3, vec_out):
    rows, at = z0.shape[0], own.shape[0]
    vec = (get_vec(vec_own, 0) + get_vec(g1, at)) + (get_vec(g2, at) + get_vec(g3, at))
    put_vec(vec_out, 0, vec)
    for r, dst in enumerate((z0, z1, z2, z3)):
        at = slice(r * rows, (r + 1) * rows)
        total = (own[at, :] + g1[at, :].astype(F32)) + (g2[at, :].astype(F32) + g3[at, :].astype(F32))
        dst[0:rows, :] = total.astype(dst.dtype)
        if r:
            put_vec(dst, rows, vec)


def patch_kernel(own, g1, g2, g3, out):
    rows = own.shape[0]
    total = own[...]
    for g in (g1, g2, g3):
        total = total + g[0:rows, :].astype(F32)
    out[...] = total.astype(out.dtype)


def patch_vec_kernel(scal, own, vec_own, g1, g2, g3, out, vec_out, held):
    patch_kernel(own, g1, g2, g3, out)
    rows = own.shape[0]
    me = scal[0]
    held[me] = get_vec(vec_own, 0)
    for r, g in enumerate((g1, g2, g3), 1):
        held[lax.rem(me + (4 - r), 4)] = get_vec(g, rows)
    vec_out[...] = (held[0] + held[1]) + (held[2] + held[3])


def home_kernel(scal, h0, h1, h2, h3, out_ref, grad_ref):
    own = scal[0]
    for r, h in enumerate((h0, h1, h2, h3)):
        m = lax.rem(own + r, 4)
        out_ref[m] = h[0]
        grad_ref[m] = h[1].astype(F32)


VM = pl.BlockSpec(memory_space=pltpu.VMEM)
SM = pl.BlockSpec(memory_space=pltpu.SMEM)
ANY = pl.BlockSpec(memory_space=pl.ANY)


def call(body, ins, outs, scratch=(), specs=None, flops=100_000_000, limit=16, name=None):
    moved = sum(math.prod(a.shape) * a.dtype.itemsize for a in ins)
    return pl.pallas_call(
        body,
        out_shape=[jax.ShapeDtypeStruct(s, d) for s, d in outs],
        in_specs=specs or [VM] * len(ins),
        out_specs=[VM] * len(outs),
        scratch_shapes=list(scratch),
        compiler_params=pltpu.CompilerParams(vmem_limit_bytes=limit * 2**20),
        cost_estimate=pl.CostEstimate(flops=flops, bytes_accessed=moved, transcendentals=0),
        name=name,
    )(*ins)


def rest_of_img(total):
    mask = 8
    while mask < lax.axis_size("img"):
        total = total + swap(total, mask)
        mask *= 2
    return total


def img_gather(arr):
    size = lax.axis_size("img")
    groups = [[g * 8 + k for k in range(8)] for g in range(size // 8)]
    return lax.all_gather(arr, "img", axis_index_groups=groups)


def shards(
    tokens,
    cotangent,
    patch_count,
    crop_index,
    in_weight,
    in_moment,
    in_average,
    out_weight,
    out_moment,
    out_average,
    spatial_weight,
    spatial_moment,
    spatial_average,
    vectors,
    vector_moment,
    vector_average,
):
    p = lax.axis_index("patch")
    unit = lax.axis_index("img") % 8
    micro_count, slot_count, row_count, width = tokens.shape
    hidden = in_weight.shape[1]
    gate = hidden // 2
    mix_rows, cells = spatial_weight.shape
    assert micro_count == lax.axis_size("patch") == 4 and slot_count == 1
    assert width == LANE and in_weight.shape[0] == 128 and row_count == mix_rows == 81
    grid = math.isqrt(cells)
    n = -(-cells // STEP) * STEP
    in_unit = in_weight.shape[0] // 8
    out_unit = out_weight.shape[0] // 8
    low = out_unit + STEP
    side_rows = in_unit * gate // LANE
    scal = jnp.stack([p, unit]).astype(I32)

    def over_plane(base):
        chips = [base] + [swap(base, m) for m in (2, 4, 6)]
        found = []
        for arr in chips:
            found += [arr, swap(arr, CORE)]
        return found

    wi_piece = lax.dynamic_slice_in_dim(in_weight, unit * in_unit, in_unit, 0).astype(BF)
    wi = over_plane(jnp.stack([turn(wi_piece, r) for r in (1, 2, 3)]))
    wi_own = in_weight.astype(BF)

    blk = ((row_count, width), BF)
    msg = ((low + row_count, width), BF)
    m1, m2, m3, tok_own, c1, c2, c3, cot_own, wo_own, mx_own = call(
        prep_kernel,
        [scal, tokens.reshape(4, row_count, width), cotangent.reshape(4, row_count, width), out_weight, spatial_weight],
        [msg, msg, msg, blk, blk, blk, blk, blk, (out_weight.shape, BF), ((128, LANE), BF)],
        specs=[SM] + [VM] * 4,
        name="prep",
    )
    got = [turn(m, r) for r, m in enumerate((m1, m2, m3), 1)]
    cot = [cot_own] + [turn(c, r) for r, c in enumerate((c1, c2, c3), 1)]
    wo = over_plane(jnp.stack([g[:low] for g in got]))

    count = lax.dynamic_index_in_dim(patch_count, p, 0, keepdims=False)[0]
    start = lax.dynamic_index_in_dim(crop_index, p, 0, keepdims=False)[0, 0]
    quarter = count // 4
    side = jnp.round(jnp.sqrt(count.astype(F32))).astype(I32)
    place = jnp.arange(n, dtype=I32)
    drow = place // grid - start // grid
    dcol = place % grid - start % grid
    inside = (drow >= 0) & (drow < side) & (dcol >= 0) & (dcol < side) & (place < cells)
    order = drow * side + dcol
    block = (order >= quarter).astype(I32) + (order >= 2 * quarter).astype(I32) + (order >= 3 * quarter).astype(I32)
    slot = jnp.where(inside, ((p - block) % 4) * row_count + order - block * quarter, -1)
    slot_col, slot_row = slot[:, None], slot[None, :]

    bounds = [width, width, hidden, gate, gate, cells, width]
    pieces = []
    offset = 0
    for length in bounds:
        pieces.append(vectors[None, offset : offset + length])
        offset += length
    g_one, s_one, b_in, g_two, s_two, b_mix, b_out = pieces
    b_mix = jnp.pad(b_mix[0], (0, n - cells))[:, None]

    pos, xn, xt = call(
        norm_kernel,
        [scal, slot_col, tok_own, *got, g_one, s_one],
        [((n, width), BF), ((n, width), BF), ((width, n), BF)],
        [pltpu.VMEM((width, n), BF)],
        specs=[SM] + [VM] * 7,
        name="norm_in",
    )
    (cot_pos,) = call(place_kernel, [slot_col, *cot], [((n, width), BF)], name="place_cot")
    sized = lambda kind: ((n, gate), kind)
    win, u, slope_u, vhat, rstd, slope_v, vn = call(
        gate_kernel,
        [scal, slot_col, xn, b_in, g_two, s_two, wi_own, *wi],
        [((width, hidden), BF), sized(F32), sized(F32), sized(F32), ((n, 1), F32), sized(F32), sized(BF)],
        [pltpu.VMEM((n, gate), F32), pltpu.SemaphoreType.DMA((25,))],
        specs=[SM] + [VM] * 5 + [ANY] * 9,
        flops=2_000_000_000,
        limit=24,
        name="gate",
    )
    packed = ((4, 4 * (low + side_rows), LANE), BF)
    out_pos, mix, pre_u, sg, keep_a, send_a = call(
        spatial_kernel,
        [scal, slot_col, pos, xt, cot_pos, u, slope_u, vn, b_mix, b_out, wo_own, mx_own, *wo],
        [((n, width), BF), ((n, n), BF), sized(BF), sized(BF), packed, packed],
        [
            pltpu.VMEM((gate, width), BF),
            pltpu.VMEM((512, LANE), BF),
            pltpu.VMEM((n, gate), F32),
            pltpu.VMEM((n, gate), BF),
            pltpu.VMEM((gate, width), BF),
            pltpu.SemaphoreType.DMA((50,)),
        ],
        specs=[SM] + [VM] * 9 + [ANY] * 10,
        flops=4_000_000_000,
        limit=24,
        name="spatial",
    )
    core_a = swap(send_a, CORE)
    half = ((4, 4 * side_rows, LANE), BF)
    pre_v, keep_b, send_b, rows_b = call(
        back_kernel,
        [slot_col, xt, mix, sg, vhat, rstd, slope_v, g_two],
        [sized(BF), half, half, ((6, LANE), F32)],
        [pltpu.VMEM((n, gate), F32), pltpu.VMEM((8, gate), F32), pltpu.VMEM((8, gate), F32)],
        flops=2_000_000_000,
        limit=20,
        name="back",
    )
    core_b = swap(send_b, CORE)
    rows_a, rows_b4 = 4 * (low + side_rows), 4 * side_rows
    own_a, *send_a = call(
        core_kernel, [keep_a, core_a], [((rows_a, LANE), F32)] + [((rows_a, LANE), BF)] * 3, limit=12, name="core_a"
    )
    plane_a = [swap(s, m) for s, m in zip(send_a, (2, 4, 6))]
    pair = ((2, row_count, width), BF)
    h0, h1, h2, h3, vec = call(
        token_kernel,
        [slot_col, slot_row, pos, cot_pos, win, pre_u, pre_v, sg, out_pos, g_one, rows_b, send_a[2]],
        [pair, pair, pair, pair, ((STEP, LANE), F32)],
        [
            pltpu.VMEM((n, width), F32),
            pltpu.VMEM((n, width), BF),
            pltpu.VMEM((8, width), F32),
            pltpu.VMEM((8, width), F32),
        ],
        specs=[VM] * 11 + [ANY],
        flops=2_000_000_000,
        limit=20,
        name="token_grad",
    )
    vec_got = swap(vec, CORE)
    own_b, *send_b, vec_own = call(
        core_vec_kernel,
        [keep_b, core_b, vec, vec_got],
        [((rows_b4, LANE), F32)] + [((rows_b4 + 2 * STEP, LANE), BF)] * 3 + [((2 * STEP, LANE), BF)],
        name="core_b",
    )
    plane_b = [swap(s, m) for s, m in zip(send_b, (2, 4, 6))]
    home = [h0] + [turn(h, -r) for r, h in enumerate((h1, h2, h3), 1)]
    out_tokens, in_grad = call(
        home_kernel,
        [scal, *home],
        [((4, row_count, width), BF), ((4, row_count, width), F32)],
        specs=[SM] + [VM] * 4,
        name="home",
    )
    z_rows = low + side_rows
    own_a, *patch_a = call(
        plane_kernel, [own_a, *plane_a], [((z_rows, LANE), F32)] + [((z_rows, LANE), BF)] * 3, name="plane_a"
    )
    got_a = [turn(z, r) for r, z in enumerate(patch_a, 1)]
    own_b, *patch_b, vec_own = call(
        plane_vec_kernel,
        [own_b, vec_own, *plane_b],
        [((side_rows, LANE), F32)] + [((side_rows + 2 * STEP, LANE), BF)] * 3 + [((2 * STEP, LANE), BF)],
        name="plane_b",
    )
    got_b = [turn(z, r) for r, z in enumerate(patch_b, 1)]
    kind = BF if lax.axis_size("img") == 8 else F32
    (first,) = call(patch_kernel, [own_a, *got_a], [((z_rows, LANE), kind)], name="patch_a")
    second, vec_sum = call(
        patch_vec_kernel,
        [scal, own_b, vec_own, *got_b],
        [((side_rows, LANE), kind), ((STEP, LANE), F32)],
        [pltpu.VMEM((4, STEP, LANE), F32)],
        specs=[SM] + [VM] * 5,
        name="patch_b",
    )
    first = img_gather(rest_of_img(first).astype(BF))
    second = img_gather(rest_of_img(second).astype(BF))
    vec_sum = rest_of_img(vec_sum).reshape(STEP * LANE)

    def unpack(arr):
        arr = arr.reshape(8, gate // LANE, in_unit, LANE).transpose(0, 2, 1, 3)
        return arr.reshape(8 * in_unit, gate)

    out_share = first[:, :out_unit].reshape(8 * out_unit, width).astype(F32)
    mix_share = first[:, out_unit:low].reshape(128, LANE)[:mix_rows, :cells].astype(F32)
    in_share = jnp.concatenate([unpack(first[:, low:]), unpack(second)], axis=1).astype(F32)
    head_len = 2 * width + hidden + 2 * gate
    vec_sum = jnp.concatenate(
        [vec_sum[:head_len], vec_sum[head_len + width : head_len + width + cells], vec_sum[head_len : head_len + width]]
    )

    images = micro_count * slot_count * lax.axis_size("img")
    rate_in, rate_out, rate_mix, rate_vec = step_rates(images, width, gate, cells)
    in_new = nesterov(in_weight, in_share, in_moment, in_average, rate_in)
    out_new = nesterov(out_weight, out_share, out_moment, out_average, rate_out)
    mix_new = nesterov(spatial_weight, mix_share, spatial_moment, spatial_average, rate_mix)
    vec_new = nesterov(vectors, vec_sum, vector_moment, vector_average, rate_vec)
    return (out_tokens.reshape(tokens.shape), in_grad.reshape(tokens.shape), *in_new, *out_new, *mix_new, *vec_new)


def solution(mesh):
    rows = P("patch", None)
    act = P(None, "img", "patch", None)
    return jax.shard_map(
        shards,
        mesh=mesh,
        in_specs=(act, act, P(None, "img"), P(None, "img", None), *([rows] * 9), P(), P(), P()),
        out_specs=(act, act, *([rows] * 9), P(), P(), P()),
        check_vma=False,
    )
```

```python
import functools
import math

import jax
import jax.numpy as jnp
from jax import lax
from jax.experimental import pallas as pl
from jax.experimental.pallas import tpu as pltpu
from jax.sharding import PartitionSpec as P

EPS = 1e-05
MOMENTUM = 0.9
AVG_DECAY = 0.8
BF = jnp.bfloat16
F32 = jnp.float32
I32 = jnp.int32
CORE, XBIT, YBIT = 1, 2, 4
LANE = 512
STEP = 16
ROWS = 81
HALF = 96


def step_rates(images, model_width, gate_width, cell_count):
    live_rows = 207.0 * images
    rate_in = 1.0 / (math.sqrt(model_width) * 1.4 * math.sqrt(live_rows))
    rate_out = 1.0 / (math.sqrt(gate_width / 4.0) * 1.2 * math.sqrt(live_rows))
    rate_mix = 1.0 / (math.sqrt(cell_count) * 1.5 * math.sqrt(gate_width * images / 2.0))
    rate_vec = 0.1 / (2.0 * math.sqrt(live_rows))
    return (rate_in, rate_out, rate_mix, rate_vec)


def nesterov(weight, grads, moment, average, rate):
    moment_new = MOMENTUM * moment + grads
    weight_new = weight - rate * (grads + MOMENTUM * moment_new)
    average_new = AVG_DECAY * average + (1.0 - AVG_DECAY) * weight_new
    return (weight_new, moment_new, average_new)


def turn(arr, r):
    n = lax.axis_size("patch")
    return lax.ppermute(arr, "patch", [(s, (s + r) % n) for s in range(n)])


def swap(arr, mask):
    n = lax.axis_size("img")
    return lax.ppermute(arr, "img", [(k, k ^ mask) for k in range(n)])


def dot(a, b, ca=1, cb=0):
    return lax.dot_general(a, b, (((ca,), (cb,)), ((), ())), preferred_element_type=F32)


def aligned(v, by):
    return pl.multiple_of(v, by)


def rows_of(i):
    return pl.ds(aligned(i * STEP, STEP), STEP)


def each_tile(n):
    steps = n // STEP
    return pl.loop(0, steps, unroll=7 if steps % 7 == 0 else 1)


def gelu_parts(pre):
    phi = 0.5 * (1.0 + lax.erf(pre * math.sqrt(0.5)))
    slope = phi + pre * (jnp.exp(-0.5 * pre * pre) * (1.0 / math.sqrt(2.0 * math.pi)))
    return pre * phi, slope


def mean_rows(v):
    return jnp.sum(v, axis=-1, keepdims=True) * (1.0 / v.shape[-1])


def slot_kernel(grid, scal, counts, crops, col_ref, row_ref):
    own = scal[0]
    lane = lax.broadcasted_iota(I32, counts.shape, 1)
    count = jnp.sum(jnp.where(lane == own, counts[...], 0), axis=1, keepdims=True)
    start = crops[own][:, 0:1]
    cells = grid * grid
    side = jnp.zeros_like(count)
    top = jnp.zeros_like(count)
    for k in range(1, grid + 1):
        side = jnp.where(count == k * k, k, side)
        top = top + jnp.where(start >= k * grid, 1, 0)
    quarter = count >> 2
    left = start - top * grid
    for ref, dim in ((col_ref, 0), (row_ref, 1)):
        place = lax.broadcasted_iota(I32, ref.shape, dim)
        row = jnp.zeros(ref.shape, I32)
        for k in range(1, grid):
            row = row + jnp.where(place >= k * grid, 1, 0)
        drow = row - top
        dcol = place - row * grid - left
        inside = (drow >= 0) & (drow < side) & (dcol >= 0) & (dcol < side) & (place < cells)
        order = drow * side + dcol
        block = jnp.zeros(ref.shape, I32)
        for k in (1, 2, 3):
            block = block + jnp.where(order >= k * quarter, 1, 0)
        slot = ((own - block) & 3) * ROWS + order - block * quarter
        ref[...] = jnp.where(inside, slot, -1)


def onehot(slot, lanes, base):
    lane = lax.broadcasted_iota(I32, (slot.shape[0], lanes), 1) + base
    return jnp.where(slot == lane, 1.0, 0.0).astype(BF)


class Copies:
    def __init__(self, sems):
        self.sems, self.all = sems, []

    def bring(self, src, dst):
        copy = pltpu.make_async_copy(src, dst, self.sems.at[len(self.all)])
        copy.start()
        self.all.append(copy)

    def wait(self):
        for copy in self.all:
            copy.wait()


def prep_kernel(scal, tok, cot, w_out, mix, m1, m2, m3, tok_own, cot_own, held, strip, sems):
    own, unit = scal[0], scal[1]
    rows = held.shape[0]
    low = rows + STEP
    count = tok.shape[1]
    copies = Copies(sems)
    copies.bring(w_out.at[pl.ds(aligned(unit * rows, STEP), rows), :], held)
    strip[...] = jnp.zeros_like(strip)
    strip[0 : mix.shape[0], 0 : mix.shape[1]] = mix[...].astype(BF)
    copies.wait()
    for r, msg in enumerate((m1, m2, m3), 1):
        to = lax.rem(own + r, 4)
        msg[0:rows, :] = held[...].astype(BF)
        msg[rows:low, :] = strip[pl.ds(aligned(unit * STEP, STEP), STEP), :]
        msg[low : low + count, :] = tok[to]
        msg[low + HALF : low + HALF + count, :] = cot[to]
    tok_own[...] = tok[own]
    cot_own[...] = cot[own]


def hold_kernel(src, tie, dst):
    dst[...] = src[...]


def stack_tied_kernel(m1, m2, m3, tie, out):
    stack_kernel(m1, m2, m3, out)


def join_kernel(p0, p1, p2, p3, tie, out):
    for e, part in enumerate((p0, p1, p2, p3)):
        out[e] = part[...]


def stack_kernel(m1, m2, m3, out):
    for r, msg in enumerate((m1, m2, m3)):
        out[r] = msg[0 : out.shape[1], :]


def place(slot_ref, own, others, at, pos_ref):
    slot = slot_ref[...]
    lanes = own.shape[0]
    total = dot(onehot(slot, lanes, 0), own[...])
    for r, msg in enumerate(others, 1):
        total = total + dot(onehot(slot, lanes, r * lanes), msg[at : at + lanes, :])
    pos_ref[...] = total.astype(BF)


def place_kernel(at, slot_ref, own, m1, m2, m3, tie, pos_ref):
    place(slot_ref, own, (m1, m2, m3), at, pos_ref)


ORDER = [(c, y, x, r) for c in (0, 1) for y in (0, 1) for x in (0, 1) for r in range(4)]


def norm_kernel(at, scal, slot_ref, own_blk, m1, m2, m3, gain, shift, pos_ref, xn_ref, xt_ref, turned):
    place(slot_ref, own_blk, (m1, m2, m3), at, pos_ref)
    own, unit = scal[0], scal[1]

    @each_tile(pos_ref.shape[0])
    def _(i):
        x = pos_ref[rows_of(i), :].astype(F32)
        cen = x - mean_rows(x)
        rstd = lax.rsqrt(mean_rows(cen * cen) + EPS)
        xn_ref[rows_of(i), :] = (cen * rstd * gain[...] + shift[...]).astype(BF)

    turned[...] = xn_ref[...].T
    for k, (c, y, x, r) in enumerate(ORDER):
        who = lax.rem(own + r, 4)
        e = c + 2 * x + 4 * y
        src = who * 128 + (unit ^ e) * STEP
        xt_ref[k * STEP : (k + 1) * STEP, :] = turned[pl.ds(aligned(src, STEP), STEP), :]


def right_kernel(scal, slot_ref, xn_ref, b_in, g_two, s_two, wi_own, *rest):
    wi, rest = rest[:8], rest[8:]
    win, vhat_ref, rstd_ref, slope_v, vn_ref, pre, held, sems = rest
    own, unit = scal[0], scal[1]
    n, gate = vhat_ref.shape
    tiles = gate // LANE
    copies = Copies(sems)
    copies.bring(wi_own, held)
    for e in range(8):
        for r in (1, 2, 3):
            who = lax.rem(own + (4 - r), 4)
            at = who * 128 + (unit ^ e) * STEP
            copies.bring(wi[e].at[r - 1], win.at[pl.ds(aligned(at, STEP), STEP), :])
    copies.all[0].wait()
    win[pl.ds(aligned(own * 128, 128), 128), :] = held[...].astype(BF)
    for copy in copies.all[1:]:
        copy.wait()

    xn = xn_ref[...]
    for k in range(tiles):
        cols = slice(k * LANE, (k + 1) * LANE)
        wide = slice(gate + k * LANE, gate + (k + 1) * LANE)
        pre[:, cols] = dot(xn, win[:, wide]) + b_in[:, wide]

    @each_tile(n)
    def _(i):
        rows = rows_of(i)
        v, slope = gelu_parts(pre[rows, :])
        slope_v[rows, :] = slope
        cen = v - mean_rows(v)
        rstd = lax.rsqrt(mean_rows(cen * cen) + EPS)
        vhat = cen * rstd
        vhat_ref[rows, :] = vhat
        rstd_ref[rows, :] = rstd
        vn = jnp.where(slot_ref[rows, :] >= 0, vhat * g_two[...] + s_two[...], 0.0)
        vn_ref[rows, :] = vn.astype(BF)


def left_kernel(xn_ref, b_in, win, *rest):
    u_ref, slope_u, pre = rest[-3:]
    n, gate = u_ref.shape
    xn = xn_ref[...]
    for k in range(gate // LANE):
        cols = slice(k * LANE, (k + 1) * LANE)
        pre[:, cols] = dot(xn, win[:, cols]) + b_in[:, cols]

    @each_tile(n)
    def _(i):
        rows = rows_of(i)
        u, slope = gelu_parts(pre[rows, :])
        u_ref[rows, :] = u
        slope_u[rows, :] = slope


def spatial_kernel(scal, xt_ref, cot_ref, u_ref, slope_u, vn_ref, b_mix, mix_own, wo_own, *rest):
    wo, rest = rest[:2], rest[2:]
    mix_ref, pre_u, sg_ref, gated, wout, keep, send, *rest = rest
    mixp, spat, gtmp, held, sems = rest
    own, unit = scal[0], scal[1]
    n, gate = u_ref.shape
    tiles = gate // LANE
    out_unit = wout.shape[0] // 32
    copies = Copies(sems)
    copies.bring(wo_own, held)
    for e in range(8):
        for r in (1, 2, 3):
            who = lax.rem(own + (4 - r), 4)
            at = (who * 8 + (unit ^ e)) * out_unit
            copies.bring(wo[e % 2].at[e // 2, r - 1, pl.ds(0, out_unit)], wout.at[pl.ds(aligned(at, STEP), out_unit), :])
            at = who * 128 + (unit ^ e) * STEP
            copies.bring(wo[e % 2].at[e // 2, r - 1, pl.ds(out_unit, STEP)], mixp.at[pl.ds(aligned(at, STEP), STEP), :])
    per, cells = mix_own.shape
    mine = aligned(own * 128, 128)
    mixp[pl.ds(mine, 128), :] = jnp.zeros((128, LANE), BF)
    mixp[pl.ds(mine, per), 0:cells] = mix_own[...].astype(BF)
    copies.all[0].wait()
    wout[pl.ds(aligned(own * 8 * out_unit, STEP), 8 * out_unit), :] = held[...].astype(BF)
    for copy in copies.all[1:]:
        copy.wait()
    cell = lax.broadcasted_iota(I32, (n, mixp.shape[0]), 0)
    lane = lax.broadcasted_iota(I32, (n, mixp.shape[0]), 1)
    part = jnp.where(cell >= per, 1, 0) + jnp.where(cell >= 2 * per, 1, 0) + jnp.where(cell >= 3 * per, 1, 0)
    pick = jnp.where(lane == cell + part * (128 - per), 1.0, 0.0).astype(BF)
    mix_ref[...] = dot(pick, mixp[:, :n]).astype(BF)
    mix = mix_ref[...]
    for k in range(tiles):
        cols = slice(k * LANE, (k + 1) * LANE)
        sp = dot(mix, vn_ref[:, cols]) + b_mix[...]
        spat[:, cols] = sp
        gated[:, cols] = (u_ref[:, cols] * sp).astype(BF)

    cot = cot_ref[...]
    for k in range(tiles):
        cols = slice(k * LANE, (k + 1) * LANE)
        gg = dot(cot, wout[cols, :], 1, 1)
        sg_ref[:, cols] = (gg * u_ref[:, cols]).astype(BF)
        pre_u[:, cols] = (gg * spat[:, cols] * slope_u[:, cols]).astype(BF)

    low = out_unit + STEP
    for k in range(tiles):
        rows = slice(k * LANE, (k + 1) * LANE)
        gtmp[rows, :] = dot(gated[:, rows], cot, 0, 0).astype(BF)
    height = keep.shape[1] // 4
    for c, dst in ((0, keep), (1, send)):
        for e in range(4):
            for r in range(4):
                at = (lax.rem(own + r, 4) * 8 + (unit ^ (c + 2 * e))) * out_unit
                dst[e, r * height : r * height + out_unit, :] = gtmp[pl.ds(aligned(at, STEP), out_unit), :]
    gmix = dot(sg_ref[...], vn_ref[...], 1, 1).astype(BF)
    big = lax.broadcasted_iota(I32, (512, n), 0)
    lane = lax.broadcasted_iota(I32, (512, n), 1)
    within = ((big >> 6) ^ unit) * STEP + (big & 15)
    a = (((big >> 4) + own) & 3) * per + within
    pick = jnp.where((lane == a) & (within < per), 1.0, 0.0).astype(BF)
    padded = dot(pick, gmix).astype(BF)
    for c, dst in ((0, keep), (1, send)):
        for e in range(4):
            for r in range(4):
                at = (c + 2 * e) * 64 + r * STEP
                to = r * height + out_unit
                dst[e, to : to + STEP, :] = jnp.zeros((STEP, LANE), BF)
                dst[e, to : to + STEP, 0:n] = padded[at : at + STEP, :]
    for k in range(tiles):
        cols = slice(k * LANE, (k + 1) * LANE)
        part = dot(xt_ref[...], pre_u[:, cols]).astype(BF)
        for j, (c, y, x, r) in enumerate(ORDER):
            to = r * height + low + k * STEP
            (send if c else keep)[x + 2 * y, to : to + STEP, :] = part[j * STEP : (j + 1) * STEP, :]


def back_kernel(slot_ref, xt_ref, mix_ref, sg_ref, vhat_ref, rstd_ref, slope_v, g_two, pre_v, keep, send, rows_ref, vng, gain, shift):
    n, gate = vhat_ref.shape
    tiles = gate // LANE
    mix = mix_ref[...]
    for k in range(tiles):
        cols = slice(k * LANE, (k + 1) * LANE)
        vng[:, cols] = dot(mix, sg_ref[:, cols], 0, 0)
    gain[...] = jnp.zeros_like(gain)
    shift[...] = jnp.zeros_like(shift)

    @each_tile(n)
    def _(i):
        rows = rows_of(i)
        vg = jnp.where(slot_ref[rows, :] >= 0, vng[rows, :], 0.0)
        vhat = vhat_ref[rows, :]
        gain[...] += jnp.sum((vg * vhat).reshape(2, 8, gate), 0)
        shift[...] += jnp.sum(vg.reshape(2, 8, gate), 0)
        h = vg * g_two[...]
        v_grad = rstd_ref[rows, :] * (h - mean_rows(h) - vhat * mean_rows(h * vhat))
        pre_v[rows, :] = (v_grad * slope_v[rows, :]).astype(BF)

    height = keep.shape[1] // 4
    for k in range(tiles):
        cols = slice(k * LANE, (k + 1) * LANE)
        part = dot(xt_ref[...], pre_v[:, cols]).astype(BF)
        for j, (c, y, x, r) in enumerate(ORDER):
            to = r * height + k * STEP
            (send if c else keep)[x + 2 * y, to : to + STEP, :] = part[j * STEP : (j + 1) * STEP, :]
        rows_ref[k : k + 1, :] = jnp.sum(gain[:, cols], 0, keepdims=True)
        rows_ref[tiles + k : tiles + k + 1, :] = jnp.sum(shift[:, cols], 0, keepdims=True)


def token_kernel(slot_ref, slot_row, pos_ref, cot_ref, win, pre_u, pre_v, sg_ref, gated, wout, g_one, b_out, rows_ref, *rest):
    _, h0, h1, h2, h3, vec, xg, out_ref, in_ref, gain, shift = rest
    n, gate = pre_u.shape
    xg[...] = dot(pre_u[...], win[:, :gate], 1, 1) + dot(pre_v[...], win[:, gate:], 1, 1)
    gain[...] = jnp.zeros_like(gain)
    shift[...] = jnp.zeros_like(shift)
    width = xg.shape[1]

    @each_tile(n)
    def _(i):
        rows = rows_of(i)
        x = pos_ref[rows, :].astype(F32)
        cen = x - mean_rows(x)
        rstd = lax.rsqrt(mean_rows(cen * cen) + EPS)
        xhat = cen * rstd
        g = xg[rows, :]
        gain[...] += jnp.sum((g * xhat).reshape(2, 8, width), 0)
        shift[...] += jnp.sum(g.reshape(2, 8, width), 0)
        h = g * g_one[...]
        x_grad = rstd * (h - mean_rows(h) - xhat * mean_rows(h * xhat))
        total = cot_ref[rows, :].astype(F32) + x_grad
        in_ref[rows, :] = jnp.where(slot_ref[rows, :] >= 0, total, 0.0).astype(BF)

    branch = dot(gated[...], wout[...]) + b_out[...]
    out_ref[...] = jnp.where(slot_ref[...] >= 0, pos_ref[...].astype(F32) + branch, 0.0).astype(BF)
    for r, dst in enumerate((h0, h1, h2, h3)):
        spot = lax.broadcasted_iota(I32, (ROWS, n), 0) + r * ROWS
        pick = jnp.where(slot_row[...] == spot, 1.0, 0.0).astype(BF)
        dst[0:ROWS, :] = dot(pick, out_ref[...]).astype(BF)
        dst[HALF : HALF + ROWS, :] = dot(pick, in_ref[...]).astype(BF)

    ones = jnp.ones((8, n), BF)
    tiles = gate // LANE
    vec[0:1, :] = jnp.sum(gain[...], 0, keepdims=True)
    vec[1:2, :] = jnp.sum(shift[...], 0, keepdims=True)
    for k in range(tiles):
        cols = slice(k * LANE, (k + 1) * LANE)
        vec[2 + k : 3 + k, :] = dot(ones, pre_u[:, cols])[0:1]
        vec[2 + tiles + k : 3 + tiles + k, :] = dot(ones, pre_v[:, cols])[0:1]
    at = 2 + 2 * tiles
    vec[at : at + 2 * tiles, :] = rows_ref[...]
    at += 2 * tiles
    cells = 4 * ROWS
    lane = lax.broadcasted_iota(I32, (1, LANE), 1)
    last = pltpu.roll(dot(ones, cot_ref[...])[0:1], cells, 1)
    vec[at : at + 1, 0:n] = dot(jnp.ones((8, gate), BF), sg_ref[...], 1, 1)[0:1]
    vec[at : at + 1, :] = jnp.where(lane < cells, vec[at : at + 1, :], last)
    vec[at + 1 : at + 2, :] = jnp.where(lane < cells, last, 0.0)


def split_low(v):
    high = v.astype(BF)
    return high, (v - high.astype(F32)).astype(BF)


def put_vec(ref, at, v):
    high, low = split_low(v)
    ref[at : at + STEP, :] = high
    ref[at + STEP : at + 2 * STEP, :] = low


def get_vec(ref, at):
    return ref[at : at + STEP, :].astype(F32) + ref[at + STEP : at + 2 * STEP, :].astype(F32)


def core_kernel(keep, got, own, s1, s2, s3):
    for e, dst in enumerate((own, s1, s2, s3)):
        dst[...] = (keep[e].astype(F32) + got[e].astype(F32)).astype(dst.dtype)


def core_vec_kernel(keep, got, vec, vec_got, tie, own, s1, s2, s3, vec_own):
    rows = own.shape[0]
    total = vec[...] + vec_got[...]
    put_vec(vec_own, 0, total)
    for e, dst in enumerate((own, s1, s2, s3)):
        dst[0:rows, :] = (keep[e].astype(F32) + got[e].astype(F32)).astype(dst.dtype)
        if e:
            put_vec(dst, rows, total)


def plane_kernel(own, g1, g2, g3, z0, z1, z2, z3):
    rows = z0.shape[0]
    for r, dst in enumerate((z0, z1, z2, z3)):
        at = slice(r * rows, (r + 1) * rows)
        total = (own[at, :] + g1[at, :].astype(F32)) + (g2[at, :].astype(F32) + g3[at, :].astype(F32))
        dst[...] = total.astype(dst.dtype)


def plane_vec_kernel(own, vec_own, g1, g2, g3, tie, z0, z1, z2, z3, vec_out):
    rows, at = z0.shape[0], own.shape[0]
    vec = (get_vec(vec_own, 0) + get_vec(g1, at)) + (get_vec(g2, at) + get_vec(g3, at))
    put_vec(vec_out, 0, vec)
    for r, dst in enumerate((z0, z1, z2, z3)):
        at = slice(r * rows, (r + 1) * rows)
        total = (own[at, :] + g1[at, :].astype(F32)) + (g2[at, :].astype(F32) + g3[at, :].astype(F32))
        dst[0:rows, :] = total.astype(dst.dtype)
        if r:
            put_vec(dst, rows, vec)


def patch_kernel(own, g1, g2, g3, out):
    rows = own.shape[0]
    total = own[...]
    for g in (g1, g2, g3):
        total = total + g[0:rows, :].astype(F32)
    out[...] = total.astype(out.dtype)


def patch_vec_kernel(scal, own, vec_own, g1, g2, g3, tie, tie_home, out, vec_out, held):
    patch_kernel(own, g1, g2, g3, out)
    rows = own.shape[0]
    me = scal[0]
    held[me] = get_vec(vec_own, 0)
    for r, g in enumerate((g1, g2, g3), 1):
        held[lax.rem(me + (4 - r), 4)] = get_vec(g, rows)
    vec_out[...] = (held[0] + held[1]) + (held[2] + held[3])


def home_kernel(scal, h0, h1, h2, h3, out_ref, grad_ref, held):
    for r, h in enumerate((h0, h1, h2, h3)):
        m = lax.rem(scal[0] + r, 4)
        held[m] = h[0:ROWS, :]
        grad_ref[m, :, 0, :] = h[HALF : HALF + ROWS, :].astype(F32)
    for m in range(4):
        out_ref[:, m, :] = held[m]


def update_kernel(rates, first, second, *rest):
    olds, rest = rest[:9], rest[9:]
    news, rest = rest[:9], rest[9:]
    made, sems = rest[:9], rest[9]
    copies = Copies(sems)
    out_unit = olds[3].shape[0] // 8
    low = out_unit + STEP

    def step(which, rows, cols, grads):
        old, new = olds[3 * which : 3 * which + 3], made[3 * which : 3 * which + 3]
        at = (slice(*rows), slice(*cols))
        fresh = nesterov(old[0][at], grads.astype(F32), old[1][at], old[2][at], rates[which])
        for ref, value in zip(new, fresh):
            ref[at] = value

    def send(which):
        for j in range(3 * which, 3 * which + 3):
            copies.bring(made[j], news[j])

    width = olds[3].shape[1]
    for u in range(8):
        step(1, (u * out_unit, (u + 1) * out_unit), (0, width), first[u, 0:out_unit, :])
    send(1)
    mix_rows, cells = olds[6].shape
    for u in range(-(-mix_rows // STEP)):
        rows = min(STEP, mix_rows - u * STEP)
        step(2, (u * STEP, u * STEP + rows), (0, cells), first[u, out_unit : out_unit + rows, 0:cells])
    send(2)
    tiles = olds[0].shape[1] // LANE
    for u in range(8):
        for k in range(tiles):
            if k < tiles // 2:
                grads = first[u, low + k * STEP : low + (k + 1) * STEP, :]
            else:
                j = k - tiles // 2
                grads = second[u, j * STEP : (j + 1) * STEP, :]
            step(0, (u * STEP, (u + 1) * STEP), (k * LANE, (k + 1) * LANE), grads)
    send(0)
    copies.wait()


VM = pl.BlockSpec(memory_space=pltpu.VMEM)
SM = pl.BlockSpec(memory_space=pltpu.SMEM)
ANY = pl.BlockSpec(memory_space=pl.ANY)


def call(body, ins, outs, scratch=(), specs=None, out_specs=None, flops=100_000_000, limit=16, name=None):
    moved = sum(math.prod(a.shape) * a.dtype.itemsize for a in ins)
    return pl.pallas_call(
        body,
        out_shape=[jax.ShapeDtypeStruct(s, d) for s, d in outs],
        in_specs=specs or [VM] * len(ins),
        out_specs=out_specs or [VM] * len(outs),
        scratch_shapes=list(scratch),
        compiler_params=pltpu.CompilerParams(vmem_limit_bytes=limit * 2**20),
        cost_estimate=pl.CostEstimate(flops=flops, bytes_accessed=moved, transcendentals=0),
        name=name,
    )(*ins)


def rest_of_img(total):
    mask = 8
    while mask < lax.axis_size("img"):
        total = total + swap(total, mask)
        mask *= 2
    return total


def img_gather(arr):
    size = lax.axis_size("img")
    groups = [[g * 8 + k for k in range(8)] for g in range(size // 8)]
    return lax.all_gather(arr, "img", axis_index_groups=groups)


def shards(
    tokens,
    cotangent,
    patch_count,
    crop_index,
    in_weight,
    in_moment,
    in_average,
    out_weight,
    out_moment,
    out_average,
    spatial_weight,
    spatial_moment,
    spatial_average,
    vectors,
    vector_moment,
    vector_average,
):
    p = lax.axis_index("patch")
    unit = lax.axis_index("img") % 8
    micro_count, slot_count, row_count, width = tokens.shape
    hidden = in_weight.shape[1]
    gate = hidden // 2
    mix_rows, cells = spatial_weight.shape
    assert micro_count == lax.axis_size("patch") == 4 and slot_count == 1
    assert width == LANE and in_weight.shape[0] == 128 and row_count == mix_rows == 81
    grid = math.isqrt(cells)
    n = -(-cells // STEP) * STEP
    in_unit = in_weight.shape[0] // 8
    out_unit = out_weight.shape[0] // 8
    low = out_unit + STEP
    side_rows = in_unit * gate // LANE
    scal = jnp.stack([p, unit]).astype(I32)

    def over_plane(base):
        chips = [base] + [swap(base, m) for m in (2, 4, 6)]
        found = []
        for arr in chips:
            found += [arr, swap(arr, CORE)]
        return found

    wi_piece = lax.dynamic_slice_in_dim(in_weight, unit * in_unit, in_unit, 0).astype(BF)

    blk = ((row_count, width), BF)
    msg = ((low + HALF + row_count, width), BF)
    m1, m2, m3, tok_own, cot_own = call(
        prep_kernel,
        [scal, tokens.reshape(4, row_count, width), cotangent.reshape(4, row_count, width), out_weight, spatial_weight],
        [msg, msg, msg, blk, blk],
        [pltpu.VMEM((out_unit, width), F32), pltpu.VMEM((128, LANE), BF), pltpu.SemaphoreType.DMA((1,))],
        specs=[SM, VM, VM, ANY, VM],
        limit=8,
        name="prep",
    )
    (base_in,) = call(
        stack_tied_kernel,
        [turn(wi_piece, r) for r in (1, 2, 3)] + [m1],
        [((3, in_unit, hidden), BF)],
        specs=[VM] * 3 + [ANY],
        limit=8,
        name="stack_i",
    )
    wi = over_plane(base_in)
    got = [turn(m, r) for r, m in enumerate((m1, m2, m3), 1)]
    (base,) = call(stack_tied_kernel, [*got, wi[2]], [((3, low, LANE), BF)], specs=[VM] * 3 + [ANY], limit=8, name="stack_o")
    plane_out = [base] + [swap(base, m) for m in (2, 4, 6)]

    slot_col, slot_row = call(
        functools.partial(slot_kernel, grid),
        [scal, patch_count.reshape(1, 4), crop_index],
        [((n, 1), I32), ((1, n), I32)],
        specs=[SM, VM, VM],
        limit=8,
        name="slots",
    )

    bounds = [width, width, hidden, gate, gate, cells, width]
    pieces = []
    offset = 0
    for length in bounds:
        pieces.append(vectors[None, offset : offset + length])
        offset += length
    g_one, s_one, b_in, g_two, s_two, b_mix, b_out = pieces
    b_mix = jnp.pad(b_mix[0], (0, n - cells))[:, None]

    pos, xn, xt = call(
        functools.partial(norm_kernel, low),
        [scal, slot_col, tok_own, *got, g_one, s_one],
        [((n, width), BF), ((n, width), BF), ((width, n), BF)],
        [pltpu.VMEM((width, n), BF)],
        specs=[SM] + [VM] * 7,
        name="norm_in",
    )
    sized = lambda kind: ((n, gate), kind)
    win, vhat, rstd, slope_v, vn = call(
        right_kernel,
        [scal, slot_col, xn, b_in, g_two, s_two, in_weight, *wi],
        [((width, hidden), BF), sized(F32), ((n, 1), F32), sized(F32), sized(BF)],
        [pltpu.VMEM((n, gate), F32), pltpu.VMEM(in_weight.shape, F32), pltpu.SemaphoreType.DMA((25,))],
        specs=[SM] + [VM] * 5 + [ANY] * 9,
        flops=1_500_000_000,
        limit=20,
        name="right",
    )
    (joined,) = call(
        join_kernel, [*plane_out, vn], [((4, 3, low, LANE), BF)], specs=[VM] * 4 + [ANY], limit=8, name="join"
    )
    (cot_pos,) = call(
        functools.partial(place_kernel, low + HALF),
        [slot_col, cot_own, *got, joined],
        [((n, width), BF)],
        specs=[VM] * 5 + [ANY],
        name="place_cot",
    )
    u, slope_u = call(
        left_kernel,
        [xn, b_in, win, cot_pos],
        [sized(F32), sized(F32)],
        [pltpu.VMEM((n, gate), F32)],
        specs=[VM] * 3 + [ANY],
        flops=1_000_000_000,
        limit=16,
        name="left",
    )
    packed = ((4, 4 * (low + side_rows), LANE), BF)
    mix, pre_u, sg, gated, wout, keep_a, send_a = call(
        spatial_kernel,
        [scal, xt, cot_pos, u, slope_u, vn, b_mix, spatial_weight, out_weight, joined, swap(joined, CORE)],
        [((n, n), BF), sized(BF), sized(BF), sized(BF), ((gate, width), BF), packed, packed],
        [
            pltpu.VMEM((512, LANE), BF),
            pltpu.VMEM((n, gate), F32),
            pltpu.VMEM((gate, width), BF),
            pltpu.VMEM(out_weight.shape, F32),
            pltpu.SemaphoreType.DMA((50,)),
        ],
        specs=[SM] + [VM] * 7 + [ANY] * 3,
        flops=4_000_000_000,
        limit=24,
        name="spatial",
    )
    core_a = swap(send_a, CORE)
    half = ((4, 4 * side_rows, LANE), BF)
    pre_v, keep_b, send_b, rows_b = call(
        back_kernel,
        [slot_col, xt, mix, sg, vhat, rstd, slope_v, g_two],
        [sized(BF), half, half, ((6, LANE), F32)],
        [pltpu.VMEM((n, gate), F32), pltpu.VMEM((8, gate), F32), pltpu.VMEM((8, gate), F32)],
        flops=2_000_000_000,
        limit=20,
        name="back",
    )
    core_b = swap(send_b, CORE)
    rows_a, rows_b4 = 4 * (low + side_rows), 4 * side_rows
    own_a, *send_a = call(
        core_kernel, [keep_a, core_a], [((rows_a, LANE), F32)] + [((rows_a, LANE), BF)] * 3, limit=12, name="core_a"
    )
    plane_a = [swap(s, m) for s, m in zip(send_a, (2, 4, 6))]
    *home, vec = call(
        token_kernel,
        [slot_col, slot_row, pos, cot_pos, win, pre_u, pre_v, sg, gated, wout, g_one, b_out, rows_b, send_a[2]],
        [((HALF + row_count, width), BF)] * 4 + [((STEP, LANE), F32)],
        [
            pltpu.VMEM((n, width), F32),
            pltpu.VMEM((n, width), BF),
            pltpu.VMEM((n, width), BF),
            pltpu.VMEM((8, width), F32),
            pltpu.VMEM((8, width), F32),
        ],
        specs=[VM] * 13 + [ANY],
        flops=2_000_000_000,
        limit=20,
        name="token_grad",
    )
    vec_got = swap(vec, CORE)
    own_b, *send_b, vec_own = call(
        core_vec_kernel,
        [keep_b, core_b, vec, vec_got, send_a[0]],
        [((rows_b4, LANE), F32)] + [((rows_b4 + 2 * STEP, LANE), BF)] * 3 + [((2 * STEP, LANE), BF)],
        specs=[VM] * 4 + [ANY],
        name="core_b",
    )
    plane_b = [swap(s, m) for s, m in zip(send_b, (2, 4, 6))]
    home = [home[0]] + [turn(h, -r) for r, h in enumerate(home[1:], 1)]
    out_tokens, in_grad = call(
        home_kernel,
        [scal, *home],
        [((row_count, 4, width), BF), ((4, row_count, 1, width), F32)],
        [pltpu.VMEM((4, row_count, width), BF)],
        specs=[SM] + [VM] * 4,
        limit=8,
        name="home",
    )
    z_rows = low + side_rows
    own_a, *patch_a = call(
        plane_kernel, [own_a, *plane_a], [((z_rows, LANE), F32)] + [((z_rows, LANE), BF)] * 3, name="plane_a"
    )
    got_a = [turn(z, r) for r, z in enumerate(patch_a, 1)]
    own_b, *patch_b, vec_own = call(
        plane_vec_kernel,
        [own_b, vec_own, *plane_b, patch_a[0]],
        [((side_rows, LANE), F32)] + [((side_rows + 2 * STEP, LANE), BF)] * 3 + [((2 * STEP, LANE), BF)],
        specs=[VM] * 5 + [ANY],
        name="plane_b",
    )
    got_b = [turn(z, r) for r, z in enumerate(patch_b, 1)]
    kind = BF if lax.axis_size("img") == 8 else F32
    (first,) = call(patch_kernel, [own_a, *got_a], [((z_rows, LANE), kind)], name="patch_a")
    first = img_gather(rest_of_img(first).astype(BF))
    second, vec_sum = call(
        patch_vec_kernel,
        [scal, own_b, vec_own, *got_b, first, in_grad],
        [((side_rows, LANE), kind), ((STEP, LANE), F32)],
        [pltpu.VMEM((4, STEP, LANE), F32)],
        specs=[SM] + [VM] * 5 + [ANY] * 2,
        name="patch_b",
    )
    second = img_gather(rest_of_img(second).astype(BF))
    vec_sum = rest_of_img(vec_sum).reshape(STEP * LANE)

    vec_sum = vec_sum[: vectors.shape[0]]

    images = micro_count * slot_count * lax.axis_size("img")
    rate_in, rate_out, rate_mix, rate_vec = step_rates(images, width, gate, cells)
    olds = [in_weight, in_moment, in_average, out_weight, out_moment, out_average]
    olds += [spatial_weight, spatial_moment, spatial_average]
    news = call(
        functools.partial(update_kernel, (rate_in, rate_out, rate_mix)),
        [first, second, *olds],
        [(a.shape, F32) for a in olds],
        [pltpu.VMEM(a.shape, F32) for a in olds] + [pltpu.SemaphoreType.DMA((9,))],
        specs=[VM] * 11,
        out_specs=[ANY] * 9,
        limit=20,
        name="update",
    )
    vec_new = nesterov(vectors, vec_sum, vector_moment, vector_average, rate_vec)
    return (out_tokens.transpose(1, 0, 2).reshape(tokens.shape), in_grad.transpose(0, 2, 1, 3), *news, *vec_new)


def solution(mesh):
    rows = P("patch", None)
    act = P(None, "img", "patch", None)
    return jax.shard_map(
        shards,
        mesh=mesh,
        in_specs=(act, act, P(None, "img"), P(None, "img", None), *([rows] * 9), P(), P(), P()),
        out_specs=(act, act, *([rows] * 9), P(), P(), P()),
        check_vma=False,
    )
```

```python
import functools
import math

import jax
import jax.numpy as jnp
from jax import lax
from jax.experimental import pallas as pl
from jax.experimental.pallas import tpu as pltpu
from jax.sharding import PartitionSpec as P

EPS = 1e-05
MOMENTUM = 0.9
AVG_DECAY = 0.8
BF = jnp.bfloat16
F32 = jnp.float32
I32 = jnp.int32
CORE, XBIT, YBIT = 1, 2, 4
LANE = 512
STEP = 16
ROWS = 81
HALF = 96


def step_rates(images, model_width, gate_width, cell_count):
    live_rows = 207.0 * images
    rate_in = 1.0 / (math.sqrt(model_width) * 1.4 * math.sqrt(live_rows))
    rate_out = 1.0 / (math.sqrt(gate_width / 4.0) * 1.2 * math.sqrt(live_rows))
    rate_mix = 1.0 / (math.sqrt(cell_count) * 1.5 * math.sqrt(gate_width * images / 2.0))
    rate_vec = 0.1 / (2.0 * math.sqrt(live_rows))
    return (rate_in, rate_out, rate_mix, rate_vec)


def nesterov(weight, grads, moment, average, rate):
    moment_new = MOMENTUM * moment + grads
    weight_new = weight - rate * (grads + MOMENTUM * moment_new)
    average_new = AVG_DECAY * average + (1.0 - AVG_DECAY) * weight_new
    return (weight_new, moment_new, average_new)


def turn(arr, r):
    n = lax.axis_size("patch")
    return lax.ppermute(arr, "patch", [(s, (s + r) % n) for s in range(n)])


def swap(arr, mask):
    n = lax.axis_size("img")
    return lax.ppermute(arr, "img", [(k, k ^ mask) for k in range(n)])


def dot(a, b, ca=1, cb=0):
    return lax.dot_general(a, b, (((ca,), (cb,)), ((), ())), preferred_element_type=F32)


def aligned(v, by):
    return pl.multiple_of(v, by)


def rows_of(i):
    return pl.ds(aligned(i * STEP, STEP), STEP)


def each_tile(n):
    steps = n // STEP
    return pl.loop(0, steps, unroll=7 if steps % 7 == 0 else 1)


def gelu_parts(pre):
    phi = 0.5 * (1.0 + lax.erf(pre * math.sqrt(0.5)))
    slope = phi + pre * (jnp.exp(-0.5 * pre * pre) * (1.0 / math.sqrt(2.0 * math.pi)))
    return pre * phi, slope


def mean_rows(v):
    return jnp.sum(v, axis=-1, keepdims=True) * (1.0 / v.shape[-1])


def slot_kernel(grid, scal, counts, crops, col_ref, row_ref):
    own = scal[0]
    lane = lax.broadcasted_iota(I32, counts.shape, 1)
    count = jnp.sum(jnp.where(lane == own, counts[...], 0), axis=1, keepdims=True)
    start = crops[own][:, 0:1]
    cells = grid * grid
    side = jnp.zeros_like(count)
    top = jnp.zeros_like(count)
    for k in range(1, grid + 1):
        side = jnp.where(count == k * k, k, side)
        top = top + jnp.where(start >= k * grid, 1, 0)
    quarter = count >> 2
    left = start - top * grid
    for ref, dim in ((col_ref, 0), (row_ref, 1)):
        place = lax.broadcasted_iota(I32, ref.shape, dim)
        row = jnp.zeros(ref.shape, I32)
        for k in range(1, grid):
            row = row + jnp.where(place >= k * grid, 1, 0)
        drow = row - top
        dcol = place - row * grid - left
        inside = (drow >= 0) & (drow < side) & (dcol >= 0) & (dcol < side) & (place < cells)
        order = drow * side + dcol
        block = jnp.zeros(ref.shape, I32)
        for k in (1, 2, 3):
            block = block + jnp.where(order >= k * quarter, 1, 0)
        slot = ((own - block) & 3) * ROWS + order - block * quarter
        ref[...] = jnp.where(inside, slot, -1)


def onehot(slot, lanes, base):
    lane = lax.broadcasted_iota(I32, (slot.shape[0], lanes), 1) + base
    return jnp.where(slot == lane, 1.0, 0.0).astype(BF)


class Copies:
    def __init__(self, sems):
        self.sems, self.all = sems, []

    def bring(self, src, dst):
        copy = pltpu.make_async_copy(src, dst, self.sems.at[len(self.all)])
        copy.start()
        self.all.append(copy)

    def wait(self):
        for copy in self.all:
            copy.wait()


def prep_kernel(grid, scal, counts, crops, tok, w_out, mix, m1, m2, m3, tok_own, col_ref, row_ref, held, strip, sems):
    own, unit = scal[0], scal[1]
    rows = held.shape[0]
    low = rows + STEP
    count = tok.shape[1]
    copies = Copies(sems)
    copies.bring(w_out.at[pl.ds(aligned(unit * rows, STEP), rows), :], held)
    slot_kernel(grid, scal, counts, crops, col_ref, row_ref)
    strip[...] = jnp.zeros_like(strip)
    strip[0 : mix.shape[0], 0 : mix.shape[1]] = mix[...].astype(BF)
    copies.wait()
    for r, msg in enumerate((m1, m2, m3), 1):
        to = lax.rem(own + r, 4)
        msg[0:rows, :] = held[...].astype(BF)
        msg[rows:low, :] = strip[pl.ds(aligned(unit * STEP, STEP), STEP), :]
        msg[low : low + count, :] = tok[to]
    tok_own[...] = tok[own]


def cot_kernel(scal, cot, tie, c0, c1, c2, c3):
    for r, out in enumerate((c0, c1, c2, c3)):
        out[...] = cot[lax.rem(scal[0] + r, 4)]


def hold_kernel(src, tie, dst):
    dst[...] = src[...]


def stack_tied_kernel(m1, m2, m3, tie, out):
    stack_kernel(m1, m2, m3, out)


def join_kernel(p0, p1, p2, p3, tie, out):
    for e, part in enumerate((p0, p1, p2, p3)):
        out[e] = part[...]


def stack_kernel(m1, m2, m3, out):
    for r, msg in enumerate((m1, m2, m3)):
        out[r] = msg[0 : out.shape[1], :]


def place(slot_ref, own, others, at, pos_ref):
    slot = slot_ref[...]
    lanes = own.shape[0]
    total = dot(onehot(slot, lanes, 0), own[...])
    for r, msg in enumerate(others, 1):
        total = total + dot(onehot(slot, lanes, r * lanes), msg[at : at + lanes, :])
    pos_ref[...] = total.astype(BF)


def place_kernel(at, slot_ref, own, m1, m2, m3, tie, pos_ref):
    place(slot_ref, own, (m1, m2, m3), at, pos_ref)


ORDER = [(c, y, x, r) for c in (0, 1) for y in (0, 1) for x in (0, 1) for r in range(4)]


def norm_kernel(at, scal, slot_ref, own_blk, m1, m2, m3, gain, shift, pos_ref, xn_ref, xt_ref, turned):
    place(slot_ref, own_blk, (m1, m2, m3), at, pos_ref)
    own, unit = scal[0], scal[1]

    @each_tile(pos_ref.shape[0])
    def _(i):
        x = pos_ref[rows_of(i), :].astype(F32)
        cen = x - mean_rows(x)
        rstd = lax.rsqrt(mean_rows(cen * cen) + EPS)
        xn_ref[rows_of(i), :] = (cen * rstd * gain[...] + shift[...]).astype(BF)

    turned[...] = xn_ref[...].T
    for k, (c, y, x, r) in enumerate(ORDER):
        who = lax.rem(own + r, 4)
        e = c + 2 * x + 4 * y
        src = who * 128 + (unit ^ e) * STEP
        xt_ref[k * STEP : (k + 1) * STEP, :] = turned[pl.ds(aligned(src, STEP), STEP), :]


def right_kernel(scal, slot_ref, xn_ref, b_in, g_two, s_two, wi_own, *rest):
    wi, rest = rest[:8], rest[9:]
    win, vhat_ref, rstd_ref, slope_v, vn_ref, pre = rest
    own, unit = scal[0], scal[1]
    n, gate = vhat_ref.shape
    tiles = gate // LANE
    win[pl.ds(aligned(own * 128, 128), 128), :] = wi_own[...].astype(BF)
    for e in range(8):
        for r in (1, 2, 3):
            who = lax.rem(own + (4 - r), 4)
            at = who * 128 + (unit ^ e) * STEP
            win[pl.ds(aligned(at, STEP), STEP), :] = wi[e][r - 1]

    xn = xn_ref[...]
    for k in range(tiles):
        cols = slice(k * LANE, (k + 1) * LANE)
        wide = slice(gate + k * LANE, gate + (k + 1) * LANE)
        pre[:, cols] = dot(xn, win[:, wide]) + b_in[:, wide]

    @each_tile(n)
    def _(i):
        rows = rows_of(i)
        v, slope = gelu_parts(pre[rows, :])
        slope_v[rows, :] = slope
        cen = v - mean_rows(v)
        rstd = lax.rsqrt(mean_rows(cen * cen) + EPS)
        vhat = cen * rstd
        vhat_ref[rows, :] = vhat
        rstd_ref[rows, :] = rstd
        vn = jnp.where(slot_ref[rows, :] >= 0, vhat * g_two[...] + s_two[...], 0.0)
        vn_ref[rows, :] = vn.astype(BF)


def left_kernel(xn_ref, b_in, win, *rest):
    u_ref, slope_u, pre = rest[-3:]
    n, gate = u_ref.shape
    xn = xn_ref[...]
    for k in range(gate // LANE):
        cols = slice(k * LANE, (k + 1) * LANE)
        pre[:, cols] = dot(xn, win[:, cols]) + b_in[:, cols]

    @each_tile(n)
    def _(i):
        rows = rows_of(i)
        u, slope = gelu_parts(pre[rows, :])
        u_ref[rows, :] = u
        slope_u[rows, :] = slope


def spatial_kernel(scal, xt_ref, cot_ref, u_ref, slope_u, vn_ref, b_mix, mix_own, wo_own, *rest):
    wo, rest = rest[:2], rest[2:]
    mix_ref, pre_u, sg_ref, gated, wout, keep, send, *rest = rest
    mixp, spat, gtmp = rest
    own, unit = scal[0], scal[1]
    n, gate = u_ref.shape
    tiles = gate // LANE
    out_unit = wout.shape[0] // 32
    wout[pl.ds(aligned(own * 8 * out_unit, STEP), 8 * out_unit), :] = wo_own[...].astype(BF)
    for e in range(8):
        for r in (1, 2, 3):
            who = lax.rem(own + (4 - r), 4)
            at = (who * 8 + (unit ^ e)) * out_unit
            wout[pl.ds(aligned(at, STEP), out_unit), :] = wo[e % 2][e // 2, r - 1, 0:out_unit, :]
            at = who * 128 + (unit ^ e) * STEP
            mixp[pl.ds(aligned(at, STEP), STEP), :] = wo[e % 2][e // 2, r - 1, out_unit:, :]
    per, cells = mix_own.shape
    mine = aligned(own * 128, 128)
    mixp[pl.ds(mine, 128), :] = jnp.zeros((128, LANE), BF)
    mixp[pl.ds(mine, per), 0:cells] = mix_own[...].astype(BF)
    cell = lax.broadcasted_iota(I32, (n, mixp.shape[0]), 0)
    lane = lax.broadcasted_iota(I32, (n, mixp.shape[0]), 1)
    part = jnp.where(cell >= per, 1, 0) + jnp.where(cell >= 2 * per, 1, 0) + jnp.where(cell >= 3 * per, 1, 0)
    pick = jnp.where(lane == cell + part * (128 - per), 1.0, 0.0).astype(BF)
    mix_ref[...] = dot(pick, mixp[:, :n]).astype(BF)
    mix = mix_ref[...]
    for k in range(tiles):
        cols = slice(k * LANE, (k + 1) * LANE)
        sp = dot(mix, vn_ref[:, cols]) + b_mix[...]
        spat[:, cols] = sp
        gated[:, cols] = (u_ref[:, cols] * sp).astype(BF)

    cot = cot_ref[...]
    for k in range(tiles):
        cols = slice(k * LANE, (k + 1) * LANE)
        gg = dot(cot, wout[cols, :], 1, 1)
        sg_ref[:, cols] = (gg * u_ref[:, cols]).astype(BF)
        pre_u[:, cols] = (gg * spat[:, cols] * slope_u[:, cols]).astype(BF)

    low = out_unit + STEP
    for k in range(tiles):
        rows = slice(k * LANE, (k + 1) * LANE)
        gtmp[rows, :] = dot(gated[:, rows], cot, 0, 0).astype(BF)
    height = keep.shape[1] // 4
    for c, dst in ((0, keep), (1, send)):
        for e in range(4):
            for r in range(4):
                at = (lax.rem(own + r, 4) * 8 + (unit ^ (c + 2 * e))) * out_unit
                dst[e, r * height : r * height + out_unit, :] = gtmp[pl.ds(aligned(at, STEP), out_unit), :]
    gmix = dot(sg_ref[...], vn_ref[...], 1, 1).astype(BF)
    big = lax.broadcasted_iota(I32, (512, n), 0)
    lane = lax.broadcasted_iota(I32, (512, n), 1)
    within = ((big >> 6) ^ unit) * STEP + (big & 15)
    a = (((big >> 4) + own) & 3) * per + within
    pick = jnp.where((lane == a) & (within < per), 1.0, 0.0).astype(BF)
    padded = dot(pick, gmix).astype(BF)
    for c, dst in ((0, keep), (1, send)):
        for e in range(4):
            for r in range(4):
                at = (c + 2 * e) * 64 + r * STEP
                to = r * height + out_unit
                dst[e, to : to + STEP, :] = jnp.zeros((STEP, LANE), BF)
                dst[e, to : to + STEP, 0:n] = padded[at : at + STEP, :]
    for k in range(tiles):
        cols = slice(k * LANE, (k + 1) * LANE)
        part = dot(xt_ref[...], pre_u[:, cols]).astype(BF)
        for j, (c, y, x, r) in enumerate(ORDER):
            to = r * height + low + k * STEP
            (send if c else keep)[x + 2 * y, to : to + STEP, :] = part[j * STEP : (j + 1) * STEP, :]


def back_kernel(slot_ref, xt_ref, mix_ref, sg_ref, vhat_ref, rstd_ref, slope_v, g_two, pre_v, keep, send, rows_ref, vng, gain, shift):
    n, gate = vhat_ref.shape
    tiles = gate // LANE
    mix = mix_ref[...]
    for k in range(tiles):
        cols = slice(k * LANE, (k + 1) * LANE)
        vng[:, cols] = dot(mix, sg_ref[:, cols], 0, 0)
    gain[...] = jnp.zeros_like(gain)
    shift[...] = jnp.zeros_like(shift)

    @each_tile(n)
    def _(i):
        rows = rows_of(i)
        vg = jnp.where(slot_ref[rows, :] >= 0, vng[rows, :], 0.0)
        vhat = vhat_ref[rows, :]
        gain[...] += jnp.sum((vg * vhat).reshape(2, 8, gate), 0)
        shift[...] += jnp.sum(vg.reshape(2, 8, gate), 0)
        h = vg * g_two[...]
        v_grad = rstd_ref[rows, :] * (h - mean_rows(h) - vhat * mean_rows(h * vhat))
        pre_v[rows, :] = (v_grad * slope_v[rows, :]).astype(BF)

    height = keep.shape[1] // 4
    for k in range(tiles):
        cols = slice(k * LANE, (k + 1) * LANE)
        part = dot(xt_ref[...], pre_v[:, cols]).astype(BF)
        for j, (c, y, x, r) in enumerate(ORDER):
            to = r * height + k * STEP
            (send if c else keep)[x + 2 * y, to : to + STEP, :] = part[j * STEP : (j + 1) * STEP, :]
        rows_ref[k : k + 1, :] = jnp.sum(gain[:, cols], 0, keepdims=True)
        rows_ref[tiles + k : tiles + k + 1, :] = jnp.sum(shift[:, cols], 0, keepdims=True)


def token_kernel(slot_ref, slot_row, pos_ref, cot_ref, win, pre_u, pre_v, sg_ref, gated, wout, g_one, b_out, rows_ref, *rest):
    _, h0, h1, h2, h3, vec, xg, out_ref, in_ref, gain, shift = rest
    n, gate = pre_u.shape
    xg[...] = dot(pre_u[...], win[:, :gate], 1, 1) + dot(pre_v[...], win[:, gate:], 1, 1)
    gain[...] = jnp.zeros_like(gain)
    shift[...] = jnp.zeros_like(shift)
    width = xg.shape[1]

    @each_tile(n)
    def _(i):
        rows = rows_of(i)
        x = pos_ref[rows, :].astype(F32)
        cen = x - mean_rows(x)
        rstd = lax.rsqrt(mean_rows(cen * cen) + EPS)
        xhat = cen * rstd
        g = xg[rows, :]
        gain[...] += jnp.sum((g * xhat).reshape(2, 8, width), 0)
        shift[...] += jnp.sum(g.reshape(2, 8, width), 0)
        h = g * g_one[...]
        x_grad = rstd * (h - mean_rows(h) - xhat * mean_rows(h * xhat))
        total = cot_ref[rows, :].astype(F32) + x_grad
        in_ref[rows, :] = jnp.where(slot_ref[rows, :] >= 0, total, 0.0).astype(BF)

    branch = dot(gated[...], wout[...]) + b_out[...]
    out_ref[...] = jnp.where(slot_ref[...] >= 0, pos_ref[...].astype(F32) + branch, 0.0).astype(BF)
    for r, dst in enumerate((h0, h1, h2, h3)):
        spot = lax.broadcasted_iota(I32, (ROWS, n), 0) + r * ROWS
        pick = jnp.where(slot_row[...] == spot, 1.0, 0.0).astype(BF)
        dst[0:ROWS, :] = dot(pick, out_ref[...]).astype(BF)
        dst[HALF : HALF + ROWS, :] = dot(pick, in_ref[...]).astype(BF)

    ones = jnp.ones((8, n), BF)
    tiles = gate // LANE
    vec[0:1, :] = jnp.sum(gain[...], 0, keepdims=True)
    vec[1:2, :] = jnp.sum(shift[...], 0, keepdims=True)
    for k in range(tiles):
        cols = slice(k * LANE, (k + 1) * LANE)
        vec[2 + k : 3 + k, :] = dot(ones, pre_u[:, cols])[0:1]
        vec[2 + tiles + k : 3 + tiles + k, :] = dot(ones, pre_v[:, cols])[0:1]
    at = 2 + 2 * tiles
    vec[at : at + 2 * tiles, :] = rows_ref[...]
    at += 2 * tiles
    cells = 4 * ROWS
    lane = lax.broadcasted_iota(I32, (1, LANE), 1)
    last = pltpu.roll(dot(ones, cot_ref[...])[0:1], cells, 1)
    vec[at : at + 1, 0:n] = dot(jnp.ones((8, gate), BF), sg_ref[...], 1, 1)[0:1]
    vec[at : at + 1, :] = jnp.where(lane < cells, vec[at : at + 1, :], last)
    vec[at + 1 : at + 2, :] = jnp.where(lane < cells, last, 0.0)


def split_low(v):
    high = v.astype(BF)
    return high, (v - high.astype(F32)).astype(BF)


def put_vec(ref, at, v):
    high, low = split_low(v)
    ref[at : at + STEP, :] = high
    ref[at + STEP : at + 2 * STEP, :] = low


def get_vec(ref, at):
    return ref[at : at + STEP, :].astype(F32) + ref[at + STEP : at + 2 * STEP, :].astype(F32)


def core_kernel(keep, got, own, s1, s2, s3):
    for e, dst in enumerate((own, s1, s2, s3)):
        dst[...] = (keep[e].astype(F32) + got[e].astype(F32)).astype(dst.dtype)


def core_vec_kernel(keep, got, vec, vec_got, tie, own, s1, s2, s3, vec_own):
    rows = own.shape[0]
    total = vec[...] + vec_got[...]
    put_vec(vec_own, 0, total)
    for e, dst in enumerate((own, s1, s2, s3)):
        dst[0:rows, :] = (keep[e].astype(F32) + got[e].astype(F32)).astype(dst.dtype)
        if e:
            put_vec(dst, rows, total)


def plane_kernel(own, g1, g2, g3, z0, z1, z2, z3):
    rows = z0.shape[0]
    for r, dst in enumerate((z0, z1, z2, z3)):
        at = slice(r * rows, (r + 1) * rows)
        total = (own[at, :] + g1[at, :].astype(F32)) + (g2[at, :].astype(F32) + g3[at, :].astype(F32))
        dst[...] = total.astype(dst.dtype)


def plane_vec_kernel(own, vec_own, g1, g2, g3, tie, z0, z1, z2, z3, vec_out):
    rows, at = z0.shape[0], own.shape[0]
    vec = (get_vec(vec_own, 0) + get_vec(g1, at)) + (get_vec(g2, at) + get_vec(g3, at))
    put_vec(vec_out, 0, vec)
    for r, dst in enumerate((z0, z1, z2, z3)):
        at = slice(r * rows, (r + 1) * rows)
        total = (own[at, :] + g1[at, :].astype(F32)) + (g2[at, :].astype(F32) + g3[at, :].astype(F32))
        dst[0:rows, :] = total.astype(dst.dtype)
        if r:
            put_vec(dst, rows, vec)


def patch_kernel(own, g1, g2, g3, out):
    rows = own.shape[0]
    total = own[...]
    for g in (g1, g2, g3):
        total = total + g[0:rows, :].astype(F32)
    out[...] = total.astype(out.dtype)


def patch_vec_kernel(scal, own, vec_own, g1, g2, g3, tie, tie_home, out, vec_out, held):
    patch_kernel(own, g1, g2, g3, out)
    rows = own.shape[0]
    me = scal[0]
    held[me] = get_vec(vec_own, 0)
    for r, g in enumerate((g1, g2, g3), 1):
        held[lax.rem(me + (4 - r), 4)] = get_vec(g, rows)
    vec_out[...] = (held[0] + held[1]) + (held[2] + held[3])


def home_kernel(scal, h0, h1, h2, h3, out_ref, grad_ref, held):
    for r, h in enumerate((h0, h1, h2, h3)):
        m = lax.rem(scal[0] + r, 4)
        held[m] = h[0:ROWS, :]
        grad_ref[m, :, 0, :] = h[HALF : HALF + ROWS, :].astype(F32)
    for m in range(4):
        out_ref[:, m, :] = held[m]


def update_kernel(rates, first, second, *rest):
    olds, rest = rest[:9], rest[9:]
    news, rest = rest[:9], rest[9:]
    made, sems = rest[:9], rest[9]
    copies = Copies(sems)
    out_unit = olds[3].shape[0] // 8
    low = out_unit + STEP

    def step(which, rows, cols, grads):
        old, new = olds[3 * which : 3 * which + 3], made[3 * which : 3 * which + 3]
        at = (slice(*rows), slice(*cols))
        fresh = nesterov(old[0][at], grads.astype(F32), old[1][at], old[2][at], rates[which])
        for ref, value in zip(new, fresh):
            ref[at] = value

    def send(which):
        for j in range(3 * which, 3 * which + 3):
            copies.bring(made[j], news[j])

    width = olds[3].shape[1]
    for u in range(8):
        step(1, (u * out_unit, (u + 1) * out_unit), (0, width), first[u, 0:out_unit, :])
    send(1)
    mix_rows, cells = olds[6].shape
    for u in range(-(-mix_rows // STEP)):
        rows = min(STEP, mix_rows - u * STEP)
        step(2, (u * STEP, u * STEP + rows), (0, cells), first[u, out_unit : out_unit + rows, 0:cells])
    send(2)
    tiles = olds[0].shape[1] // LANE
    for u in range(8):
        for k in range(tiles):
            if k < tiles // 2:
                grads = first[u, low + k * STEP : low + (k + 1) * STEP, :]
            else:
                j = k - tiles // 2
                grads = second[u, j * STEP : (j + 1) * STEP, :]
            step(0, (u * STEP, (u + 1) * STEP), (k * LANE, (k + 1) * LANE), grads)
    send(0)
    copies.wait()


VM = pl.BlockSpec(memory_space=pltpu.VMEM)
SM = pl.BlockSpec(memory_space=pltpu.SMEM)
ANY = pl.BlockSpec(memory_space=pl.ANY)


def call(body, ins, outs, scratch=(), specs=None, out_specs=None, flops=100_000_000, limit=16, name=None):
    moved = sum(math.prod(a.shape) * a.dtype.itemsize for a in ins)
    return pl.pallas_call(
        body,
        out_shape=[jax.ShapeDtypeStruct(s, d) for s, d in outs],
        in_specs=specs or [VM] * len(ins),
        out_specs=out_specs or [VM] * len(outs),
        scratch_shapes=list(scratch),
        compiler_params=pltpu.CompilerParams(vmem_limit_bytes=limit * 2**20),
        cost_estimate=pl.CostEstimate(flops=flops, bytes_accessed=moved, transcendentals=0),
        name=name,
    )(*ins)


def rest_of_img(total):
    mask = 8
    while mask < lax.axis_size("img"):
        total = total + swap(total, mask)
        mask *= 2
    return total


def img_gather(arr):
    size = lax.axis_size("img")
    groups = [[g * 8 + k for k in range(8)] for g in range(size // 8)]
    return lax.all_gather(arr, "img", axis_index_groups=groups)


def shards(
    tokens,
    cotangent,
    patch_count,
    crop_index,
    in_weight,
    in_moment,
    in_average,
    out_weight,
    out_moment,
    out_average,
    spatial_weight,
    spatial_moment,
    spatial_average,
    vectors,
    vector_moment,
    vector_average,
):
    p = lax.axis_index("patch")
    unit = lax.axis_index("img") % 8
    micro_count, slot_count, row_count, width = tokens.shape
    hidden = in_weight.shape[1]
    gate = hidden // 2
    mix_rows, cells = spatial_weight.shape
    assert micro_count == lax.axis_size("patch") == 4 and slot_count == 1
    assert width == LANE and in_weight.shape[0] == 128 and row_count == mix_rows == 81
    grid = math.isqrt(cells)
    n = -(-cells // STEP) * STEP
    in_unit = in_weight.shape[0] // 8
    out_unit = out_weight.shape[0] // 8
    low = out_unit + STEP
    side_rows = in_unit * gate // LANE
    scal = jnp.stack([p, unit]).astype(I32)

    def over_plane(base):
        near = swap(base, XBIT)
        chips = [base, near, swap(base, YBIT), swap(near, YBIT)]
        found = []
        for arr in chips:
            found += [arr, swap(arr, CORE)]
        return found

    wi_piece = lax.dynamic_slice_in_dim(in_weight, unit * in_unit, in_unit, 0).astype(BF)

    blk = ((row_count, width), BF)
    msg = ((low + row_count, width), BF)
    m1, m2, m3, tok_own, slot_col, slot_row = call(
        functools.partial(prep_kernel, grid),
        [scal, patch_count.reshape(1, 4), crop_index, tokens.reshape(4, row_count, width), out_weight, spatial_weight],
        [msg, msg, msg, blk, ((n, 1), I32), ((1, n), I32)],
        [pltpu.VMEM((out_unit, width), F32), pltpu.VMEM((128, LANE), BF), pltpu.SemaphoreType.DMA((1,))],
        specs=[SM, VM, VM, VM, ANY, VM],
        limit=8,
        name="prep",
    )
    (base_in,) = call(
        stack_tied_kernel,
        [turn(wi_piece, r) for r in (1, 2, 3)] + [m1],
        [((3, in_unit, hidden), BF)],
        specs=[VM] * 3 + [ANY],
        limit=8,
        name="stack_i",
    )
    wi = over_plane(base_in)
    got = [turn(m, r) for r, m in enumerate((m1, m2, m3), 1)]
    (base,) = call(stack_tied_kernel, [*got, wi[2]], [((3, low, LANE), BF)], specs=[VM] * 3 + [ANY], limit=8, name="stack_o")
    cot = call(
        cot_kernel,
        [scal, cotangent.reshape(4, row_count, width), base],
        [blk] * 4,
        specs=[SM, VM, ANY],
        limit=8,
        name="prep_cot",
    )
    cot = [cot[0]] + [turn(c, r) for r, c in enumerate(cot[1:], 1)]
    plane_out = [base] + [swap(base, m) for m in (2, 4, 6)]

    bounds = [width, width, hidden, gate, gate, cells, width]
    pieces = []
    offset = 0
    for length in bounds:
        pieces.append(vectors[None, offset : offset + length])
        offset += length
    g_one, s_one, b_in, g_two, s_two, b_mix, b_out = pieces
    b_mix = jnp.pad(b_mix[0], (0, n - cells))[:, None]

    pos, xn, xt = call(
        functools.partial(norm_kernel, low),
        [scal, slot_col, tok_own, *got, g_one, s_one],
        [((n, width), BF), ((n, width), BF), ((width, n), BF)],
        [pltpu.VMEM((width, n), BF)],
        specs=[SM] + [VM] * 7,
        name="norm_in",
    )
    sized = lambda kind: ((n, gate), kind)
    (cot_pos,) = call(
        functools.partial(place_kernel, 0),
        [slot_col, *cot, xn],
        [((n, width), BF)],
        specs=[VM] * 5 + [ANY],
        name="place_cot",
    )
    win, vhat, rstd, slope_v, vn = call(
        right_kernel,
        [scal, slot_col, xn, b_in, g_two, s_two, in_weight, *wi, cot_pos],
        [((width, hidden), BF), sized(F32), ((n, 1), F32), sized(F32), sized(BF)],
        [pltpu.VMEM((n, gate), F32)],
        specs=[SM] + [VM] * 14 + [ANY],
        flops=1_500_000_000,
        limit=20,
        name="right",
    )
    (joined,) = call(
        join_kernel, [*plane_out, vn], [((4, 3, low, LANE), BF)], specs=[VM] * 4 + [ANY], limit=8, name="join"
    )
    u, slope_u = call(
        left_kernel,
        [xn, b_in, win, joined],
        [sized(F32), sized(F32)],
        [pltpu.VMEM((n, gate), F32)],
        specs=[VM] * 3 + [ANY],
        flops=1_000_000_000,
        limit=16,
        name="left",
    )
    packed = ((4, 4 * (low + side_rows), LANE), BF)
    mix, pre_u, sg, gated, wout, keep_a, send_a = call(
        spatial_kernel,
        [scal, xt, cot_pos, u, slope_u, vn, b_mix, spatial_weight, out_weight, joined, swap(joined, CORE)],
        [((n, n), BF), sized(BF), sized(BF), sized(BF), ((gate, width), BF), packed, packed],
        [
            pltpu.VMEM((512, LANE), BF),
            pltpu.VMEM((n, gate), F32),
            pltpu.VMEM((gate, width), BF),
        ],
        specs=[SM] + [VM] * 10,
        flops=4_000_000_000,
        limit=24,
        name="spatial",
    )
    core_a = swap(send_a, CORE)
    half = ((4, 4 * side_rows, LANE), BF)
    pre_v, keep_b, send_b, rows_b = call(
        back_kernel,
        [slot_col, xt, mix, sg, vhat, rstd, slope_v, g_two],
        [sized(BF), half, half, ((6, LANE), F32)],
        [pltpu.VMEM((n, gate), F32), pltpu.VMEM((8, gate), F32), pltpu.VMEM((8, gate), F32)],
        flops=2_000_000_000,
        limit=20,
        name="back",
    )
    core_b = swap(send_b, CORE)
    rows_a, rows_b4 = 4 * (low + side_rows), 4 * side_rows
    own_a, *send_a = call(
        core_kernel, [keep_a, core_a], [((rows_a, LANE), F32)] + [((rows_a, LANE), BF)] * 3, limit=12, name="core_a"
    )
    plane_a = [swap(s, m) for s, m in zip(send_a, (2, 4, 6))]
    *home, vec = call(
        token_kernel,
        [slot_col, slot_row, pos, cot_pos, win, pre_u, pre_v, sg, gated, wout, g_one, b_out, rows_b, send_a[2]],
        [((HALF + row_count, width), BF)] * 4 + [((STEP, LANE), F32)],
        [
            pltpu.VMEM((n, width), F32),
            pltpu.VMEM((n, width), BF),
            pltpu.VMEM((n, width), BF),
            pltpu.VMEM((8, width), F32),
            pltpu.VMEM((8, width), F32),
        ],
        specs=[VM] * 13 + [ANY],
        flops=2_000_000_000,
        limit=20,
        name="token_grad",
    )
    vec_got = swap(vec, CORE)
    own_b, *send_b, vec_own = call(
        core_vec_kernel,
        [keep_b, core_b, vec, vec_got, send_a[0]],
        [((rows_b4, LANE), F32)] + [((rows_b4 + 2 * STEP, LANE), BF)] * 3 + [((2 * STEP, LANE), BF)],
        specs=[VM] * 4 + [ANY],
        name="core_b",
    )
    plane_b = [swap(s, m) for s, m in zip(send_b, (2, 4, 6))]
    home = [home[0]] + [turn(h, -r) for r, h in enumerate(home[1:], 1)]
    out_tokens, in_grad = call(
        home_kernel,
        [scal, *home],
        [((row_count, 4, width), BF), ((4, row_count, 1, width), F32)],
        [pltpu.VMEM((4, row_count, width), BF)],
        specs=[SM] + [VM] * 4,
        limit=8,
        name="home",
    )
    z_rows = low + side_rows
    own_a, *patch_a = call(
        plane_kernel, [own_a, *plane_a], [((z_rows, LANE), F32)] + [((z_rows, LANE), BF)] * 3, name="plane_a"
    )
    got_a = [turn(z, r) for r, z in enumerate(patch_a, 1)]
    own_b, *patch_b, vec_own = call(
        plane_vec_kernel,
        [own_b, vec_own, *plane_b, patch_a[0]],
        [((side_rows, LANE), F32)] + [((side_rows + 2 * STEP, LANE), BF)] * 3 + [((2 * STEP, LANE), BF)],
        specs=[VM] * 5 + [ANY],
        name="plane_b",
    )
    got_b = [turn(z, r) for r, z in enumerate(patch_b, 1)]
    kind = BF if lax.axis_size("img") == 8 else F32
    (first,) = call(patch_kernel, [own_a, *got_a], [((z_rows, LANE), kind)], name="patch_a")
    first = img_gather(rest_of_img(first).astype(BF))
    second, vec_sum = call(
        patch_vec_kernel,
        [scal, own_b, vec_own, *got_b, first, in_grad],
        [((side_rows, LANE), kind), ((STEP, LANE), F32)],
        [pltpu.VMEM((4, STEP, LANE), F32)],
        specs=[SM] + [VM] * 5 + [ANY] * 2,
        name="patch_b",
    )
    second = img_gather(rest_of_img(second).astype(BF))
    vec_sum = rest_of_img(vec_sum).reshape(STEP * LANE)

    vec_sum = vec_sum[: vectors.shape[0]]

    images = micro_count * slot_count * lax.axis_size("img")
    rate_in, rate_out, rate_mix, rate_vec = step_rates(images, width, gate, cells)
    olds = [in_weight, in_moment, in_average, out_weight, out_moment, out_average]
    olds += [spatial_weight, spatial_moment, spatial_average]
    news = call(
        functools.partial(update_kernel, (rate_in, rate_out, rate_mix)),
        [first, second, *olds],
        [(a.shape, F32) for a in olds],
        [pltpu.VMEM(a.shape, F32) for a in olds] + [pltpu.SemaphoreType.DMA((9,))],
        specs=[VM] * 11,
        out_specs=[ANY] * 9,
        limit=20,
        name="update",
    )
    vec_new = nesterov(vectors, vec_sum, vector_moment, vector_average, rate_vec)
    return (out_tokens.transpose(1, 0, 2).reshape(tokens.shape), in_grad.transpose(0, 2, 1, 3), *news, *vec_new)


def solution(mesh):
    rows = P("patch", None)
    act = P(None, "img", "patch", None)
    return jax.shard_map(
        shards,
        mesh=mesh,
        in_specs=(act, act, P(None, "img"), P(None, "img", None), *([rows] * 9), P(), P(), P()),
        out_specs=(act, act, *([rows] * 9), P(), P(), P()),
        check_vma=False,
    )
```

```python
import functools
import math

import jax
import jax.numpy as jnp
from jax import lax
from jax.experimental import pallas as pl
from jax.experimental.pallas import tpu as pltpu
from jax.sharding import PartitionSpec as P

EPS = 1e-05
MOMENTUM = 0.9
AVG_DECAY = 0.8
BF = jnp.bfloat16
F32 = jnp.float32
I32 = jnp.int32
CORE, XBIT, YBIT = 1, 2, 4
LANE = 512
STEP = 16
ROWS = 81
HALF = 96


def step_rates(images, model_width, gate_width, cell_count):
    live_rows = 207.0 * images
    rate_in = 1.0 / (math.sqrt(model_width) * 1.4 * math.sqrt(live_rows))
    rate_out = 1.0 / (math.sqrt(gate_width / 4.0) * 1.2 * math.sqrt(live_rows))
    rate_mix = 1.0 / (math.sqrt(cell_count) * 1.5 * math.sqrt(gate_width * images / 2.0))
    rate_vec = 0.1 / (2.0 * math.sqrt(live_rows))
    return (rate_in, rate_out, rate_mix, rate_vec)


def nesterov(weight, grads, moment, average, rate):
    moment_new = MOMENTUM * moment + grads
    weight_new = weight - rate * (grads + MOMENTUM * moment_new)
    average_new = AVG_DECAY * average + (1.0 - AVG_DECAY) * weight_new
    return (weight_new, moment_new, average_new)


def turn(arr, r):
    n = lax.axis_size("patch")
    return lax.ppermute(arr, "patch", [(s, (s + r) % n) for s in range(n)])


def swap(arr, mask):
    n = lax.axis_size("img")
    return lax.ppermute(arr, "img", [(k, k ^ mask) for k in range(n)])


def dot(a, b, ca=1, cb=0):
    return lax.dot_general(a, b, (((ca,), (cb,)), ((), ())), preferred_element_type=F32)


def aligned(v, by):
    return pl.multiple_of(v, by)


def rows_of(i):
    return pl.ds(aligned(i * STEP, STEP), STEP)


def each_tile(n):
    steps = n // STEP
    return pl.loop(0, steps, unroll=7 if steps % 7 == 0 else 1)


def gelu_parts(pre):
    phi = 0.5 * (1.0 + lax.erf(pre * math.sqrt(0.5)))
    slope = phi + pre * (jnp.exp(-0.5 * pre * pre) * (1.0 / math.sqrt(2.0 * math.pi)))
    return pre * phi, slope


def mean_rows(v):
    return jnp.sum(v, axis=-1, keepdims=True) * (1.0 / v.shape[-1])


def slot_kernel(grid, scal, counts, crops, col_ref, row_ref):
    own = scal[0]
    lane = lax.broadcasted_iota(I32, counts.shape, 1)
    count = jnp.sum(jnp.where(lane == own, counts[...], 0), axis=1, keepdims=True)
    start = crops[own][:, 0:1]
    cells = grid * grid
    side = jnp.zeros_like(count)
    top = jnp.zeros_like(count)
    for k in range(1, grid + 1):
        side = jnp.where(count == k * k, k, side)
        top = top + jnp.where(start >= k * grid, 1, 0)
    quarter = count >> 2
    left = start - top * grid
    for ref, dim in ((col_ref, 0), (row_ref, 1)):
        place = lax.broadcasted_iota(I32, ref.shape, dim)
        row = jnp.zeros(ref.shape, I32)
        for k in range(1, grid):
            row = row + jnp.where(place >= k * grid, 1, 0)
        drow = row - top
        dcol = place - row * grid - left
        inside = (drow >= 0) & (drow < side) & (dcol >= 0) & (dcol < side) & (place < cells)
        order = drow * side + dcol
        block = jnp.zeros(ref.shape, I32)
        for k in (1, 2, 3):
            block = block + jnp.where(order >= k * quarter, 1, 0)
        slot = ((own - block) & 3) * ROWS + order - block * quarter
        ref[...] = jnp.where(inside, slot, -1)


def onehot(slot, lanes, base):
    lane = lax.broadcasted_iota(I32, (slot.shape[0], lanes), 1) + base
    return jnp.where(slot == lane, 1.0, 0.0).astype(BF)


def side_kernel(scal, slot_ref, m0, m1, m2, m3, xn_ref, tie, pos_ref, xt_ref, turned):
    place_kernel(slot_ref, m0, m1, m2, m3, pos_ref)
    own, unit = scal[0], scal[1]
    turned[...] = xn_ref[...].T
    for k, (c, y, x, r) in enumerate(ORDER):
        who = lax.rem(own + r, 4)
        e = c + 2 * x + 4 * y
        src = who * 128 + (unit ^ e) * STEP
        xt_ref[k * STEP : (k + 1) * STEP, :] = turned[pl.ds(aligned(src, STEP), STEP), :]


class Copies:
    def __init__(self, sems):
        self.sems, self.all = sems, []

    def bring(self, src, dst):
        copy = pltpu.make_async_copy(src, dst, self.sems.at[len(self.all)])
        copy.start()
        self.all.append(copy)

    def wait(self):
        for copy in self.all:
            copy.wait()


def out_kernel(grid, scal, counts, crops, w_out, mix, msg, col_ref, row_ref, held, strip, sems):
    unit = scal[1]
    rows = held.shape[0]
    copies = Copies(sems)
    copies.bring(w_out.at[pl.ds(aligned(unit * rows, STEP), rows), :], held)
    slot_kernel(grid, scal, counts, crops, col_ref, row_ref)
    strip[...] = jnp.zeros_like(strip)
    strip[0 : mix.shape[0], 0 : mix.shape[1]] = mix[...].astype(BF)
    copies.wait()
    msg[0:rows, :] = held[...].astype(BF)
    msg[rows:, :] = strip[pl.ds(aligned(unit * STEP, STEP), STEP), :]


def rows_kernel(scal, tok, cot, tie, m0, m1, m2, m3):
    for r, msg in enumerate((m0, m1, m2, m3)):
        to = lax.rem(scal[0] + r, 4)
        msg[0:ROWS, :] = tok[to]
        msg[HALF : HALF + ROWS, :] = cot[to]


def hold_kernel(src, tie, dst):
    dst[...] = src[...]


def stack_tied_kernel(m1, m2, m3, tie, out):
    stack_kernel(m1, m2, m3, out)


def join_kernel(p0, p1, p2, p3, out):
    for e, part in enumerate((p0, p1, p2, p3)):
        out[e] = part[...]


def join_tied_kernel(p0, p1, p2, p3, tie, out):
    join_kernel(p0, p1, p2, p3, out)


def stack_kernel(m1, m2, m3, out):
    for r, msg in enumerate((m1, m2, m3)):
        out[r] = msg[0 : out.shape[1], :]


def place(slot_ref, blocks, at, pos_ref):
    slot = slot_ref[...]
    total = None
    for r, msg in enumerate(blocks):
        part = dot(onehot(slot, ROWS, r * ROWS), msg[at : at + ROWS, :])
        total = part if total is None else total + part
    pos_ref[...] = total.astype(BF)


def place_kernel(slot_ref, m0, m1, m2, m3, pos_ref):
    place(slot_ref, (m0, m1, m2, m3), HALF, pos_ref)


ORDER = [(c, y, x, r) for c in (0, 1) for y in (0, 1) for x in (0, 1) for r in range(4)]


def norm_kernel(slot_ref, m0, m1, m2, m3, gain, shift, pos_ref, xn_ref):
    place(slot_ref, (m0, m1, m2, m3), 0, pos_ref)
    @each_tile(pos_ref.shape[0])
    def _(i):
        x = pos_ref[rows_of(i), :].astype(F32)
        cen = x - mean_rows(x)
        rstd = lax.rsqrt(mean_rows(cen * cen) + EPS)
        xn_ref[rows_of(i), :] = (cen * rstd * gain[...] + shift[...]).astype(BF)


def right_kernel(scal, slot_ref, xn_ref, b_in, g_two, s_two, wi_own, *rest):
    wi, rest = rest[:8], rest[8:]
    win, vhat_ref, rstd_ref, slope_v, vn_ref, pre = rest
    own, unit = scal[0], scal[1]
    n, gate = vhat_ref.shape
    tiles = gate // LANE
    win[pl.ds(aligned(own * 128, 128), 128), :] = wi_own[...].astype(BF)
    for e in range(8):
        for r in (1, 2, 3):
            who = lax.rem(own + (4 - r), 4)
            at = who * 128 + (unit ^ e) * STEP
            win[pl.ds(aligned(at, STEP), STEP), :] = wi[e][r - 1]

    xn = xn_ref[...]
    for k in range(tiles):
        cols = slice(k * LANE, (k + 1) * LANE)
        wide = slice(gate + k * LANE, gate + (k + 1) * LANE)
        pre[:, cols] = dot(xn, win[:, wide]) + b_in[:, wide]

    @each_tile(n)
    def _(i):
        rows = rows_of(i)
        v, slope = gelu_parts(pre[rows, :])
        slope_v[rows, :] = slope
        cen = v - mean_rows(v)
        rstd = lax.rsqrt(mean_rows(cen * cen) + EPS)
        vhat = cen * rstd
        vhat_ref[rows, :] = vhat
        rstd_ref[rows, :] = rstd
        vn = jnp.where(slot_ref[rows, :] >= 0, vhat * g_two[...] + s_two[...], 0.0)
        vn_ref[rows, :] = vn.astype(BF)


def left_kernel(xn_ref, b_in, win, *rest):
    u_ref, slope_u, pre = rest[-3:]
    n, gate = u_ref.shape
    xn = xn_ref[...]
    for k in range(gate // LANE):
        cols = slice(k * LANE, (k + 1) * LANE)
        pre[:, cols] = dot(xn, win[:, cols]) + b_in[:, cols]

    @each_tile(n)
    def _(i):
        rows = rows_of(i)
        u, slope = gelu_parts(pre[rows, :])
        u_ref[rows, :] = u
        slope_u[rows, :] = slope


def spatial_kernel(scal, xt_ref, cot_ref, u_ref, slope_u, vn_ref, b_mix, mix_own, wo_own, *rest):
    wo, rest = rest[:2], rest[2:]
    mix_ref, pre_u, sg_ref, gated, wout, keep, send, *rest = rest
    mixp, spat, gtmp = rest
    own, unit = scal[0], scal[1]
    n, gate = u_ref.shape
    tiles = gate // LANE
    out_unit = wout.shape[0] // 32
    wout[pl.ds(aligned(own * 8 * out_unit, STEP), 8 * out_unit), :] = wo_own[...].astype(BF)
    for k in range(4):
        for c in (0, 1):
            piece = 2 * k + ((unit & 1) ^ c)
            for r in (1, 2, 3):
                who = lax.rem(own + (4 - r), 4)
                at = (who * 8 + piece) * out_unit
                wout[pl.ds(aligned(at, STEP), out_unit), :] = wo[c][k, r - 1, 0:out_unit, :]
                at = who * 128 + piece * STEP
                mixp[pl.ds(aligned(at, STEP), STEP), :] = wo[c][k, r - 1, out_unit:, :]
    per, cells = mix_own.shape
    mine = aligned(own * 128, 128)
    mixp[pl.ds(mine, 128), :] = jnp.zeros((128, LANE), BF)
    mixp[pl.ds(mine, per), 0:cells] = mix_own[...].astype(BF)
    cell = lax.broadcasted_iota(I32, (n, mixp.shape[0]), 0)
    lane = lax.broadcasted_iota(I32, (n, mixp.shape[0]), 1)
    part = jnp.where(cell >= per, 1, 0) + jnp.where(cell >= 2 * per, 1, 0) + jnp.where(cell >= 3 * per, 1, 0)
    pick = jnp.where(lane == cell + part * (128 - per), 1.0, 0.0).astype(BF)
    mix_ref[...] = dot(pick, mixp[:, :n]).astype(BF)
    mix = mix_ref[...]
    for k in range(tiles):
        cols = slice(k * LANE, (k + 1) * LANE)
        sp = dot(mix, vn_ref[:, cols]) + b_mix[...]
        spat[:, cols] = sp
        gated[:, cols] = (u_ref[:, cols] * sp).astype(BF)

    cot = cot_ref[...]
    for k in range(tiles):
        cols = slice(k * LANE, (k + 1) * LANE)
        gg = dot(cot, wout[cols, :], 1, 1)
        sg_ref[:, cols] = (gg * u_ref[:, cols]).astype(BF)
        pre_u[:, cols] = (gg * spat[:, cols] * slope_u[:, cols]).astype(BF)

    low = out_unit + STEP
    for k in range(tiles):
        rows = slice(k * LANE, (k + 1) * LANE)
        gtmp[rows, :] = dot(gated[:, rows], cot, 0, 0).astype(BF)
    height = keep.shape[1] // 4
    for c, dst in ((0, keep), (1, send)):
        for e in range(4):
            for r in range(4):
                at = (lax.rem(own + r, 4) * 8 + (unit ^ (c + 2 * e))) * out_unit
                dst[e, r * height : r * height + out_unit, :] = gtmp[pl.ds(aligned(at, STEP), out_unit), :]
    gmix = dot(sg_ref[...], vn_ref[...], 1, 1).astype(BF)
    big = lax.broadcasted_iota(I32, (512, n), 0)
    lane = lax.broadcasted_iota(I32, (512, n), 1)
    within = ((big >> 6) ^ unit) * STEP + (big & 15)
    a = (((big >> 4) + own) & 3) * per + within
    pick = jnp.where((lane == a) & (within < per), 1.0, 0.0).astype(BF)
    padded = dot(pick, gmix).astype(BF)
    for c, dst in ((0, keep), (1, send)):
        for e in range(4):
            for r in range(4):
                at = (c + 2 * e) * 64 + r * STEP
                to = r * height + out_unit
                dst[e, to : to + STEP, :] = jnp.zeros((STEP, LANE), BF)
                dst[e, to : to + STEP, 0:n] = padded[at : at + STEP, :]
    for k in range(tiles):
        cols = slice(k * LANE, (k + 1) * LANE)
        part = dot(xt_ref[...], pre_u[:, cols]).astype(BF)
        for j, (c, y, x, r) in enumerate(ORDER):
            to = r * height + low + k * STEP
            (send if c else keep)[x + 2 * y, to : to + STEP, :] = part[j * STEP : (j + 1) * STEP, :]


def back_kernel(slot_ref, xt_ref, mix_ref, sg_ref, vhat_ref, rstd_ref, slope_v, g_two, pre_v, keep, send, rows_ref, vng, gain, shift):
    n, gate = vhat_ref.shape
    tiles = gate // LANE
    mix = mix_ref[...]
    for k in range(tiles):
        cols = slice(k * LANE, (k + 1) * LANE)
        vng[:, cols] = dot(mix, sg_ref[:, cols], 0, 0)
    gain[...] = jnp.zeros_like(gain)
    shift[...] = jnp.zeros_like(shift)

    @each_tile(n)
    def _(i):
        rows = rows_of(i)
        vg = jnp.where(slot_ref[rows, :] >= 0, vng[rows, :], 0.0)
        vhat = vhat_ref[rows, :]
        gain[...] += jnp.sum((vg * vhat).reshape(2, 8, gate), 0)
        shift[...] += jnp.sum(vg.reshape(2, 8, gate), 0)
        h = vg * g_two[...]
        v_grad = rstd_ref[rows, :] * (h - mean_rows(h) - vhat * mean_rows(h * vhat))
        pre_v[rows, :] = (v_grad * slope_v[rows, :]).astype(BF)

    height = keep.shape[1] // 4
    for k in range(tiles):
        cols = slice(k * LANE, (k + 1) * LANE)
        part = dot(xt_ref[...], pre_v[:, cols]).astype(BF)
        for j, (c, y, x, r) in enumerate(ORDER):
            to = r * height + k * STEP
            (send if c else keep)[x + 2 * y, to : to + STEP, :] = part[j * STEP : (j + 1) * STEP, :]
        rows_ref[k : k + 1, :] = jnp.sum(gain[:, cols], 0, keepdims=True)
        rows_ref[tiles + k : tiles + k + 1, :] = jnp.sum(shift[:, cols], 0, keepdims=True)


def token_kernel(slot_ref, slot_row, pos_ref, cot_ref, win, pre_u, pre_v, sg_ref, gated, wout, g_one, b_out, rows_ref, *rest):
    _, h0, h1, h2, h3, vec, xg, out_ref, in_ref, gain, shift = rest
    n, gate = pre_u.shape
    xg[...] = dot(pre_u[...], win[:, :gate], 1, 1) + dot(pre_v[...], win[:, gate:], 1, 1)
    gain[...] = jnp.zeros_like(gain)
    shift[...] = jnp.zeros_like(shift)
    width = xg.shape[1]

    @each_tile(n)
    def _(i):
        rows = rows_of(i)
        x = pos_ref[rows, :].astype(F32)
        cen = x - mean_rows(x)
        rstd = lax.rsqrt(mean_rows(cen * cen) + EPS)
        xhat = cen * rstd
        g = xg[rows, :]
        gain[...] += jnp.sum((g * xhat).reshape(2, 8, width), 0)
        shift[...] += jnp.sum(g.reshape(2, 8, width), 0)
        h = g * g_one[...]
        x_grad = rstd * (h - mean_rows(h) - xhat * mean_rows(h * xhat))
        total = cot_ref[rows, :].astype(F32) + x_grad
        in_ref[rows, :] = jnp.where(slot_ref[rows, :] >= 0, total, 0.0).astype(BF)

    branch = dot(gated[...], wout[...]) + b_out[...]
    out_ref[...] = jnp.where(slot_ref[...] >= 0, pos_ref[...].astype(F32) + branch, 0.0).astype(BF)
    for r, dst in enumerate((h0, h1, h2, h3)):
        spot = lax.broadcasted_iota(I32, (ROWS, n), 0) + r * ROWS
        pick = jnp.where(slot_row[...] == spot, 1.0, 0.0).astype(BF)
        dst[0:ROWS, :] = dot(pick, out_ref[...]).astype(BF)
        dst[HALF : HALF + ROWS, :] = dot(pick, in_ref[...]).astype(BF)

    ones = jnp.ones((8, n), BF)
    tiles = gate // LANE
    vec[0:1, :] = jnp.sum(gain[...], 0, keepdims=True)
    vec[1:2, :] = jnp.sum(shift[...], 0, keepdims=True)
    for k in range(tiles):
        cols = slice(k * LANE, (k + 1) * LANE)
        vec[2 + k : 3 + k, :] = dot(ones, pre_u[:, cols])[0:1]
        vec[2 + tiles + k : 3 + tiles + k, :] = dot(ones, pre_v[:, cols])[0:1]
    at = 2 + 2 * tiles
    vec[at : at + 2 * tiles, :] = rows_ref[...]
    at += 2 * tiles
    cells = 4 * ROWS
    lane = lax.broadcasted_iota(I32, (1, LANE), 1)
    last = pltpu.roll(dot(ones, cot_ref[...])[0:1], cells, 1)
    vec[at : at + 1, 0:n] = dot(jnp.ones((8, gate), BF), sg_ref[...], 1, 1)[0:1]
    vec[at : at + 1, :] = jnp.where(lane < cells, vec[at : at + 1, :], last)
    vec[at + 1 : at + 2, :] = jnp.where(lane < cells, last, 0.0)


def put_vec(ref, at, v):
    ref[at : at + STEP, :] = v.astype(BF)


def get_vec(ref, at):
    return ref[at : at + STEP, :].astype(F32)


def core_kernel(keep, got, own, s1, s2, s3):
    for e, dst in enumerate((own, s1, s2, s3)):
        dst[...] = (keep[e].astype(F32) + got[e].astype(F32)).astype(dst.dtype)


def core_vec_kernel(keep, got, vec, vec_got, tie, own, s1, s2, s3, vec_own):
    rows = own.shape[0]
    total = vec[...] + vec_got[...]
    put_vec(vec_own, 0, total)
    for e, dst in enumerate((own, s1, s2, s3)):
        dst[0:rows, :] = (keep[e].astype(F32) + got[e].astype(F32)).astype(dst.dtype)
        if e:
            put_vec(dst, rows, total)


def plane_kernel(own, g1, g2, g3, z0, z1, z2, z3):
    rows = z0.shape[0]
    for r, dst in enumerate((z0, z1, z2, z3)):
        at = slice(r * rows, (r + 1) * rows)
        total = (own[at, :] + g1[at, :].astype(F32)) + (g2[at, :].astype(F32) + g3[at, :].astype(F32))
        dst[...] = total.astype(dst.dtype)


def plane_vec_kernel(own, vec_own, g1, g2, g3, tie, z0, z1, z2, z3, vec_out):
    rows, at = z0.shape[0], own.shape[0]
    vec = (get_vec(vec_own, 0) + get_vec(g1, at)) + (get_vec(g2, at) + get_vec(g3, at))
    put_vec(vec_out, 0, vec)
    for r, dst in enumerate((z0, z1, z2, z3)):
        at = slice(r * rows, (r + 1) * rows)
        total = (own[at, :] + g1[at, :].astype(F32)) + (g2[at, :].astype(F32) + g3[at, :].astype(F32))
        dst[0:rows, :] = total.astype(dst.dtype)
        if r:
            put_vec(dst, rows, vec)


def patch_kernel(own, g1, g2, g3, out):
    rows = own.shape[0]
    total = own[...]
    for g in (g1, g2, g3):
        total = total + g[0:rows, :].astype(F32)
    out[...] = total.astype(out.dtype)


def patch_vec_kernel(scal, own, vec_own, g1, g2, g3, tie, tie_home, out, vec_out, held):
    patch_kernel(own, g1, g2, g3, out)
    rows = own.shape[0]
    me = scal[0]
    held[me] = get_vec(vec_own, 0)
    for r, g in enumerate((g1, g2, g3), 1):
        held[lax.rem(me + (4 - r), 4)] = get_vec(g, rows)
    vec_out[...] = (held[0] + held[1]) + (held[2] + held[3])


def home_kernel(scal, h0, h1, h2, h3, out_ref, grad_ref, held):
    for r, h in enumerate((h0, h1, h2, h3)):
        m = lax.rem(scal[0] + r, 4)
        held[m] = h[0:ROWS, :]
        grad_ref[m, :, 0, :] = h[HALF : HALF + ROWS, :].astype(F32)
    for m in range(4):
        out_ref[:, m, :] = held[m]


def update_kernel(rates, first, second, *rest):
    olds, rest = rest[:9], rest[9:]
    news, rest = rest[:9], rest[9:]
    made, sems = rest[:9], rest[9]
    copies = Copies(sems)
    out_unit = olds[3].shape[0] // 8
    low = out_unit + STEP

    def step(which, rows, cols, grads):
        old, new = olds[3 * which : 3 * which + 3], made[3 * which : 3 * which + 3]
        at = (slice(*rows), slice(*cols))
        fresh = nesterov(old[0][at], grads.astype(F32), old[1][at], old[2][at], rates[which])
        for ref, value in zip(new, fresh):
            ref[at] = value

    def send(which):
        for j in range(3 * which, 3 * which + 3):
            copies.bring(made[j], news[j])

    width = olds[3].shape[1]
    for u in range(8):
        step(1, (u * out_unit, (u + 1) * out_unit), (0, width), first[u, 0:out_unit, :])
    send(1)
    mix_rows, cells = olds[6].shape
    for u in range(-(-mix_rows // STEP)):
        rows = min(STEP, mix_rows - u * STEP)
        step(2, (u * STEP, u * STEP + rows), (0, cells), first[u, out_unit : out_unit + rows, 0:cells])
    send(2)
    tiles = olds[0].shape[1] // LANE
    for u in range(8):
        for k in range(tiles):
            if k < tiles // 2:
                grads = first[u, low + k * STEP : low + (k + 1) * STEP, :]
            else:
                j = k - tiles // 2
                grads = second[u, j * STEP : (j + 1) * STEP, :]
            step(0, (u * STEP, (u + 1) * STEP), (k * LANE, (k + 1) * LANE), grads)
    send(0)
    copies.wait()


VM = pl.BlockSpec(memory_space=pltpu.VMEM)
SM = pl.BlockSpec(memory_space=pltpu.SMEM)
ANY = pl.BlockSpec(memory_space=pl.ANY)


def call(body, ins, outs, scratch=(), specs=None, out_specs=None, flops=100_000_000, limit=16, name=None):
    moved = sum(math.prod(a.shape) * a.dtype.itemsize for a in ins)
    return pl.pallas_call(
        body,
        out_shape=[jax.ShapeDtypeStruct(s, d) for s, d in outs],
        in_specs=specs or [VM] * len(ins),
        out_specs=out_specs or [VM] * len(outs),
        scratch_shapes=list(scratch),
        compiler_params=pltpu.CompilerParams(vmem_limit_bytes=limit * 2**20),
        cost_estimate=pl.CostEstimate(flops=flops, bytes_accessed=moved, transcendentals=0),
        name=name,
    )(*ins)


def rest_of_img(total):
    mask = 8
    while mask < lax.axis_size("img"):
        total = total + swap(total, mask)
        mask *= 2
    return total


def img_gather(arr):
    size = lax.axis_size("img")
    groups = [[g * 8 + k for k in range(8)] for g in range(size // 8)]
    return lax.all_gather(arr, "img", axis_index_groups=groups)


def shards(
    tokens,
    cotangent,
    patch_count,
    crop_index,
    in_weight,
    in_moment,
    in_average,
    out_weight,
    out_moment,
    out_average,
    spatial_weight,
    spatial_moment,
    spatial_average,
    vectors,
    vector_moment,
    vector_average,
):
    p = lax.axis_index("patch")
    unit = lax.axis_index("img") % 8
    micro_count, slot_count, row_count, width = tokens.shape
    hidden = in_weight.shape[1]
    gate = hidden // 2
    mix_rows, cells = spatial_weight.shape
    assert micro_count == lax.axis_size("patch") == 4 and slot_count == 1
    assert width == LANE and in_weight.shape[0] == 128 and row_count == mix_rows == 81
    grid = math.isqrt(cells)
    n = -(-cells // STEP) * STEP
    in_unit = in_weight.shape[0] // 8
    out_unit = out_weight.shape[0] // 8
    low = out_unit + STEP
    side_rows = in_unit * gate // LANE
    scal = jnp.stack([p, unit]).astype(I32)

    def over_plane(base):
        near = swap(base, XBIT)
        return [base, near, swap(base, YBIT), swap(near, YBIT)]

    wi_piece = lax.dynamic_slice_in_dim(in_weight, unit * in_unit, in_unit, 0).astype(BF)

    msg, slot_col, slot_row = call(
        functools.partial(out_kernel, grid),
        [scal, patch_count.reshape(1, 4), crop_index, out_weight, spatial_weight],
        [((low, LANE), BF), ((n, 1), I32), ((1, n), I32)],
        [pltpu.VMEM((out_unit, width), F32), pltpu.VMEM((128, LANE), BF), pltpu.SemaphoreType.DMA((1,))],
        specs=[SM, VM, VM, ANY, VM],
        limit=8,
        name="prep_out",
    )
    (base_in,) = call(
        stack_tied_kernel,
        [turn(wi_piece, r) for r in (1, 2, 3)] + [msg],
        [((3, in_unit, hidden), BF)],
        specs=[VM] * 3 + [ANY],
        limit=8,
        name="stack_i",
    )
    plane_in = over_plane(base_in)
    wi = [arr for part in plane_in for arr in (part, swap(part, CORE))]
    (base,) = call(
        stack_tied_kernel,
        [turn(msg, r) for r in (1, 2, 3)] + [base_in],
        [((3, low, LANE), BF)],
        specs=[VM] * 3 + [ANY],
        limit=8,
        name="stack_o",
    )
    got = call(
        rows_kernel,
        [scal, tokens.reshape(4, row_count, width), cotangent.reshape(4, row_count, width), base],
        [((HALF + row_count, width), BF)] * 4,
        specs=[SM, VM, VM, ANY],
        limit=8,
        name="prep_rows",
    )
    got = [got[0]] + [turn(m, r) for r, m in enumerate(got[1:], 1)]
    (held,) = call(hold_kernel, [base, plane_in[2]], [((3, low, LANE), BF)], specs=[VM, ANY], limit=8, name="hold_out")
    planes = [[8 * g + c + 2 * k for k in range(4)] for g in range(lax.axis_size("img") // 8) for c in (0, 1)]
    joined = lax.all_gather(held, "img", axis_index_groups=planes)
    joined_got = swap(joined, CORE)

    bounds = [width, width, hidden, gate, gate, cells, width]
    pieces = []
    offset = 0
    for length in bounds:
        pieces.append(vectors[None, offset : offset + length])
        offset += length
    g_one, s_one, b_in, g_two, s_two, b_mix, b_out = pieces
    b_mix = jnp.pad(b_mix[0], (0, n - cells))[:, None]

    pos, xn = call(
        norm_kernel,
        [slot_col, *got, g_one, s_one],
        [((n, width), BF), ((n, width), BF)],
        name="norm_in",
    )
    sized = lambda kind: ((n, gate), kind)
    win, vhat, rstd, slope_v, vn = call(
        right_kernel,
        [scal, slot_col, xn, b_in, g_two, s_two, in_weight, *wi],
        [((width, hidden), BF), sized(F32), ((n, 1), F32), sized(F32), sized(BF)],
        [pltpu.VMEM((n, gate), F32)],
        specs=[SM] + [VM] * 14,
        flops=1_500_000_000,
        limit=20,
        name="right",
    )
    cot_pos, xt = call(
        side_kernel,
        [scal, slot_col, *got, xn, vn],
        [((n, width), BF), ((width, n), BF)],
        [pltpu.VMEM((width, n), BF)],
        specs=[SM] + [VM] * 6 + [ANY],
        name="place_cot",
    )
    u, slope_u = call(
        left_kernel,
        [xn, b_in, win, joined_got],
        [sized(F32), sized(F32)],
        [pltpu.VMEM((n, gate), F32)],
        specs=[VM] * 3 + [ANY],
        flops=1_000_000_000,
        limit=16,
        name="left",
    )
    packed = ((4, 4 * (low + side_rows), LANE), BF)
    mix, pre_u, sg, gated, wout, keep_a, send_a = call(
        spatial_kernel,
        [scal, xt, cot_pos, u, slope_u, vn, b_mix, spatial_weight, out_weight, joined, joined_got],
        [((n, n), BF), sized(BF), sized(BF), sized(BF), ((gate, width), BF), packed, packed],
        [
            pltpu.VMEM((512, LANE), BF),
            pltpu.VMEM((n, gate), F32),
            pltpu.VMEM((gate, width), BF),
        ],
        specs=[SM] + [VM] * 10,
        flops=4_000_000_000,
        limit=24,
        name="spatial",
    )
    core_a = swap(send_a, CORE)
    half = ((4, 4 * side_rows, LANE), BF)
    pre_v, keep_b, send_b, rows_b = call(
        back_kernel,
        [slot_col, xt, mix, sg, vhat, rstd, slope_v, g_two],
        [sized(BF), half, half, ((6, LANE), F32)],
        [pltpu.VMEM((n, gate), F32), pltpu.VMEM((8, gate), F32), pltpu.VMEM((8, gate), F32)],
        flops=2_000_000_000,
        limit=20,
        name="back",
    )
    core_b = swap(send_b, CORE)
    rows_a, rows_b4 = 4 * (low + side_rows), 4 * side_rows
    own_a, *send_a = call(
        core_kernel, [keep_a, core_a], [((rows_a, LANE), F32)] + [((rows_a, LANE), BF)] * 3, limit=12, name="core_a"
    )
    plane_a = [swap(s, m) for s, m in zip(send_a, (2, 4, 6))]
    *home, vec = call(
        token_kernel,
        [slot_col, slot_row, pos, cot_pos, win, pre_u, pre_v, sg, gated, wout, g_one, b_out, rows_b, send_a[2]],
        [((HALF + row_count, width), BF)] * 4 + [((STEP, LANE), F32)],
        [
            pltpu.VMEM((n, width), F32),
            pltpu.VMEM((n, width), BF),
            pltpu.VMEM((n, width), BF),
            pltpu.VMEM((8, width), F32),
            pltpu.VMEM((8, width), F32),
        ],
        specs=[VM] * 13 + [ANY],
        flops=2_000_000_000,
        limit=20,
        name="token_grad",
    )
    vec_got = swap(vec, CORE)
    own_b, *send_b, vec_own = call(
        core_vec_kernel,
        [keep_b, core_b, vec, vec_got, send_a[0]],
        [((rows_b4, LANE), F32)] + [((rows_b4 + STEP, LANE), BF)] * 3 + [((STEP, LANE), BF)],
        specs=[VM] * 4 + [ANY],
        name="core_b",
    )
    plane_b = [swap(s, m) for s, m in zip(send_b, (2, 4, 6))]
    home = [home[0]] + [turn(h, -r) for r, h in enumerate(home[1:], 1)]
    out_tokens, in_grad = call(
        home_kernel,
        [scal, *home],
        [((row_count, 4, width), BF), ((4, row_count, 1, width), F32)],
        [pltpu.VMEM((4, row_count, width), BF)],
        specs=[SM] + [VM] * 4,
        limit=8,
        name="home",
    )
    z_rows = low + side_rows
    own_a, *patch_a = call(
        plane_kernel, [own_a, *plane_a], [((z_rows, LANE), F32)] + [((z_rows, LANE), BF)] * 3, name="plane_a"
    )
    got_a = [turn(z, r) for r, z in enumerate(patch_a, 1)]
    own_b, *patch_b, vec_own = call(
        plane_vec_kernel,
        [own_b, vec_own, *plane_b, patch_a[0]],
        [((side_rows, LANE), F32)] + [((side_rows + STEP, LANE), BF)] * 3 + [((STEP, LANE), BF)],
        specs=[VM] * 5 + [ANY],
        name="plane_b",
    )
    got_b = [turn(z, r) for r, z in enumerate(patch_b, 1)]
    kind = BF if lax.axis_size("img") == 8 else F32
    (first,) = call(patch_kernel, [own_a, *got_a], [((z_rows, LANE), kind)], name="patch_a")
    first = img_gather(rest_of_img(first).astype(BF))
    second, vec_sum = call(
        patch_vec_kernel,
        [scal, own_b, vec_own, *got_b, first, in_grad],
        [((side_rows, LANE), kind), ((STEP, LANE), F32)],
        [pltpu.VMEM((4, STEP, LANE), F32)],
        specs=[SM] + [VM] * 5 + [ANY] * 2,
        name="patch_b",
    )
    second = img_gather(rest_of_img(second).astype(BF))
    vec_sum = rest_of_img(vec_sum).reshape(STEP * LANE)

    vec_sum = vec_sum[: vectors.shape[0]]

    images = micro_count * slot_count * lax.axis_size("img")
    rate_in, rate_out, rate_mix, rate_vec = step_rates(images, width, gate, cells)
    olds = [in_weight, in_moment, in_average, out_weight, out_moment, out_average]
    olds += [spatial_weight, spatial_moment, spatial_average]
    news = call(
        functools.partial(update_kernel, (rate_in, rate_out, rate_mix)),
        [first, second, *olds],
        [(a.shape, F32) for a in olds],
        [pltpu.VMEM(a.shape, F32) for a in olds] + [pltpu.SemaphoreType.DMA((9,))],
        specs=[VM] * 11,
        out_specs=[ANY] * 9,
        limit=20,
        name="update",
    )
    vec_new = nesterov(vectors, vec_sum, vector_moment, vector_average, rate_vec)
    return (out_tokens.transpose(1, 0, 2).reshape(tokens.shape), in_grad.transpose(0, 2, 1, 3), *news, *vec_new)


def solution(mesh):
    rows = P("patch", None)
    act = P(None, "img", "patch", None)
    return jax.shard_map(
        shards,
        mesh=mesh,
        in_specs=(act, act, P(None, "img"), P(None, "img", None), *([rows] * 9), P(), P(), P()),
        out_specs=(act, act, *([rows] * 9), P(), P(), P()),
        check_vma=False,
    )
```

```python
import functools
import math

import jax
import jax.numpy as jnp
from jax import lax
from jax.experimental import pallas as pl
from jax.experimental.pallas import tpu as pltpu
from jax.sharding import PartitionSpec as P

EPS = 1e-05
MOMENTUM = 0.9
AVG_DECAY = 0.8
BF = jnp.bfloat16
F32 = jnp.float32
I32 = jnp.int32
CORE, XBIT, YBIT = 1, 2, 4
LANE = 512
STEP = 16
ROWS = 81
HALF = 96


def step_rates(images, model_width, gate_width, cell_count):
    live_rows = 207.0 * images
    rate_in = 1.0 / (math.sqrt(model_width) * 1.4 * math.sqrt(live_rows))
    rate_out = 1.0 / (math.sqrt(gate_width / 4.0) * 1.2 * math.sqrt(live_rows))
    rate_mix = 1.0 / (math.sqrt(cell_count) * 1.5 * math.sqrt(gate_width * images / 2.0))
    rate_vec = 0.1 / (2.0 * math.sqrt(live_rows))
    return (rate_in, rate_out, rate_mix, rate_vec)


def nesterov(weight, grads, moment, average, rate):
    moment_new = MOMENTUM * moment + grads
    weight_new = weight - rate * (grads + MOMENTUM * moment_new)
    average_new = AVG_DECAY * average + (1.0 - AVG_DECAY) * weight_new
    return (weight_new, moment_new, average_new)


def turn(arr, r):
    n = lax.axis_size("patch")
    return lax.ppermute(arr, "patch", [(s, (s + r) % n) for s in range(n)])


def swap(arr, mask):
    n = lax.axis_size("img")
    return lax.ppermute(arr, "img", [(k, k ^ mask) for k in range(n)])


def dot(a, b, ca=1, cb=0):
    return lax.dot_general(a, b, (((ca,), (cb,)), ((), ())), preferred_element_type=F32)


def aligned(v, by):
    return pl.multiple_of(v, by)


def rows_of(i):
    return pl.ds(aligned(i * STEP, STEP), STEP)


def each_tile(n):
    steps = n // STEP
    return pl.loop(0, steps, unroll=7 if steps % 7 == 0 else 1)


def gelu_parts(pre):
    phi = 0.5 * (1.0 + lax.erf(pre * math.sqrt(0.5)))
    slope = phi + pre * (jnp.exp(-0.5 * pre * pre) * (1.0 / math.sqrt(2.0 * math.pi)))
    return pre * phi, slope


def mean_rows(v):
    return jnp.sum(v, axis=-1, keepdims=True) * (1.0 / v.shape[-1])


def slot_kernel(grid, scal, counts, crops, col_ref, row_ref):
    own = scal[0]
    lane = lax.broadcasted_iota(I32, counts.shape, 1)
    count = jnp.sum(jnp.where(lane == own, counts[...], 0), axis=1, keepdims=True)
    start = crops[own][:, 0:1]
    cells = grid * grid
    side = jnp.zeros_like(count)
    top = jnp.zeros_like(count)
    for k in range(1, grid + 1):
        side = jnp.where(count == k * k, k, side)
        top = top + jnp.where(start >= k * grid, 1, 0)
    quarter = count >> 2
    left = start - top * grid
    for ref, dim in ((col_ref, 0), (row_ref, 1)):
        place = lax.broadcasted_iota(I32, ref.shape, dim)
        row = jnp.zeros(ref.shape, I32)
        for k in range(1, grid):
            row = row + jnp.where(place >= k * grid, 1, 0)
        drow = row - top
        dcol = place - row * grid - left
        inside = (drow >= 0) & (drow < side) & (dcol >= 0) & (dcol < side) & (place < cells)
        order = drow * side + dcol
        block = jnp.zeros(ref.shape, I32)
        for k in (1, 2, 3):
            block = block + jnp.where(order >= k * quarter, 1, 0)
        slot = ((own - block) & 3) * ROWS + order - block * quarter
        ref[...] = jnp.where(inside, slot, -1)


def onehot(slot, lanes, base):
    lane = lax.broadcasted_iota(I32, (slot.shape[0], lanes), 1) + base
    return jnp.where(slot == lane, 1.0, 0.0).astype(BF)


def side_kernel(scal, slot_ref, m0, m1, m2, m3, xn_ref, tie, pos_ref, xt_ref, turned):
    place_kernel(slot_ref, m0, m1, m2, m3, pos_ref)
    own, unit = scal[0], scal[1]
    turned[...] = xn_ref[...].T
    for k, (c, y, x, r) in enumerate(ORDER):
        who = lax.rem(own + r, 4)
        e = c + 2 * x + 4 * y
        src = who * 128 + (unit ^ e) * STEP
        xt_ref[k * STEP : (k + 1) * STEP, :] = turned[pl.ds(aligned(src, STEP), STEP), :]


class Copies:
    def __init__(self, sems):
        self.sems, self.all = sems, []

    def bring(self, src, dst):
        copy = pltpu.make_async_copy(src, dst, self.sems.at[len(self.all)])
        copy.start()
        self.all.append(copy)

    def wait(self):
        for copy in self.all:
            copy.wait()


def pick_kernel(per, own, unit, pick_ref, pack_ref):
    n = pick_ref.shape[0]
    cell = lax.broadcasted_iota(I32, (n, pick_ref.shape[1]), 0)
    lane = lax.broadcasted_iota(I32, (n, pick_ref.shape[1]), 1)
    part = jnp.where(cell >= per, 1, 0) + jnp.where(cell >= 2 * per, 1, 0) + jnp.where(cell >= 3 * per, 1, 0)
    pick_ref[...] = jnp.where(lane == cell + part * (128 - per), 1.0, 0.0).astype(BF)
    big = lax.broadcasted_iota(I32, (512, n), 0)
    lane = lax.broadcasted_iota(I32, (512, n), 1)
    within = ((big >> 6) ^ unit) * STEP + (big & 15)
    a = (((big >> 4) + own) & 3) * per + within
    pack_ref[...] = jnp.where((lane == a) & (within < per), 1.0, 0.0).astype(BF)


def out_kernel(grid, scal, counts, crops, w_out, mix, msg, col_ref, row_ref, pick_ref, pack_ref, held, strip, sems):
    unit = scal[1]
    rows = held.shape[0]
    copies = Copies(sems)
    copies.bring(w_out.at[pl.ds(aligned(unit * rows, STEP), rows), :], held)
    slot_kernel(grid, scal, counts, crops, col_ref, row_ref)
    pick_kernel(mix.shape[0], scal[0], unit, pick_ref, pack_ref)
    strip[...] = jnp.zeros_like(strip)
    strip[0 : mix.shape[0], 0 : mix.shape[1]] = mix[...].astype(BF)
    copies.wait()
    msg[0:rows, :] = held[...].astype(BF)
    msg[rows:, :] = strip[pl.ds(aligned(unit * STEP, STEP), STEP), :]


def rows_kernel(scal, tok, cot, tie, m0, m1, m2, m3):
    for r, msg in enumerate((m0, m1, m2, m3)):
        to = lax.rem(scal[0] + r, 4)
        msg[0:ROWS, :] = tok[to]
        msg[HALF : HALF + ROWS, :] = cot[to]


def hold_kernel(src, tie, dst):
    dst[...] = src[...]


def stack_tied_kernel(m1, m2, m3, tie, out):
    stack_kernel(m1, m2, m3, out)


def join_kernel(p0, p1, p2, p3, out):
    for e, part in enumerate((p0, p1, p2, p3)):
        out[e] = part[...]


def join_tied_kernel(p0, p1, p2, p3, tie, out):
    join_kernel(p0, p1, p2, p3, out)


def stack_kernel(m1, m2, m3, out):
    for r, msg in enumerate((m1, m2, m3)):
        out[r] = msg[0 : out.shape[1], :]


def place(slot_ref, blocks, at, pos_ref):
    slot = slot_ref[...]
    total = None
    for r, msg in enumerate(blocks):
        part = dot(onehot(slot, ROWS, r * ROWS), msg[at : at + ROWS, :])
        total = part if total is None else total + part
    pos_ref[...] = total.astype(BF)


def place_kernel(slot_ref, m0, m1, m2, m3, pos_ref):
    place(slot_ref, (m0, m1, m2, m3), HALF, pos_ref)


ORDER = [(c, y, x, r) for c in (0, 1) for y in (0, 1) for x in (0, 1) for r in range(4)]


def norm_kernel(slot_ref, m0, m1, m2, m3, gain, shift, pos_ref, xn_ref):
    place(slot_ref, (m0, m1, m2, m3), 0, pos_ref)
    @each_tile(pos_ref.shape[0])
    def _(i):
        x = pos_ref[rows_of(i), :].astype(F32)
        cen = x - mean_rows(x)
        rstd = lax.rsqrt(mean_rows(cen * cen) + EPS)
        xn_ref[rows_of(i), :] = (cen * rstd * gain[...] + shift[...]).astype(BF)


def right_kernel(scal, slot_ref, xn_ref, b_in, g_two, s_two, wi_own, *rest):
    wi, rest = rest[:8], rest[8:]
    win, vhat_ref, rstd_ref, slope_v, vn_ref, pre = rest
    own, unit = scal[0], scal[1]
    n, gate = vhat_ref.shape
    tiles = gate // LANE
    win[pl.ds(aligned(own * 128, 128), 128), :] = wi_own[...].astype(BF)
    for e in range(8):
        for r in (1, 2, 3):
            who = lax.rem(own + (4 - r), 4)
            at = who * 128 + (unit ^ e) * STEP
            win[pl.ds(aligned(at, STEP), STEP), :] = wi[e][r - 1]

    xn = xn_ref[...]
    for k in range(tiles):
        cols = slice(k * LANE, (k + 1) * LANE)
        wide = slice(gate + k * LANE, gate + (k + 1) * LANE)
        pre[:, cols] = dot(xn, win[:, wide]) + b_in[:, wide]

    @each_tile(n)
    def _(i):
        rows = rows_of(i)
        v, slope = gelu_parts(pre[rows, :])
        slope_v[rows, :] = slope
        cen = v - mean_rows(v)
        rstd = lax.rsqrt(mean_rows(cen * cen) + EPS)
        vhat = cen * rstd
        vhat_ref[rows, :] = vhat
        rstd_ref[rows, :] = rstd
        vn = jnp.where(slot_ref[rows, :] >= 0, vhat * g_two[...] + s_two[...], 0.0)
        vn_ref[rows, :] = vn.astype(BF)


def left_kernel(xn_ref, b_in, win, *rest):
    u_ref, slope_u, pre = rest[-3:]
    n, gate = u_ref.shape
    xn = xn_ref[...]
    for k in range(gate // LANE):
        cols = slice(k * LANE, (k + 1) * LANE)
        pre[:, cols] = dot(xn, win[:, cols]) + b_in[:, cols]

    @each_tile(n)
    def _(i):
        rows = rows_of(i)
        u, slope = gelu_parts(pre[rows, :])
        u_ref[rows, :] = u
        slope_u[rows, :] = slope


def spatial_kernel(scal, pick_ref, pack_ref, xt_ref, cot_ref, u_ref, slope_u, vn_ref, b_mix, mix_own, wo_own, *rest):
    wo, rest = rest[:2], rest[2:]
    mix_ref, pre_u, sg_ref, gated, wout, keep, send, *rest = rest
    mixp, spat, gtmp = rest
    own, unit = scal[0], scal[1]
    n, gate = u_ref.shape
    tiles = gate // LANE
    out_unit = wout.shape[0] // 32
    wout[pl.ds(aligned(own * 8 * out_unit, STEP), 8 * out_unit), :] = wo_own[...].astype(BF)
    for k in range(4):
        for c in (0, 1):
            piece = 2 * k + ((unit & 1) ^ c)
            for r in (1, 2, 3):
                who = lax.rem(own + (4 - r), 4)
                at = (who * 8 + piece) * out_unit
                wout[pl.ds(aligned(at, STEP), out_unit), :] = wo[c][k, r - 1, 0:out_unit, :]
                at = who * 128 + piece * STEP
                mixp[pl.ds(aligned(at, STEP), STEP), :] = wo[c][k, r - 1, out_unit:, :]
    per, cells = mix_own.shape
    mine = aligned(own * 128, 128)
    mixp[pl.ds(mine, 128), :] = jnp.zeros((128, LANE), BF)
    mixp[pl.ds(mine, per), 0:cells] = mix_own[...].astype(BF)
    mix_ref[...] = dot(pick_ref[...], mixp[:, :n]).astype(BF)
    mix = mix_ref[...]
    for k in range(tiles):
        cols = slice(k * LANE, (k + 1) * LANE)
        sp = dot(mix, vn_ref[:, cols]) + b_mix[...]
        spat[:, cols] = sp
        gated[:, cols] = (u_ref[:, cols] * sp).astype(BF)

    cot = cot_ref[...]
    for k in range(tiles):
        cols = slice(k * LANE, (k + 1) * LANE)
        gg = dot(cot, wout[cols, :], 1, 1)
        sg_ref[:, cols] = (gg * u_ref[:, cols]).astype(BF)
        pre_u[:, cols] = (gg * spat[:, cols] * slope_u[:, cols]).astype(BF)

    low = out_unit + STEP
    for k in range(tiles):
        rows = slice(k * LANE, (k + 1) * LANE)
        gtmp[rows, :] = dot(gated[:, rows], cot, 0, 0).astype(BF)
    height = keep.shape[1] // 4
    for c, dst in ((0, keep), (1, send)):
        for e in range(4):
            for r in range(4):
                at = (lax.rem(own + r, 4) * 8 + (unit ^ (c + 2 * e))) * out_unit
                dst[e, r * height : r * height + out_unit, :] = gtmp[pl.ds(aligned(at, STEP), out_unit), :]
    gmix = dot(sg_ref[...], vn_ref[...], 1, 1).astype(BF)
    padded = dot(pack_ref[...], gmix).astype(BF)
    for c, dst in ((0, keep), (1, send)):
        for e in range(4):
            for r in range(4):
                at = (c + 2 * e) * 64 + r * STEP
                to = r * height + out_unit
                dst[e, to : to + STEP, :] = jnp.zeros((STEP, LANE), BF)
                dst[e, to : to + STEP, 0:n] = padded[at : at + STEP, :]
    for k in range(tiles):
        cols = slice(k * LANE, (k + 1) * LANE)
        part = dot(xt_ref[...], pre_u[:, cols]).astype(BF)
        for j, (c, y, x, r) in enumerate(ORDER):
            to = r * height + low + k * STEP
            (send if c else keep)[x + 2 * y, to : to + STEP, :] = part[j * STEP : (j + 1) * STEP, :]


def back_kernel(slot_ref, xt_ref, mix_ref, sg_ref, vhat_ref, rstd_ref, slope_v, g_two, pre_v, keep, send, rows_ref, vng, gain, shift):
    n, gate = vhat_ref.shape
    tiles = gate // LANE
    mix = mix_ref[...]
    for k in range(tiles):
        cols = slice(k * LANE, (k + 1) * LANE)
        vng[:, cols] = dot(mix, sg_ref[:, cols], 0, 0)
    gain[...] = jnp.zeros_like(gain)
    shift[...] = jnp.zeros_like(shift)

    @each_tile(n)
    def _(i):
        rows = rows_of(i)
        vg = jnp.where(slot_ref[rows, :] >= 0, vng[rows, :], 0.0)
        vhat = vhat_ref[rows, :]
        gain[...] += jnp.sum((vg * vhat).reshape(2, 8, gate), 0)
        shift[...] += jnp.sum(vg.reshape(2, 8, gate), 0)
        h = vg * g_two[...]
        v_grad = rstd_ref[rows, :] * (h - mean_rows(h) - vhat * mean_rows(h * vhat))
        pre_v[rows, :] = (v_grad * slope_v[rows, :]).astype(BF)

    height = keep.shape[1] // 4
    for k in range(tiles):
        cols = slice(k * LANE, (k + 1) * LANE)
        part = dot(xt_ref[...], pre_v[:, cols]).astype(BF)
        for j, (c, y, x, r) in enumerate(ORDER):
            to = r * height + k * STEP
            (send if c else keep)[x + 2 * y, to : to + STEP, :] = part[j * STEP : (j + 1) * STEP, :]
        rows_ref[k : k + 1, :] = jnp.sum(gain[:, cols], 0, keepdims=True)
        rows_ref[tiles + k : tiles + k + 1, :] = jnp.sum(shift[:, cols], 0, keepdims=True)


def token_kernel(slot_ref, slot_row, pos_ref, cot_ref, win, pre_u, pre_v, sg_ref, gated, wout, g_one, b_out, rows_ref, *rest):
    _, h0, h1, h2, h3, vec, xg, out_ref, in_ref, gain, shift = rest
    n, gate = pre_u.shape
    xg[...] = dot(pre_u[...], win[:, :gate], 1, 1) + dot(pre_v[...], win[:, gate:], 1, 1)
    gain[...] = jnp.zeros_like(gain)
    shift[...] = jnp.zeros_like(shift)
    width = xg.shape[1]

    @each_tile(n)
    def _(i):
        rows = rows_of(i)
        x = pos_ref[rows, :].astype(F32)
        cen = x - mean_rows(x)
        rstd = lax.rsqrt(mean_rows(cen * cen) + EPS)
        xhat = cen * rstd
        g = xg[rows, :]
        gain[...] += jnp.sum((g * xhat).reshape(2, 8, width), 0)
        shift[...] += jnp.sum(g.reshape(2, 8, width), 0)
        h = g * g_one[...]
        x_grad = rstd * (h - mean_rows(h) - xhat * mean_rows(h * xhat))
        total = cot_ref[rows, :].astype(F32) + x_grad
        in_ref[rows, :] = jnp.where(slot_ref[rows, :] >= 0, total, 0.0).astype(BF)

    branch = dot(gated[...], wout[...]) + b_out[...]
    out_ref[...] = jnp.where(slot_ref[...] >= 0, pos_ref[...].astype(F32) + branch, 0.0).astype(BF)
    for r, dst in enumerate((h0, h1, h2, h3)):
        spot = lax.broadcasted_iota(I32, (ROWS, n), 0) + r * ROWS
        pick = jnp.where(slot_row[...] == spot, 1.0, 0.0).astype(BF)
        dst[0:ROWS, :] = dot(pick, out_ref[...]).astype(BF)
        dst[HALF : HALF + ROWS, :] = dot(pick, in_ref[...]).astype(BF)

    ones = jnp.ones((8, n), BF)
    tiles = gate // LANE
    vec[0:1, :] = jnp.sum(gain[...], 0, keepdims=True)
    vec[1:2, :] = jnp.sum(shift[...], 0, keepdims=True)
    for k in range(tiles):
        cols = slice(k * LANE, (k + 1) * LANE)
        vec[2 + k : 3 + k, :] = dot(ones, pre_u[:, cols])[0:1]
        vec[2 + tiles + k : 3 + tiles + k, :] = dot(ones, pre_v[:, cols])[0:1]
    at = 2 + 2 * tiles
    vec[at : at + 2 * tiles, :] = rows_ref[...]
    at += 2 * tiles
    cells = 4 * ROWS
    lane = lax.broadcasted_iota(I32, (1, LANE), 1)
    last = pltpu.roll(dot(ones, cot_ref[...])[0:1], cells, 1)
    vec[at : at + 1, 0:n] = dot(jnp.ones((8, gate), BF), sg_ref[...], 1, 1)[0:1]
    vec[at : at + 1, :] = jnp.where(lane < cells, vec[at : at + 1, :], last)
    vec[at + 1 : at + 2, :] = jnp.where(lane < cells, last, 0.0)


def put_vec(ref, at, v):
    ref[at : at + STEP, :] = v.astype(BF)


def get_vec(ref, at):
    return ref[at : at + STEP, :].astype(F32)


def core_kernel(keep, got, own, s1, s2, s3):
    for e, dst in enumerate((own, s1, s2, s3)):
        dst[...] = (keep[e].astype(F32) + got[e].astype(F32)).astype(dst.dtype)


def core_vec_kernel(keep, got, vec, vec_got, tie, own, s1, s2, s3, vec_own):
    rows = own.shape[0]
    total = vec[...] + vec_got[...]
    put_vec(vec_own, 0, total)
    for e, dst in enumerate((own, s1, s2, s3)):
        dst[0:rows, :] = (keep[e].astype(F32) + got[e].astype(F32)).astype(dst.dtype)
        if e:
            put_vec(dst, rows, total)


def plane_kernel(own, g1, g2, g3, z0, z1, z2, z3):
    rows = z0.shape[0]
    for r, dst in enumerate((z0, z1, z2, z3)):
        at = slice(r * rows, (r + 1) * rows)
        total = (own[at, :] + g1[at, :].astype(F32)) + (g2[at, :].astype(F32) + g3[at, :].astype(F32))
        dst[...] = total.astype(dst.dtype)


def plane_vec_kernel(own, vec_own, g1, g2, g3, tie, z0, z1, z2, z3, vec_out):
    rows, at = z0.shape[0], own.shape[0]
    vec = (get_vec(vec_own, 0) + get_vec(g1, at)) + (get_vec(g2, at) + get_vec(g3, at))
    put_vec(vec_out, 0, vec)
    for r, dst in enumerate((z0, z1, z2, z3)):
        at = slice(r * rows, (r + 1) * rows)
        total = (own[at, :] + g1[at, :].astype(F32)) + (g2[at, :].astype(F32) + g3[at, :].astype(F32))
        dst[0:rows, :] = total.astype(dst.dtype)
        if r:
            put_vec(dst, rows, vec)


def patch_kernel(own, g1, g2, g3, out):
    rows = own.shape[0]
    total = own[...]
    for g in (g1, g2, g3):
        total = total + g[0:rows, :].astype(F32)
    out[...] = total.astype(out.dtype)


def patch_vec_kernel(scal, own, vec_own, g1, g2, g3, tie, tie_home, out, vec_out, held):
    patch_kernel(own, g1, g2, g3, out)
    rows = own.shape[0]
    me = scal[0]
    held[me] = get_vec(vec_own, 0)
    for r, g in enumerate((g1, g2, g3), 1):
        held[lax.rem(me + (4 - r), 4)] = get_vec(g, rows)
    vec_out[...] = (held[0] + held[1]) + (held[2] + held[3])


def home_kernel(scal, h0, h1, h2, h3, out_ref, grad_ref, held):
    for r, h in enumerate((h0, h1, h2, h3)):
        m = lax.rem(scal[0] + r, 4)
        held[m] = h[0:ROWS, :]
        grad_ref[m, :, 0, :] = h[HALF : HALF + ROWS, :].astype(F32)
    for m in range(4):
        out_ref[:, m, :] = held[m]


def update_kernel(rates, first, second, *rest):
    olds, rest = rest[:9], rest[9:]
    news, rest = rest[:9], rest[9:]
    made, sems = rest[:9], rest[9]
    copies = Copies(sems)
    out_unit = olds[3].shape[0] // 8
    low = out_unit + STEP

    def step(which, rows, cols, grads):
        old, new = olds[3 * which : 3 * which + 3], made[3 * which : 3 * which + 3]
        at = (slice(*rows), slice(*cols))
        fresh = nesterov(old[0][at], grads.astype(F32), old[1][at], old[2][at], rates[which])
        for ref, value in zip(new, fresh):
            ref[at] = value

    def send(which):
        for j in range(3 * which, 3 * which + 3):
            copies.bring(made[j], news[j])

    width = olds[3].shape[1]
    for u in range(8):
        step(1, (u * out_unit, (u + 1) * out_unit), (0, width), first[u, 0:out_unit, :])
    send(1)
    mix_rows, cells = olds[6].shape
    for u in range(-(-mix_rows // STEP)):
        rows = min(STEP, mix_rows - u * STEP)
        step(2, (u * STEP, u * STEP + rows), (0, cells), first[u, out_unit : out_unit + rows, 0:cells])
    send(2)
    tiles = olds[0].shape[1] // LANE
    for u in range(8):
        for k in range(tiles):
            if k < tiles // 2:
                grads = first[u, low + k * STEP : low + (k + 1) * STEP, :]
            else:
                j = k - tiles // 2
                grads = second[u, j * STEP : (j + 1) * STEP, :]
            step(0, (u * STEP, (u + 1) * STEP), (k * LANE, (k + 1) * LANE), grads)
    send(0)
    copies.wait()


VM = pl.BlockSpec(memory_space=pltpu.VMEM)
SM = pl.BlockSpec(memory_space=pltpu.SMEM)
ANY = pl.BlockSpec(memory_space=pl.ANY)


def call(body, ins, outs, scratch=(), specs=None, out_specs=None, flops=100_000_000, limit=16, name=None):
    moved = sum(math.prod(a.shape) * a.dtype.itemsize for a in ins)
    return pl.pallas_call(
        body,
        out_shape=[jax.ShapeDtypeStruct(s, d) for s, d in outs],
        in_specs=specs or [VM] * len(ins),
        out_specs=out_specs or [VM] * len(outs),
        scratch_shapes=list(scratch),
        compiler_params=pltpu.CompilerParams(vmem_limit_bytes=limit * 2**20),
        cost_estimate=pl.CostEstimate(flops=flops, bytes_accessed=moved, transcendentals=0),
        name=name,
    )(*ins)


def rest_of_img(total):
    mask = 8
    while mask < lax.axis_size("img"):
        total = total + swap(total, mask)
        mask *= 2
    return total


def img_gather(arr):
    size = lax.axis_size("img")
    groups = [[g * 8 + k for k in range(8)] for g in range(size // 8)]
    return lax.all_gather(arr, "img", axis_index_groups=groups)


def shards(
    tokens,
    cotangent,
    patch_count,
    crop_index,
    in_weight,
    in_moment,
    in_average,
    out_weight,
    out_moment,
    out_average,
    spatial_weight,
    spatial_moment,
    spatial_average,
    vectors,
    vector_moment,
    vector_average,
):
    p = lax.axis_index("patch")
    unit = lax.axis_index("img") % 8
    micro_count, slot_count, row_count, width = tokens.shape
    hidden = in_weight.shape[1]
    gate = hidden // 2
    mix_rows, cells = spatial_weight.shape
    assert micro_count == lax.axis_size("patch") == 4 and slot_count == 1
    assert width == LANE and in_weight.shape[0] == 128 and row_count == mix_rows == 81
    grid = math.isqrt(cells)
    n = -(-cells // STEP) * STEP
    in_unit = in_weight.shape[0] // 8
    out_unit = out_weight.shape[0] // 8
    low = out_unit + STEP
    side_rows = in_unit * gate // LANE
    scal = jnp.stack([p, unit]).astype(I32)

    def over_plane(base):
        near = swap(base, XBIT)
        return [base, near, swap(base, YBIT), swap(near, YBIT)]

    wi_piece = lax.dynamic_slice_in_dim(in_weight, unit * in_unit, in_unit, 0).astype(BF)

    msg, slot_col, slot_row, pick, pack = call(
        functools.partial(out_kernel, grid),
        [scal, patch_count.reshape(1, 4), crop_index, out_weight, spatial_weight],
        [((low, LANE), BF), ((n, 1), I32), ((1, n), I32), ((n, 512), BF), ((512, n), BF)],
        [pltpu.VMEM((out_unit, width), F32), pltpu.VMEM((128, LANE), BF), pltpu.SemaphoreType.DMA((1,))],
        specs=[SM, VM, VM, ANY, VM],
        limit=8,
        name="prep_out",
    )
    (base_in,) = call(
        stack_tied_kernel,
        [turn(wi_piece, r) for r in (1, 2, 3)] + [msg],
        [((3, in_unit, hidden), BF)],
        specs=[VM] * 3 + [ANY],
        limit=8,
        name="stack_i",
    )
    plane_in = over_plane(base_in)
    wi = [arr for part in plane_in for arr in (part, swap(part, CORE))]
    (base,) = call(
        stack_tied_kernel,
        [turn(msg, r) for r in (1, 2, 3)] + [base_in],
        [((3, low, LANE), BF)],
        specs=[VM] * 3 + [ANY],
        limit=8,
        name="stack_o",
    )
    got = call(
        rows_kernel,
        [scal, tokens.reshape(4, row_count, width), cotangent.reshape(4, row_count, width), base_in],
        [((HALF + row_count, width), BF)] * 4,
        specs=[SM, VM, VM, ANY],
        limit=8,
        name="prep_rows",
    )
    got = [got[0]] + [turn(m, r) for r, m in enumerate(got[1:], 1)]
    (held,) = call(hold_kernel, [base, plane_in[2]], [((3, low, LANE), BF)], specs=[VM, ANY], limit=8, name="hold_out")
    planes = [[8 * g + c + 2 * k for k in range(4)] for g in range(lax.axis_size("img") // 8) for c in (0, 1)]
    joined = lax.all_gather(held, "img", axis_index_groups=planes)
    joined_got = swap(joined, CORE)

    bounds = [width, width, hidden, gate, gate, cells, width]
    pieces = []
    offset = 0
    for length in bounds:
        pieces.append(vectors[None, offset : offset + length])
        offset += length
    g_one, s_one, b_in, g_two, s_two, b_mix, b_out = pieces
    b_mix = jnp.pad(b_mix[0], (0, n - cells))[:, None]

    pos, xn = call(
        norm_kernel,
        [slot_col, *got, g_one, s_one],
        [((n, width), BF), ((n, width), BF)],
        name="norm_in",
    )
    sized = lambda kind: ((n, gate), kind)
    win, vhat, rstd, slope_v, vn = call(
        right_kernel,
        [scal, slot_col, xn, b_in, g_two, s_two, in_weight, *wi],
        [((width, hidden), BF), sized(F32), ((n, 1), F32), sized(F32), sized(BF)],
        [pltpu.VMEM((n, gate), F32)],
        specs=[SM] + [VM] * 14,
        flops=1_500_000_000,
        limit=20,
        name="right",
    )
    cot_pos, xt = call(
        side_kernel,
        [scal, slot_col, *got, xn, vn],
        [((n, width), BF), ((width, n), BF)],
        [pltpu.VMEM((width, n), BF)],
        specs=[SM] + [VM] * 6 + [ANY],
        name="place_cot",
    )
    u, slope_u = call(
        left_kernel,
        [xn, b_in, win, joined_got],
        [sized(F32), sized(F32)],
        [pltpu.VMEM((n, gate), F32)],
        specs=[VM] * 3 + [ANY],
        flops=1_000_000_000,
        limit=16,
        name="left",
    )
    packed = ((4, 4 * (low + side_rows), LANE), BF)
    mix, pre_u, sg, gated, wout, keep_a, send_a = call(
        spatial_kernel,
        [scal, pick, pack, xt, cot_pos, u, slope_u, vn, b_mix, spatial_weight, out_weight, joined, joined_got],
        [((n, n), BF), sized(BF), sized(BF), sized(BF), ((gate, width), BF), packed, packed],
        [
            pltpu.VMEM((512, LANE), BF),
            pltpu.VMEM((n, gate), F32),
            pltpu.VMEM((gate, width), BF),
        ],
        specs=[SM] + [VM] * 12,
        flops=4_000_000_000,
        limit=24,
        name="spatial",
    )
    core_a = swap(send_a, CORE)
    half = ((4, 4 * side_rows, LANE), BF)
    pre_v, keep_b, send_b, rows_b = call(
        back_kernel,
        [slot_col, xt, mix, sg, vhat, rstd, slope_v, g_two],
        [sized(BF), half, half, ((6, LANE), F32)],
        [pltpu.VMEM((n, gate), F32), pltpu.VMEM((8, gate), F32), pltpu.VMEM((8, gate), F32)],
        flops=2_000_000_000,
        limit=20,
        name="back",
    )
    core_b = swap(send_b, CORE)
    rows_a, rows_b4 = 4 * (low + side_rows), 4 * side_rows
    own_a, *send_a = call(
        core_kernel, [keep_a, core_a], [((rows_a, LANE), F32)] + [((rows_a, LANE), BF)] * 3, limit=12, name="core_a"
    )
    plane_a = [swap(s, m) for s, m in zip(send_a, (2, 4, 6))]
    *home, vec = call(
        token_kernel,
        [slot_col, slot_row, pos, cot_pos, win, pre_u, pre_v, sg, gated, wout, g_one, b_out, rows_b, send_a[2]],
        [((HALF + row_count, width), BF)] * 4 + [((STEP, LANE), F32)],
        [
            pltpu.VMEM((n, width), F32),
            pltpu.VMEM((n, width), BF),
            pltpu.VMEM((n, width), BF),
            pltpu.VMEM((8, width), F32),
            pltpu.VMEM((8, width), F32),
        ],
        specs=[VM] * 13 + [ANY],
        flops=2_000_000_000,
        limit=20,
        name="token_grad",
    )
    vec_got = swap(vec, CORE)
    own_b, *send_b, vec_own = call(
        core_vec_kernel,
        [keep_b, core_b, vec, vec_got, send_a[0]],
        [((rows_b4, LANE), F32)] + [((rows_b4 + STEP, LANE), BF)] * 3 + [((STEP, LANE), BF)],
        specs=[VM] * 4 + [ANY],
        name="core_b",
    )
    plane_b = [swap(s, m) for s, m in zip(send_b, (2, 4, 6))]
    home = [home[0]] + [turn(h, -r) for r, h in enumerate(home[1:], 1)]
    out_tokens, in_grad = call(
        home_kernel,
        [scal, *home],
        [((row_count, 4, width), BF), ((4, row_count, 1, width), F32)],
        [pltpu.VMEM((4, row_count, width), BF)],
        specs=[SM] + [VM] * 4,
        limit=8,
        name="home",
    )
    z_rows = low + side_rows
    own_a, *patch_a = call(
        plane_kernel, [own_a, *plane_a], [((z_rows, LANE), F32)] + [((z_rows, LANE), BF)] * 3, name="plane_a"
    )
    got_a = [turn(z, r) for r, z in enumerate(patch_a, 1)]
    own_b, *patch_b, vec_own = call(
        plane_vec_kernel,
        [own_b, vec_own, *plane_b, patch_a[0]],
        [((side_rows, LANE), F32)] + [((side_rows + STEP, LANE), BF)] * 3 + [((STEP, LANE), BF)],
        specs=[VM] * 5 + [ANY],
        name="plane_b",
    )
    got_b = [turn(z, r) for r, z in enumerate(patch_b, 1)]
    kind = BF if lax.axis_size("img") == 8 else F32
    (first,) = call(patch_kernel, [own_a, *got_a], [((z_rows, LANE), kind)], name="patch_a")
    first = img_gather(rest_of_img(first).astype(BF))
    second, vec_sum = call(
        patch_vec_kernel,
        [scal, own_b, vec_own, *got_b, first, in_grad],
        [((side_rows, LANE), kind), ((STEP, LANE), F32)],
        [pltpu.VMEM((4, STEP, LANE), F32)],
        specs=[SM] + [VM] * 5 + [ANY] * 2,
        name="patch_b",
    )
    second = img_gather(rest_of_img(second).astype(BF))
    vec_sum = rest_of_img(vec_sum).reshape(STEP * LANE)

    vec_sum = vec_sum[: vectors.shape[0]]

    images = micro_count * slot_count * lax.axis_size("img")
    rate_in, rate_out, rate_mix, rate_vec = step_rates(images, width, gate, cells)
    olds = [in_weight, in_moment, in_average, out_weight, out_moment, out_average]
    olds += [spatial_weight, spatial_moment, spatial_average]
    news = call(
        functools.partial(update_kernel, (rate_in, rate_out, rate_mix)),
        [first, second, *olds],
        [(a.shape, F32) for a in olds],
        [pltpu.VMEM(a.shape, F32) for a in olds] + [pltpu.SemaphoreType.DMA((9,))],
        specs=[VM] * 11,
        out_specs=[ANY] * 9,
        limit=20,
        name="update",
    )
    vec_new = nesterov(vectors, vec_sum, vector_moment, vector_average, rate_vec)
    return (out_tokens.transpose(1, 0, 2).reshape(tokens.shape), in_grad.transpose(0, 2, 1, 3), *news, *vec_new)


def solution(mesh):
    rows = P("patch", None)
    act = P(None, "img", "patch", None)
    return jax.shard_map(
        shards,
        mesh=mesh,
        in_specs=(act, act, P(None, "img"), P(None, "img", None), *([rows] * 9), P(), P(), P()),
        out_specs=(act, act, *([rows] * 9), P(), P(), P()),
        check_vma=False,
    )
```

```python
import functools
import math

import jax
import jax.numpy as jnp
from jax import lax
from jax.experimental import pallas as pl
from jax.experimental.pallas import tpu as pltpu
from jax.sharding import PartitionSpec as P

EPS = 1e-05
MOMENTUM = 0.9
AVG_DECAY = 0.8
BF = jnp.bfloat16
F32 = jnp.float32
I32 = jnp.int32
CORE, XBIT, YBIT = 1, 2, 4
LANE = 512
STEP = 16
ROWS = 81
HALF = 96


def step_rates(images, model_width, gate_width, cell_count):
    live_rows = 207.0 * images
    rate_in = 1.0 / (math.sqrt(model_width) * 1.4 * math.sqrt(live_rows))
    rate_out = 1.0 / (math.sqrt(gate_width / 4.0) * 1.2 * math.sqrt(live_rows))
    rate_mix = 1.0 / (math.sqrt(cell_count) * 1.5 * math.sqrt(gate_width * images / 2.0))
    rate_vec = 0.1 / (2.0 * math.sqrt(live_rows))
    return (rate_in, rate_out, rate_mix, rate_vec)


def nesterov(weight, grads, moment, average, rate):
    moment_new = MOMENTUM * moment + grads
    weight_new = weight - rate * (grads + MOMENTUM * moment_new)
    average_new = AVG_DECAY * average + (1.0 - AVG_DECAY) * weight_new
    return (weight_new, moment_new, average_new)


def turn(arr, r):
    n = lax.axis_size("patch")
    return lax.ppermute(arr, "patch", [(s, (s + r) % n) for s in range(n)])


def swap(arr, mask):
    n = lax.axis_size("img")
    return lax.ppermute(arr, "img", [(k, k ^ mask) for k in range(n)])


def dot(a, b, ca=1, cb=0):
    return lax.dot_general(a, b, (((ca,), (cb,)), ((), ())), preferred_element_type=F32)


def aligned(v, by):
    return pl.multiple_of(v, by)


def rows_of(i):
    return pl.ds(aligned(i * STEP, STEP), STEP)


def each_tile(n):
    steps = n // STEP
    return pl.loop(0, steps, unroll=7 if steps % 7 == 0 else 1)


def gelu_parts(pre):
    phi = 0.5 * (1.0 + lax.erf(pre * math.sqrt(0.5)))
    slope = phi + pre * (jnp.exp(-0.5 * pre * pre) * (1.0 / math.sqrt(2.0 * math.pi)))
    return pre * phi, slope


def mean_rows(v):
    return jnp.sum(v, axis=-1, keepdims=True) * (1.0 / v.shape[-1])


def slot_kernel(grid, scal, counts, crops, col_ref, row_ref):
    own = scal[0]
    lane = lax.broadcasted_iota(I32, counts.shape, 1)
    count = jnp.sum(jnp.where(lane == own, counts[...], 0), axis=1, keepdims=True)
    start = crops[own][:, 0:1]
    cells = grid * grid
    side = jnp.zeros_like(count)
    top = jnp.zeros_like(count)
    for k in range(1, grid + 1):
        side = jnp.where(count == k * k, k, side)
        top = top + jnp.where(start >= k * grid, 1, 0)
    quarter = count >> 2
    left = start - top * grid
    for ref, dim in ((col_ref, 0), (row_ref, 1)):
        place = lax.broadcasted_iota(I32, ref.shape, dim)
        row = jnp.zeros(ref.shape, I32)
        for k in range(1, grid):
            row = row + jnp.where(place >= k * grid, 1, 0)
        drow = row - top
        dcol = place - row * grid - left
        inside = (drow >= 0) & (drow < side) & (dcol >= 0) & (dcol < side) & (place < cells)
        order = drow * side + dcol
        block = jnp.zeros(ref.shape, I32)
        for k in (1, 2, 3):
            block = block + jnp.where(order >= k * quarter, 1, 0)
        slot = ((block - own) & 3) * ROWS + order - block * quarter
        ref[...] = jnp.where(inside, slot, -1)


def onehot(slot, lanes, base):
    lane = lax.broadcasted_iota(I32, (slot.shape[0], lanes), 1) + base
    return jnp.where(slot == lane, 1.0, 0.0).astype(BF)


def side_kernel(scal, slot_ref, m0, m1, m2, m3, xn_ref, tie, pos_ref, xt_ref, turned):
    place_kernel(slot_ref, m0, m1, m2, m3, pos_ref)
    own, unit = scal[0], scal[1]
    turned[...] = xn_ref[...].T
    for k, (c, y, x, r) in enumerate(ORDER):
        who = lax.rem(own + r, 4)
        e = c + 2 * x + 4 * y
        src = who * 128 + (unit ^ e) * STEP
        xt_ref[k * STEP : (k + 1) * STEP, :] = turned[pl.ds(aligned(src, STEP), STEP), :]


class Copies:
    def __init__(self, sems):
        self.sems, self.all = sems, []

    def bring(self, src, dst):
        copy = pltpu.make_async_copy(src, dst, self.sems.at[len(self.all)])
        copy.start()
        self.all.append(copy)

    def wait(self):
        for copy in self.all:
            copy.wait()


def pick_kernel(per, own, unit, pick_ref, pack_ref):
    n = pick_ref.shape[0]
    cell = lax.broadcasted_iota(I32, (n, pick_ref.shape[1]), 0)
    lane = lax.broadcasted_iota(I32, (n, pick_ref.shape[1]), 1)
    part = jnp.where(cell >= per, 1, 0) + jnp.where(cell >= 2 * per, 1, 0) + jnp.where(cell >= 3 * per, 1, 0)
    pick_ref[...] = jnp.where(lane == cell + part * (128 - per), 1.0, 0.0).astype(BF)
    big = lax.broadcasted_iota(I32, (512, n), 0)
    lane = lax.broadcasted_iota(I32, (512, n), 1)
    within = ((big >> 6) ^ unit) * STEP + (big & 15)
    a = (((big >> 4) + own) & 3) * per + within
    pack_ref[...] = jnp.where((lane == a) & (within < per), 1.0, 0.0).astype(BF)


def out_kernel(grid, scal, counts, crops, w_out, mix, msg, col_ref, row_ref, pick_ref, pack_ref, held, strip, sems):
    unit = scal[1]
    rows = held.shape[0]
    copies = Copies(sems)
    copies.bring(w_out.at[pl.ds(aligned(unit * rows, STEP), rows), :], held)
    slot_kernel(grid, scal, counts, crops, col_ref, row_ref)
    pick_kernel(mix.shape[0], scal[0], unit, pick_ref, pack_ref)
    strip[...] = jnp.zeros_like(strip)
    strip[0 : mix.shape[0], 0 : mix.shape[1]] = mix[...].astype(BF)
    copies.wait()
    msg[0:rows, :] = held[...].astype(BF)
    msg[rows:, :] = strip[pl.ds(aligned(unit * STEP, STEP), STEP), :]


def rows_kernel(scal, tok, cot, tie, m0, m1, m2, m3):
    for r, msg in enumerate((m0, m1, m2, m3)):
        to = lax.rem(scal[0] + (4 - r), 4)
        msg[0:ROWS, :] = tok[to]
        msg[HALF : HALF + ROWS, :] = cot[to]


def hold_kernel(src, tie, dst):
    dst[...] = src[...]


def stack_tied_kernel(m1, m2, m3, tie, out):
    stack_kernel(m1, m2, m3, out)


def join_kernel(p0, p1, p2, p3, out):
    for e, part in enumerate((p0, p1, p2, p3)):
        out[e] = part[...]


def join_tied_kernel(p0, p1, p2, p3, tie, out):
    join_kernel(p0, p1, p2, p3, out)


def stack_kernel(m1, m2, m3, out):
    for r, msg in enumerate((m1, m2, m3)):
        out[r] = msg[0 : out.shape[1], :]


def place(slot_ref, blocks, at, pos_ref):
    slot = slot_ref[...]
    total = None
    for r, msg in enumerate(blocks):
        part = dot(onehot(slot, ROWS, r * ROWS), msg[at : at + ROWS, :])
        total = part if total is None else total + part
    pos_ref[...] = total.astype(BF)


def place_kernel(slot_ref, m0, m1, m2, m3, pos_ref):
    place(slot_ref, (m0, m1, m2, m3), HALF, pos_ref)


ORDER = [(c, y, x, r) for c in (0, 1) for y in (0, 1) for x in (0, 1) for r in range(4)]


def norm_kernel(slot_ref, m0, m1, m2, m3, gain, shift, pos_ref, xn_ref):
    place(slot_ref, (m0, m1, m2, m3), 0, pos_ref)
    @each_tile(pos_ref.shape[0])
    def _(i):
        x = pos_ref[rows_of(i), :].astype(F32)
        cen = x - mean_rows(x)
        rstd = lax.rsqrt(mean_rows(cen * cen) + EPS)
        xn_ref[rows_of(i), :] = (cen * rstd * gain[...] + shift[...]).astype(BF)


def right_kernel(scal, slot_ref, xn_ref, b_in, g_two, s_two, wi_own, *rest):
    wi, rest = rest[:8], rest[8:]
    win, vhat_ref, rstd_ref, slope_v, vn_ref, pre = rest
    own, unit = scal[0], scal[1]
    n, gate = vhat_ref.shape
    tiles = gate // LANE
    win[pl.ds(aligned(own * 128, 128), 128), :] = wi_own[...].astype(BF)
    for e in range(8):
        for r in (1, 2, 3):
            who = lax.rem(own + (4 - r), 4)
            at = who * 128 + (unit ^ e) * STEP
            win[pl.ds(aligned(at, STEP), STEP), :] = wi[e][r - 1]

    xn = xn_ref[...]
    for k in range(tiles):
        cols = slice(k * LANE, (k + 1) * LANE)
        wide = slice(gate + k * LANE, gate + (k + 1) * LANE)
        pre[:, cols] = dot(xn, win[:, wide]) + b_in[:, wide]

    @each_tile(n)
    def _(i):
        rows = rows_of(i)
        v, slope = gelu_parts(pre[rows, :])
        slope_v[rows, :] = slope
        cen = v - mean_rows(v)
        rstd = lax.rsqrt(mean_rows(cen * cen) + EPS)
        vhat = cen * rstd
        vhat_ref[rows, :] = vhat
        rstd_ref[rows, :] = rstd
        vn = jnp.where(slot_ref[rows, :] >= 0, vhat * g_two[...] + s_two[...], 0.0)
        vn_ref[rows, :] = vn.astype(BF)


def left_kernel(xn_ref, b_in, win, *rest):
    u_ref, slope_u, pre = rest[-3:]
    n, gate = u_ref.shape
    xn = xn_ref[...]
    for k in range(gate // LANE):
        cols = slice(k * LANE, (k + 1) * LANE)
        pre[:, cols] = dot(xn, win[:, cols]) + b_in[:, cols]

    @each_tile(n)
    def _(i):
        rows = rows_of(i)
        u, slope = gelu_parts(pre[rows, :])
        u_ref[rows, :] = u
        slope_u[rows, :] = slope


def spatial_kernel(scal, pick_ref, pack_ref, xt_ref, cot_ref, u_ref, slope_u, vn_ref, b_mix, mix_own, wo_own, *rest):
    wo, rest = rest[:2], rest[2:]
    mix_ref, pre_u, sg_ref, gated, wout, keep, send, *rest = rest
    mixp, spat, gtmp = rest
    own, unit = scal[0], scal[1]
    n, gate = u_ref.shape
    tiles = gate // LANE
    out_unit = wout.shape[0] // 32
    wout[pl.ds(aligned(own * 8 * out_unit, STEP), 8 * out_unit), :] = wo_own[...].astype(BF)
    for k in range(4):
        for c in (0, 1):
            piece = 2 * k + ((unit & 1) ^ c)
            for r in (1, 2, 3):
                who = lax.rem(own + (4 - r), 4)
                at = (who * 8 + piece) * out_unit
                wout[pl.ds(aligned(at, STEP), out_unit), :] = wo[c][k, r - 1, 0:out_unit, :]
                at = who * 128 + piece * STEP
                mixp[pl.ds(aligned(at, STEP), STEP), :] = wo[c][k, r - 1, out_unit:, :]
    per, cells = mix_own.shape
    mine = aligned(own * 128, 128)
    mixp[pl.ds(mine, 128), :] = jnp.zeros((128, LANE), BF)
    mixp[pl.ds(mine, per), 0:cells] = mix_own[...].astype(BF)
    mix_ref[...] = dot(pick_ref[...], mixp[:, :n]).astype(BF)
    mix = mix_ref[...]
    for k in range(tiles):
        cols = slice(k * LANE, (k + 1) * LANE)
        sp = dot(mix, vn_ref[:, cols]) + b_mix[...]
        spat[:, cols] = sp
        gated[:, cols] = (u_ref[:, cols] * sp).astype(BF)

    cot = cot_ref[...]
    for k in range(tiles):
        cols = slice(k * LANE, (k + 1) * LANE)
        gg = dot(cot, wout[cols, :], 1, 1)
        sg_ref[:, cols] = (gg * u_ref[:, cols]).astype(BF)
        pre_u[:, cols] = (gg * spat[:, cols] * slope_u[:, cols]).astype(BF)

    low = out_unit + STEP
    for k in range(tiles):
        rows = slice(k * LANE, (k + 1) * LANE)
        gtmp[rows, :] = dot(gated[:, rows], cot, 0, 0).astype(BF)
    height = keep.shape[1] // 4
    for c, dst in ((0, keep), (1, send)):
        for e in range(4):
            for r in range(4):
                at = (lax.rem(own + r, 4) * 8 + (unit ^ (c + 2 * e))) * out_unit
                dst[e, r * height : r * height + out_unit, :] = gtmp[pl.ds(aligned(at, STEP), out_unit), :]
    gmix = dot(sg_ref[...], vn_ref[...], 1, 1).astype(BF)
    padded = dot(pack_ref[...], gmix).astype(BF)
    for c, dst in ((0, keep), (1, send)):
        for e in range(4):
            for r in range(4):
                at = (c + 2 * e) * 64 + r * STEP
                to = r * height + out_unit
                dst[e, to : to + STEP, :] = jnp.zeros((STEP, LANE), BF)
                dst[e, to : to + STEP, 0:n] = padded[at : at + STEP, :]
    for k in range(tiles):
        cols = slice(k * LANE, (k + 1) * LANE)
        part = dot(xt_ref[...], pre_u[:, cols]).astype(BF)
        for j, (c, y, x, r) in enumerate(ORDER):
            to = r * height + low + k * STEP
            (send if c else keep)[x + 2 * y, to : to + STEP, :] = part[j * STEP : (j + 1) * STEP, :]


def back_kernel(slot_ref, xt_ref, mix_ref, sg_ref, vhat_ref, rstd_ref, slope_v, g_two, pre_v, keep, send, rows_ref, vng, gain, shift):
    n, gate = vhat_ref.shape
    tiles = gate // LANE
    mix = mix_ref[...]
    for k in range(tiles):
        cols = slice(k * LANE, (k + 1) * LANE)
        vng[:, cols] = dot(mix, sg_ref[:, cols], 0, 0)
    gain[...] = jnp.zeros_like(gain)
    shift[...] = jnp.zeros_like(shift)

    @each_tile(n)
    def _(i):
        rows = rows_of(i)
        vg = jnp.where(slot_ref[rows, :] >= 0, vng[rows, :], 0.0)
        vhat = vhat_ref[rows, :]
        gain[...] += jnp.sum((vg * vhat).reshape(2, 8, gate), 0)
        shift[...] += jnp.sum(vg.reshape(2, 8, gate), 0)
        h = vg * g_two[...]
        v_grad = rstd_ref[rows, :] * (h - mean_rows(h) - vhat * mean_rows(h * vhat))
        pre_v[rows, :] = (v_grad * slope_v[rows, :]).astype(BF)

    height = keep.shape[1] // 4
    for k in range(tiles):
        cols = slice(k * LANE, (k + 1) * LANE)
        part = dot(xt_ref[...], pre_v[:, cols]).astype(BF)
        for j, (c, y, x, r) in enumerate(ORDER):
            to = r * height + k * STEP
            (send if c else keep)[x + 2 * y, to : to + STEP, :] = part[j * STEP : (j + 1) * STEP, :]
        rows_ref[k : k + 1, :] = jnp.sum(gain[:, cols], 0, keepdims=True)
        rows_ref[tiles + k : tiles + k + 1, :] = jnp.sum(shift[:, cols], 0, keepdims=True)


def token_kernel(slot_ref, slot_row, pos_ref, cot_ref, win, pre_u, pre_v, sg_ref, gated, wout, g_one, b_out, rows_ref, *rest):
    _, h0, h1, h2, h3, vec, xg, out_ref, in_ref, gain, shift = rest
    n, gate = pre_u.shape
    xg[...] = dot(pre_u[...], win[:, :gate], 1, 1) + dot(pre_v[...], win[:, gate:], 1, 1)
    gain[...] = jnp.zeros_like(gain)
    shift[...] = jnp.zeros_like(shift)
    width = xg.shape[1]

    @each_tile(n)
    def _(i):
        rows = rows_of(i)
        x = pos_ref[rows, :].astype(F32)
        cen = x - mean_rows(x)
        rstd = lax.rsqrt(mean_rows(cen * cen) + EPS)
        xhat = cen * rstd
        g = xg[rows, :]
        gain[...] += jnp.sum((g * xhat).reshape(2, 8, width), 0)
        shift[...] += jnp.sum(g.reshape(2, 8, width), 0)
        h = g * g_one[...]
        x_grad = rstd * (h - mean_rows(h) - xhat * mean_rows(h * xhat))
        total = cot_ref[rows, :].astype(F32) + x_grad
        in_ref[rows, :] = jnp.where(slot_ref[rows, :] >= 0, total, 0.0).astype(BF)

    branch = dot(gated[...], wout[...]) + b_out[...]
    out_ref[...] = jnp.where(slot_ref[...] >= 0, pos_ref[...].astype(F32) + branch, 0.0).astype(BF)
    for r, dst in enumerate((h0, h1, h2, h3)):
        spot = lax.broadcasted_iota(I32, (ROWS, n), 0) + r * ROWS
        pick = jnp.where(slot_row[...] == spot, 1.0, 0.0).astype(BF)
        dst[0:ROWS, :] = dot(pick, out_ref[...]).astype(BF)
        dst[HALF : HALF + ROWS, :] = dot(pick, in_ref[...]).astype(BF)

    ones = jnp.ones((8, n), BF)
    tiles = gate // LANE
    vec[0:1, :] = jnp.sum(gain[...], 0, keepdims=True)
    vec[1:2, :] = jnp.sum(shift[...], 0, keepdims=True)
    for k in range(tiles):
        cols = slice(k * LANE, (k + 1) * LANE)
        vec[2 + k : 3 + k, :] = dot(ones, pre_u[:, cols])[0:1]
        vec[2 + tiles + k : 3 + tiles + k, :] = dot(ones, pre_v[:, cols])[0:1]
    at = 2 + 2 * tiles
    vec[at : at + 2 * tiles, :] = rows_ref[...]
    at += 2 * tiles
    cells = 4 * ROWS
    lane = lax.broadcasted_iota(I32, (1, LANE), 1)
    last = pltpu.roll(dot(ones, cot_ref[...])[0:1], cells, 1)
    vec[at : at + 1, 0:n] = dot(jnp.ones((8, gate), BF), sg_ref[...], 1, 1)[0:1]
    vec[at : at + 1, :] = jnp.where(lane < cells, vec[at : at + 1, :], last)
    vec[at + 1 : at + 2, :] = jnp.where(lane < cells, last, 0.0)


def put_vec(ref, at, v):
    ref[at : at + STEP, :] = v.astype(BF)


def get_vec(ref, at):
    return ref[at : at + STEP, :].astype(F32)


def core_kernel(keep, got, own, s1, s2, s3):
    for e, dst in enumerate((own, s1, s2, s3)):
        dst[...] = (keep[e].astype(F32) + got[e].astype(F32)).astype(dst.dtype)


def core_vec_kernel(keep, got, vec, vec_got, tie, own, s1, s2, s3, vec_own):
    rows = own.shape[0]
    total = vec[...] + vec_got[...]
    put_vec(vec_own, 0, total)
    for e, dst in enumerate((own, s1, s2, s3)):
        dst[0:rows, :] = (keep[e].astype(F32) + got[e].astype(F32)).astype(dst.dtype)
        if e:
            put_vec(dst, rows, total)


def plane_kernel(own, g1, g2, g3, z0, z1, z2, z3):
    rows = z0.shape[0]
    for r, dst in enumerate((z0, z1, z2, z3)):
        at = slice(r * rows, (r + 1) * rows)
        total = (own[at, :] + g1[at, :].astype(F32)) + (g2[at, :].astype(F32) + g3[at, :].astype(F32))
        dst[...] = total.astype(dst.dtype)


def plane_vec_kernel(own, vec_own, g1, g2, g3, tie, z0, z1, z2, z3, vec_out):
    rows, at = z0.shape[0], own.shape[0]
    vec = (get_vec(vec_own, 0) + get_vec(g1, at)) + (get_vec(g2, at) + get_vec(g3, at))
    put_vec(vec_out, 0, vec)
    for r, dst in enumerate((z0, z1, z2, z3)):
        at = slice(r * rows, (r + 1) * rows)
        total = (own[at, :] + g1[at, :].astype(F32)) + (g2[at, :].astype(F32) + g3[at, :].astype(F32))
        dst[0:rows, :] = total.astype(dst.dtype)
        if r:
            put_vec(dst, rows, vec)


def patch_kernel(own, g1, g2, g3, out):
    rows = own.shape[0]
    total = own[...]
    for g in (g1, g2, g3):
        total = total + g[0:rows, :].astype(F32)
    out[...] = total.astype(out.dtype)


def patch_vec_kernel(scal, own, vec_own, g1, g2, g3, tie, tie_home, out, vec_out, held):
    patch_kernel(own, g1, g2, g3, out)
    rows = own.shape[0]
    me = scal[0]
    held[me] = get_vec(vec_own, 0)
    for r, g in enumerate((g1, g2, g3), 1):
        held[lax.rem(me + (4 - r), 4)] = get_vec(g, rows)
    vec_out[...] = (held[0] + held[1]) + (held[2] + held[3])


def home_kernel(scal, h0, h1, h2, h3, out_ref, grad_ref, held):
    for r, h in enumerate((h0, h1, h2, h3)):
        m = lax.rem(scal[0] + (4 - r), 4)
        held[m] = h[0:ROWS, :]
        grad_ref[m, :, 0, :] = h[HALF : HALF + ROWS, :].astype(F32)
    for m in range(4):
        out_ref[:, m, :] = held[m]


def update_kernel(rates, first, second, *rest):
    olds, rest = rest[:9], rest[9:]
    news, rest = rest[:9], rest[9:]
    made, sems = rest[:9], rest[9]
    copies = Copies(sems)
    out_unit = olds[3].shape[0] // 8
    low = out_unit + STEP

    def step(which, rows, cols, grads):
        old, new = olds[3 * which : 3 * which + 3], made[3 * which : 3 * which + 3]
        at = (slice(*rows), slice(*cols))
        fresh = nesterov(old[0][at], grads.astype(F32), old[1][at], old[2][at], rates[which])
        for ref, value in zip(new, fresh):
            ref[at] = value

    def send(which):
        for j in range(3 * which, 3 * which + 3):
            copies.bring(made[j], news[j])

    width = olds[3].shape[1]
    for u in range(8):
        step(1, (u * out_unit, (u + 1) * out_unit), (0, width), first[u, 0:out_unit, :])
    send(1)
    mix_rows, cells = olds[6].shape
    for u in range(-(-mix_rows // STEP)):
        rows = min(STEP, mix_rows - u * STEP)
        step(2, (u * STEP, u * STEP + rows), (0, cells), first[u, out_unit : out_unit + rows, 0:cells])
    send(2)
    tiles = olds[0].shape[1] // LANE
    for u in range(8):
        for k in range(tiles):
            if k < tiles // 2:
                grads = first[u, low + k * STEP : low + (k + 1) * STEP, :]
            else:
                j = k - tiles // 2
                grads = second[u, j * STEP : (j + 1) * STEP, :]
            step(0, (u * STEP, (u + 1) * STEP), (k * LANE, (k + 1) * LANE), grads)
    send(0)
    copies.wait()


VM = pl.BlockSpec(memory_space=pltpu.VMEM)
SM = pl.BlockSpec(memory_space=pltpu.SMEM)
ANY = pl.BlockSpec(memory_space=pl.ANY)


def call(body, ins, outs, scratch=(), specs=None, out_specs=None, flops=100_000_000, limit=16, name=None):
    moved = sum(math.prod(a.shape) * a.dtype.itemsize for a in ins)
    return pl.pallas_call(
        body,
        out_shape=[jax.ShapeDtypeStruct(s, d) for s, d in outs],
        in_specs=specs or [VM] * len(ins),
        out_specs=out_specs or [VM] * len(outs),
        scratch_shapes=list(scratch),
        compiler_params=pltpu.CompilerParams(vmem_limit_bytes=limit * 2**20),
        cost_estimate=pl.CostEstimate(flops=flops, bytes_accessed=moved, transcendentals=0),
        name=name,
    )(*ins)


def rest_of_img(total):
    mask = 8
    while mask < lax.axis_size("img"):
        total = total + swap(total, mask)
        mask *= 2
    return total


def img_gather(arr):
    size = lax.axis_size("img")
    groups = [[g * 8 + k for k in range(8)] for g in range(size // 8)]
    return lax.all_gather(arr, "img", axis_index_groups=groups)


def shards(
    tokens,
    cotangent,
    patch_count,
    crop_index,
    in_weight,
    in_moment,
    in_average,
    out_weight,
    out_moment,
    out_average,
    spatial_weight,
    spatial_moment,
    spatial_average,
    vectors,
    vector_moment,
    vector_average,
):
    p = lax.axis_index("patch")
    unit = lax.axis_index("img") % 8
    micro_count, slot_count, row_count, width = tokens.shape
    hidden = in_weight.shape[1]
    gate = hidden // 2
    mix_rows, cells = spatial_weight.shape
    assert micro_count == lax.axis_size("patch") == 4 and slot_count == 1
    assert width == LANE and in_weight.shape[0] == 128 and row_count == mix_rows == 81
    grid = math.isqrt(cells)
    n = -(-cells // STEP) * STEP
    in_unit = in_weight.shape[0] // 8
    out_unit = out_weight.shape[0] // 8
    low = out_unit + STEP
    side_rows = in_unit * gate // LANE
    scal = jnp.stack([p, unit]).astype(I32)

    def over_plane(base):
        near = swap(base, XBIT)
        return [base, near, swap(base, YBIT), swap(near, YBIT)]

    wi_piece = lax.dynamic_slice_in_dim(in_weight, unit * in_unit, in_unit, 0).astype(BF)

    msg, slot_col, slot_row, pick, pack = call(
        functools.partial(out_kernel, grid),
        [scal, patch_count.reshape(1, 4), crop_index, out_weight, spatial_weight],
        [((low, LANE), BF), ((n, 1), I32), ((1, n), I32), ((n, 512), BF), ((512, n), BF)],
        [pltpu.VMEM((out_unit, width), F32), pltpu.VMEM((128, LANE), BF), pltpu.SemaphoreType.DMA((1,))],
        specs=[SM, VM, VM, ANY, VM],
        limit=8,
        name="prep_out",
    )
    (base_in,) = call(
        stack_tied_kernel,
        [turn(wi_piece, r) for r in (1, 2, 3)] + [msg],
        [((3, in_unit, hidden), BF)],
        specs=[VM] * 3 + [ANY],
        limit=8,
        name="stack_i",
    )
    plane_in = over_plane(base_in)
    wi = [arr for part in plane_in for arr in (part, swap(part, CORE))]
    (base,) = call(
        stack_tied_kernel,
        [turn(msg, r) for r in (1, 2, 3)] + [base_in],
        [((3, low, LANE), BF)],
        specs=[VM] * 3 + [ANY],
        limit=8,
        name="stack_o",
    )
    got = call(
        rows_kernel,
        [scal, tokens.reshape(4, row_count, width), cotangent.reshape(4, row_count, width), base_in],
        [((HALF + row_count, width), BF)] * 4,
        specs=[SM, VM, VM, ANY],
        limit=8,
        name="prep_rows",
    )
    got = [got[0]] + [turn(m, -r) for r, m in enumerate(got[1:], 1)]
    (held,) = call(hold_kernel, [base, plane_in[2]], [((3, low, LANE), BF)], specs=[VM, ANY], limit=8, name="hold_out")
    planes = [[8 * g + c + 2 * k for k in range(4)] for g in range(lax.axis_size("img") // 8) for c in (0, 1)]
    joined = lax.all_gather(held, "img", axis_index_groups=planes)
    joined_got = swap(joined, CORE)

    bounds = [width, width, hidden, gate, gate, cells, width]
    pieces = []
    offset = 0
    for length in bounds:
        pieces.append(vectors[None, offset : offset + length])
        offset += length
    g_one, s_one, b_in, g_two, s_two, b_mix, b_out = pieces
    b_mix = jnp.pad(b_mix[0], (0, n - cells))[:, None]

    pos, xn = call(
        norm_kernel,
        [slot_col, *got, g_one, s_one],
        [((n, width), BF), ((n, width), BF)],
        name="norm_in",
    )
    sized = lambda kind: ((n, gate), kind)
    win, vhat, rstd, slope_v, vn = call(
        right_kernel,
        [scal, slot_col, xn, b_in, g_two, s_two, in_weight, *wi],
        [((width, hidden), BF), sized(F32), ((n, 1), F32), sized(F32), sized(BF)],
        [pltpu.VMEM((n, gate), F32)],
        specs=[SM] + [VM] * 14,
        flops=1_500_000_000,
        limit=20,
        name="right",
    )
    cot_pos, xt = call(
        side_kernel,
        [scal, slot_col, *got, xn, vn],
        [((n, width), BF), ((width, n), BF)],
        [pltpu.VMEM((width, n), BF)],
        specs=[SM] + [VM] * 6 + [ANY],
        name="place_cot",
    )
    u, slope_u = call(
        left_kernel,
        [xn, b_in, win, joined_got],
        [sized(F32), sized(F32)],
        [pltpu.VMEM((n, gate), F32)],
        specs=[VM] * 3 + [ANY],
        flops=1_000_000_000,
        limit=16,
        name="left",
    )
    packed = ((4, 4 * (low + side_rows), LANE), BF)
    mix, pre_u, sg, gated, wout, keep_a, send_a = call(
        spatial_kernel,
        [scal, pick, pack, xt, cot_pos, u, slope_u, vn, b_mix, spatial_weight, out_weight, joined, joined_got],
        [((n, n), BF), sized(BF), sized(BF), sized(BF), ((gate, width), BF), packed, packed],
        [
            pltpu.VMEM((512, LANE), BF),
            pltpu.VMEM((n, gate), F32),
            pltpu.VMEM((gate, width), BF),
        ],
        specs=[SM] + [VM] * 12,
        flops=4_000_000_000,
        limit=24,
        name="spatial",
    )
    core_a = swap(send_a, CORE)
    half = ((4, 4 * side_rows, LANE), BF)
    pre_v, keep_b, send_b, rows_b = call(
        back_kernel,
        [slot_col, xt, mix, sg, vhat, rstd, slope_v, g_two],
        [sized(BF), half, half, ((6, LANE), F32)],
        [pltpu.VMEM((n, gate), F32), pltpu.VMEM((8, gate), F32), pltpu.VMEM((8, gate), F32)],
        flops=2_000_000_000,
        limit=20,
        name="back",
    )
    core_b = swap(send_b, CORE)
    rows_a, rows_b4 = 4 * (low + side_rows), 4 * side_rows
    own_a, *send_a = call(
        core_kernel, [keep_a, core_a], [((rows_a, LANE), F32)] + [((rows_a, LANE), BF)] * 3, limit=12, name="core_a"
    )
    plane_a = [swap(s, m) for s, m in zip(send_a, (2, 4, 6))]
    *home, vec = call(
        token_kernel,
        [slot_col, slot_row, pos, cot_pos, win, pre_u, pre_v, sg, gated, wout, g_one, b_out, rows_b, send_a[2]],
        [((HALF + row_count, width), BF)] * 4 + [((STEP, LANE), F32)],
        [
            pltpu.VMEM((n, width), F32),
            pltpu.VMEM((n, width), BF),
            pltpu.VMEM((n, width), BF),
            pltpu.VMEM((8, width), F32),
            pltpu.VMEM((8, width), F32),
        ],
        specs=[VM] * 13 + [ANY],
        flops=2_000_000_000,
        limit=20,
        name="token_grad",
    )
    vec_got = swap(vec, CORE)
    own_b, *send_b, vec_own = call(
        core_vec_kernel,
        [keep_b, core_b, vec, vec_got, send_a[0]],
        [((rows_b4, LANE), F32)] + [((rows_b4 + STEP, LANE), BF)] * 3 + [((STEP, LANE), BF)],
        specs=[VM] * 4 + [ANY],
        name="core_b",
    )
    plane_b = [swap(s, m) for s, m in zip(send_b, (2, 4, 6))]
    home = [home[0]] + [turn(h, r) for r, h in enumerate(home[1:], 1)]
    out_tokens, in_grad = call(
        home_kernel,
        [scal, *home],
        [((row_count, 4, width), BF), ((4, row_count, 1, width), F32)],
        [pltpu.VMEM((4, row_count, width), BF)],
        specs=[SM] + [VM] * 4,
        limit=8,
        name="home",
    )
    z_rows = low + side_rows
    own_a, *patch_a = call(
        plane_kernel, [own_a, *plane_a], [((z_rows, LANE), F32)] + [((z_rows, LANE), BF)] * 3, name="plane_a"
    )
    got_a = [turn(z, r) for r, z in enumerate(patch_a, 1)]
    own_b, *patch_b, vec_own = call(
        plane_vec_kernel,
        [own_b, vec_own, *plane_b, patch_a[0]],
        [((side_rows, LANE), F32)] + [((side_rows + STEP, LANE), BF)] * 3 + [((STEP, LANE), BF)],
        specs=[VM] * 5 + [ANY],
        name="plane_b",
    )
    got_b = [turn(z, r) for r, z in enumerate(patch_b, 1)]
    kind = BF if lax.axis_size("img") == 8 else F32
    (first,) = call(patch_kernel, [own_a, *got_a], [((z_rows, LANE), kind)], name="patch_a")
    first = img_gather(rest_of_img(first).astype(BF))
    second, vec_sum = call(
        patch_vec_kernel,
        [scal, own_b, vec_own, *got_b, first, in_grad],
        [((side_rows, LANE), kind), ((STEP, LANE), F32)],
        [pltpu.VMEM((4, STEP, LANE), F32)],
        specs=[SM] + [VM] * 5 + [ANY] * 2,
        name="patch_b",
    )
    second = img_gather(rest_of_img(second).astype(BF))
    vec_sum = rest_of_img(vec_sum).reshape(STEP * LANE)

    vec_sum = vec_sum[: vectors.shape[0]]

    images = micro_count * slot_count * lax.axis_size("img")
    rate_in, rate_out, rate_mix, rate_vec = step_rates(images, width, gate, cells)
    olds = [in_weight, in_moment, in_average, out_weight, out_moment, out_average]
    olds += [spatial_weight, spatial_moment, spatial_average]
    news = call(
        functools.partial(update_kernel, (rate_in, rate_out, rate_mix)),
        [first, second, *olds],
        [(a.shape, F32) for a in olds],
        [pltpu.VMEM(a.shape, F32) for a in olds] + [pltpu.SemaphoreType.DMA((9,))],
        specs=[VM] * 11,
        out_specs=[ANY] * 9,
        limit=20,
        name="update",
    )
    vec_new = nesterov(vectors, vec_sum, vector_moment, vector_average, rate_vec)
    return (out_tokens.transpose(1, 0, 2).reshape(tokens.shape), in_grad.transpose(0, 2, 1, 3), *news, *vec_new)


def solution(mesh):
    rows = P("patch", None)
    act = P(None, "img", "patch", None)
    return jax.shard_map(
        shards,
        mesh=mesh,
        in_specs=(act, act, P(None, "img"), P(None, "img", None), *([rows] * 9), P(), P(), P()),
        out_specs=(act, act, *([rows] * 9), P(), P(), P()),
        check_vma=False,
    )
```

```python
import functools
import math

import jax
import jax.numpy as jnp
from jax import lax
from jax.experimental import pallas as pl
from jax.experimental.pallas import tpu as pltpu
from jax.sharding import PartitionSpec as P

EPS = 1e-05
MOMENTUM = 0.9
AVG_DECAY = 0.8
BF = jnp.bfloat16
F32 = jnp.float32
I32 = jnp.int32
CORE, XBIT, YBIT = 1, 2, 4
LANE = 512
STEP = 16
ROWS = 81
HALF = 96


def step_rates(images, model_width, gate_width, cell_count):
    live_rows = 207.0 * images
    rate_in = 1.0 / (math.sqrt(model_width) * 1.4 * math.sqrt(live_rows))
    rate_out = 1.0 / (math.sqrt(gate_width / 4.0) * 1.2 * math.sqrt(live_rows))
    rate_mix = 1.0 / (math.sqrt(cell_count) * 1.5 * math.sqrt(gate_width * images / 2.0))
    rate_vec = 0.1 / (2.0 * math.sqrt(live_rows))
    return (rate_in, rate_out, rate_mix, rate_vec)


def nesterov(weight, grads, moment, average, rate):
    moment_new = MOMENTUM * moment + grads
    weight_new = weight - rate * (grads + MOMENTUM * moment_new)
    average_new = AVG_DECAY * average + (1.0 - AVG_DECAY) * weight_new
    return (weight_new, moment_new, average_new)


def turn(arr, r):
    n = lax.axis_size("patch")
    return lax.ppermute(arr, "patch", [(s, (s + r) % n) for s in range(n)])


def swap(arr, mask):
    n = lax.axis_size("img")
    return lax.ppermute(arr, "img", [(k, k ^ mask) for k in range(n)])


def dot(a, b, ca=1, cb=0):
    return lax.dot_general(a, b, (((ca,), (cb,)), ((), ())), preferred_element_type=F32)


def aligned(v, by):
    return pl.multiple_of(v, by)


def rows_of(i):
    return pl.ds(aligned(i * STEP, STEP), STEP)


def each_tile(n):
    steps = n // STEP
    return pl.loop(0, steps, unroll=7 if steps % 7 == 0 else 1)


def gelu_parts(pre):
    phi = 0.5 * (1.0 + lax.erf(pre * math.sqrt(0.5)))
    slope = phi + pre * (jnp.exp(-0.5 * pre * pre) * (1.0 / math.sqrt(2.0 * math.pi)))
    return pre * phi, slope


def mean_rows(v):
    return jnp.sum(v, axis=-1, keepdims=True) * (1.0 / v.shape[-1])


def slot_kernel(grid, scal, counts, crops, col_ref, row_ref):
    own = scal[0]
    lane = lax.broadcasted_iota(I32, counts.shape, 1)
    count = jnp.sum(jnp.where(lane == own, counts[...], 0), axis=1, keepdims=True)
    start = crops[own][:, 0:1]
    cells = grid * grid
    side = jnp.zeros_like(count)
    top = jnp.zeros_like(count)
    for k in range(1, grid + 1):
        side = jnp.where(count == k * k, k, side)
        top = top + jnp.where(start >= k * grid, 1, 0)
    quarter = count >> 2
    left = start - top * grid
    for ref, dim in ((col_ref, 0), (row_ref, 1)):
        place = lax.broadcasted_iota(I32, ref.shape, dim)
        row = jnp.zeros(ref.shape, I32)
        for k in range(1, grid):
            row = row + jnp.where(place >= k * grid, 1, 0)
        drow = row - top
        dcol = place - row * grid - left
        inside = (drow >= 0) & (drow < side) & (dcol >= 0) & (dcol < side) & (place < cells)
        order = drow * side + dcol
        block = jnp.zeros(ref.shape, I32)
        for k in (1, 2, 3):
            block = block + jnp.where(order >= k * quarter, 1, 0)
        slot = ((block - own) & 3) * ROWS + order - block * quarter
        ref[...] = jnp.where(inside, slot, -1)


def onehot(slot, lanes, base):
    lane = lax.broadcasted_iota(I32, (slot.shape[0], lanes), 1) + base
    return jnp.where(slot == lane, 1.0, 0.0).astype(BF)


def side_kernel(scal, slot_ref, m0, m1, m2, m3, xn_ref, tie, pos_ref, xt_ref, turned):
    place_kernel(slot_ref, m0, m1, m2, m3, pos_ref)
    own, unit = scal[0], scal[1]
    turned[...] = xn_ref[...].T
    for k, (c, y, x, r) in enumerate(ORDER):
        who = lax.rem(own + r, 4)
        e = c + 2 * x + 4 * y
        src = who * 128 + (unit ^ e) * STEP
        xt_ref[k * STEP : (k + 1) * STEP, :] = turned[pl.ds(aligned(src, STEP), STEP), :]


class Copies:
    def __init__(self, sems):
        self.sems, self.all = sems, []

    def bring(self, src, dst):
        copy = pltpu.make_async_copy(src, dst, self.sems.at[len(self.all)])
        copy.start()
        self.all.append(copy)

    def wait(self):
        for copy in self.all:
            copy.wait()


def pick_kernel(per, own, unit, pick_ref, pack_ref):
    n = pick_ref.shape[0]
    cell = lax.broadcasted_iota(I32, (n, pick_ref.shape[1]), 0)
    lane = lax.broadcasted_iota(I32, (n, pick_ref.shape[1]), 1)
    part = jnp.where(cell >= per, 1, 0) + jnp.where(cell >= 2 * per, 1, 0) + jnp.where(cell >= 3 * per, 1, 0)
    pick_ref[...] = jnp.where(lane == cell + part * (128 - per), 1.0, 0.0).astype(BF)
    big = lax.broadcasted_iota(I32, (512, n), 0)
    lane = lax.broadcasted_iota(I32, (512, n), 1)
    within = ((big >> 6) ^ unit) * STEP + (big & 15)
    a = (((big >> 4) + own) & 3) * per + within
    pack_ref[...] = jnp.where((lane == a) & (within < per), 1.0, 0.0).astype(BF)


def out_kernel(grid, scal, counts, crops, w_out, mix, msg, col_ref, row_ref, pick_ref, pack_ref, held, strip, sems):
    unit = scal[1]
    rows = held.shape[0]
    copies = Copies(sems)
    copies.bring(w_out.at[pl.ds(aligned(unit * rows, STEP), rows), :], held)
    slot_kernel(grid, scal, counts, crops, col_ref, row_ref)
    pick_kernel(mix.shape[0], scal[0], unit, pick_ref, pack_ref)
    strip[...] = jnp.zeros_like(strip)
    strip[0 : mix.shape[0], 0 : mix.shape[1]] = mix[...].astype(BF)
    copies.wait()
    msg[0:rows, :] = held[...].astype(BF)
    msg[rows:, :] = strip[pl.ds(aligned(unit * STEP, STEP), STEP), :]


def rows_kernel(scal, tok, cot, tie, m0, m1, m2, m3):
    for r, msg in enumerate((m0, m1, m2, m3)):
        to = lax.rem(scal[0] + (4 - r), 4)
        msg[0:ROWS, :] = tok[to]
        msg[HALF : HALF + ROWS, :] = cot[to]


def hold_kernel(src, tie, dst):
    dst[...] = src[...]


def stack_tied_kernel(m1, m2, m3, tie, out):
    stack_kernel(m1, m2, m3, out)


def join_kernel(p0, p1, p2, p3, out):
    for e, part in enumerate((p0, p1, p2, p3)):
        out[e] = part[...]


def join_tied_kernel(p0, p1, p2, p3, tie, out):
    join_kernel(p0, p1, p2, p3, out)


def stack_kernel(m1, m2, m3, out):
    for r, msg in enumerate((m1, m2, m3)):
        out[r] = msg[0 : out.shape[1], :]


def place(slot_ref, blocks, at, pos_ref):
    slot = slot_ref[...]
    total = None
    for r, msg in enumerate(blocks):
        part = dot(onehot(slot, ROWS, r * ROWS), msg[at : at + ROWS, :])
        total = part if total is None else total + part
    pos_ref[...] = total.astype(BF)


def place_kernel(slot_ref, m0, m1, m2, m3, pos_ref):
    place(slot_ref, (m0, m1, m2, m3), HALF, pos_ref)


ORDER = [(c, y, x, r) for c in (0, 1) for y in (0, 1) for x in (0, 1) for r in range(4)]


def norm_kernel(slot_ref, m0, m1, m2, m3, gain, shift, pos_ref, xn_ref):
    place(slot_ref, (m0, m1, m2, m3), 0, pos_ref)
    @each_tile(pos_ref.shape[0])
    def _(i):
        x = pos_ref[rows_of(i), :].astype(F32)
        cen = x - mean_rows(x)
        rstd = lax.rsqrt(mean_rows(cen * cen) + EPS)
        xn_ref[rows_of(i), :] = (cen * rstd * gain[...] + shift[...]).astype(BF)


def right_kernel(scal, slot_ref, xn_ref, b_in, g_two, s_two, wi_own, *rest):
    wi, rest = rest[:8], rest[8:]
    win, vhat_ref, rstd_ref, slope_v, vn_ref, pre = rest
    own, unit = scal[0], scal[1]
    n, gate = vhat_ref.shape
    tiles = gate // LANE
    win[pl.ds(aligned(own * 128, 128), 128), :] = wi_own[...].astype(BF)
    for e in range(8):
        for r in (1, 2, 3):
            who = lax.rem(own + r, 4)
            at = who * 128 + (unit ^ e) * STEP
            win[pl.ds(aligned(at, STEP), STEP), :] = wi[e][r - 1]

    xn = xn_ref[...]
    for k in range(tiles):
        cols = slice(k * LANE, (k + 1) * LANE)
        wide = slice(gate + k * LANE, gate + (k + 1) * LANE)
        pre[:, cols] = dot(xn, win[:, wide]) + b_in[:, wide]

    @each_tile(n)
    def _(i):
        rows = rows_of(i)
        v, slope = gelu_parts(pre[rows, :])
        slope_v[rows, :] = slope
        cen = v - mean_rows(v)
        rstd = lax.rsqrt(mean_rows(cen * cen) + EPS)
        vhat = cen * rstd
        vhat_ref[rows, :] = vhat
        rstd_ref[rows, :] = rstd
        vn = jnp.where(slot_ref[rows, :] >= 0, vhat * g_two[...] + s_two[...], 0.0)
        vn_ref[rows, :] = vn.astype(BF)


def left_kernel(xn_ref, b_in, win, *rest):
    u_ref, slope_u, pre = rest[-3:]
    n, gate = u_ref.shape
    xn = xn_ref[...]
    for k in range(gate // LANE):
        cols = slice(k * LANE, (k + 1) * LANE)
        pre[:, cols] = dot(xn, win[:, cols]) + b_in[:, cols]

    @each_tile(n)
    def _(i):
        rows = rows_of(i)
        u, slope = gelu_parts(pre[rows, :])
        u_ref[rows, :] = u
        slope_u[rows, :] = slope


def spatial_kernel(scal, pick_ref, pack_ref, xt_ref, cot_ref, u_ref, slope_u, vn_ref, b_mix, mix_own, wo_own, *rest):
    wo, rest = rest[:2], rest[2:]
    mix_ref, pre_u, sg_ref, gated, wout, keep, send, *rest = rest
    mixp, spat, gtmp = rest
    own, unit = scal[0], scal[1]
    n, gate = u_ref.shape
    tiles = gate // LANE
    out_unit = wout.shape[0] // 32
    wout[pl.ds(aligned(own * 8 * out_unit, STEP), 8 * out_unit), :] = wo_own[...].astype(BF)
    for k in range(4):
        for c in (0, 1):
            piece = 2 * k + ((unit & 1) ^ c)
            for r in (1, 2, 3):
                who = lax.rem(own + (4 - r), 4)
                at = (who * 8 + piece) * out_unit
                wout[pl.ds(aligned(at, STEP), out_unit), :] = wo[c][k, r - 1, 0:out_unit, :]
                at = who * 128 + piece * STEP
                mixp[pl.ds(aligned(at, STEP), STEP), :] = wo[c][k, r - 1, out_unit:, :]
    per, cells = mix_own.shape
    mine = aligned(own * 128, 128)
    mixp[pl.ds(mine, 128), :] = jnp.zeros((128, LANE), BF)
    mixp[pl.ds(mine, per), 0:cells] = mix_own[...].astype(BF)
    mix_ref[...] = dot(pick_ref[...], mixp[:, :n]).astype(BF)
    mix = mix_ref[...]
    for k in range(tiles):
        cols = slice(k * LANE, (k + 1) * LANE)
        sp = dot(mix, vn_ref[:, cols]) + b_mix[...]
        spat[:, cols] = sp
        gated[:, cols] = (u_ref[:, cols] * sp).astype(BF)

    cot = cot_ref[...]
    for k in range(tiles):
        cols = slice(k * LANE, (k + 1) * LANE)
        gg = dot(cot, wout[cols, :], 1, 1)
        sg_ref[:, cols] = (gg * u_ref[:, cols]).astype(BF)
        pre_u[:, cols] = (gg * spat[:, cols] * slope_u[:, cols]).astype(BF)

    low = out_unit + STEP
    for k in range(tiles):
        rows = slice(k * LANE, (k + 1) * LANE)
        gtmp[rows, :] = dot(gated[:, rows], cot, 0, 0).astype(BF)
    height = keep.shape[1] // 4
    for c, dst in ((0, keep), (1, send)):
        for e in range(4):
            for r in range(4):
                at = (lax.rem(own + r, 4) * 8 + (unit ^ (c + 2 * e))) * out_unit
                dst[e, r * height : r * height + out_unit, :] = gtmp[pl.ds(aligned(at, STEP), out_unit), :]
    gmix = dot(sg_ref[...], vn_ref[...], 1, 1).astype(BF)
    padded = dot(pack_ref[...], gmix).astype(BF)
    for c, dst in ((0, keep), (1, send)):
        for e in range(4):
            for r in range(4):
                at = (c + 2 * e) * 64 + r * STEP
                to = r * height + out_unit
                dst[e, to : to + STEP, :] = jnp.zeros((STEP, LANE), BF)
                dst[e, to : to + STEP, 0:n] = padded[at : at + STEP, :]
    for k in range(tiles):
        cols = slice(k * LANE, (k + 1) * LANE)
        part = dot(xt_ref[...], pre_u[:, cols]).astype(BF)
        for j, (c, y, x, r) in enumerate(ORDER):
            to = r * height + low + k * STEP
            (send if c else keep)[x + 2 * y, to : to + STEP, :] = part[j * STEP : (j + 1) * STEP, :]


def back_kernel(slot_ref, xt_ref, mix_ref, sg_ref, vhat_ref, rstd_ref, slope_v, g_two, pre_v, keep, send, rows_ref, vng, gain, shift):
    n, gate = vhat_ref.shape
    tiles = gate // LANE
    mix = mix_ref[...]
    for k in range(tiles):
        cols = slice(k * LANE, (k + 1) * LANE)
        vng[:, cols] = dot(mix, sg_ref[:, cols], 0, 0)
    gain[...] = jnp.zeros_like(gain)
    shift[...] = jnp.zeros_like(shift)

    @each_tile(n)
    def _(i):
        rows = rows_of(i)
        vg = jnp.where(slot_ref[rows, :] >= 0, vng[rows, :], 0.0)
        vhat = vhat_ref[rows, :]
        gain[...] += jnp.sum((vg * vhat).reshape(2, 8, gate), 0)
        shift[...] += jnp.sum(vg.reshape(2, 8, gate), 0)
        h = vg * g_two[...]
        v_grad = rstd_ref[rows, :] * (h - mean_rows(h) - vhat * mean_rows(h * vhat))
        pre_v[rows, :] = (v_grad * slope_v[rows, :]).astype(BF)

    height = keep.shape[1] // 4
    for k in range(tiles):
        cols = slice(k * LANE, (k + 1) * LANE)
        part = dot(xt_ref[...], pre_v[:, cols]).astype(BF)
        for j, (c, y, x, r) in enumerate(ORDER):
            to = r * height + k * STEP
            (send if c else keep)[x + 2 * y, to : to + STEP, :] = part[j * STEP : (j + 1) * STEP, :]
        rows_ref[k : k + 1, :] = jnp.sum(gain[:, cols], 0, keepdims=True)
        rows_ref[tiles + k : tiles + k + 1, :] = jnp.sum(shift[:, cols], 0, keepdims=True)


def token_kernel(slot_ref, slot_row, pos_ref, cot_ref, win, pre_u, pre_v, sg_ref, gated, wout, g_one, b_out, rows_ref, *rest):
    _, h0, h1, h2, h3, vec, xg, out_ref, in_ref, gain, shift = rest
    n, gate = pre_u.shape
    xg[...] = dot(pre_u[...], win[:, :gate], 1, 1) + dot(pre_v[...], win[:, gate:], 1, 1)
    gain[...] = jnp.zeros_like(gain)
    shift[...] = jnp.zeros_like(shift)
    width = xg.shape[1]

    @each_tile(n)
    def _(i):
        rows = rows_of(i)
        x = pos_ref[rows, :].astype(F32)
        cen = x - mean_rows(x)
        rstd = lax.rsqrt(mean_rows(cen * cen) + EPS)
        xhat = cen * rstd
        g = xg[rows, :]
        gain[...] += jnp.sum((g * xhat).reshape(2, 8, width), 0)
        shift[...] += jnp.sum(g.reshape(2, 8, width), 0)
        h = g * g_one[...]
        x_grad = rstd * (h - mean_rows(h) - xhat * mean_rows(h * xhat))
        total = cot_ref[rows, :].astype(F32) + x_grad
        in_ref[rows, :] = jnp.where(slot_ref[rows, :] >= 0, total, 0.0).astype(BF)

    branch = dot(gated[...], wout[...]) + b_out[...]
    out_ref[...] = jnp.where(slot_ref[...] >= 0, pos_ref[...].astype(F32) + branch, 0.0).astype(BF)
    for r, dst in enumerate((h0, h1, h2, h3)):
        spot = lax.broadcasted_iota(I32, (ROWS, n), 0) + r * ROWS
        pick = jnp.where(slot_row[...] == spot, 1.0, 0.0).astype(BF)
        dst[0:ROWS, :] = dot(pick, out_ref[...]).astype(BF)
        dst[HALF : HALF + ROWS, :] = dot(pick, in_ref[...]).astype(BF)

    ones = jnp.ones((8, n), BF)
    tiles = gate // LANE
    vec[0:1, :] = jnp.sum(gain[...], 0, keepdims=True)
    vec[1:2, :] = jnp.sum(shift[...], 0, keepdims=True)
    for k in range(tiles):
        cols = slice(k * LANE, (k + 1) * LANE)
        vec[2 + k : 3 + k, :] = dot(ones, pre_u[:, cols])[0:1]
        vec[2 + tiles + k : 3 + tiles + k, :] = dot(ones, pre_v[:, cols])[0:1]
    at = 2 + 2 * tiles
    vec[at : at + 2 * tiles, :] = rows_ref[...]
    at += 2 * tiles
    cells = 4 * ROWS
    lane = lax.broadcasted_iota(I32, (1, LANE), 1)
    last = pltpu.roll(dot(ones, cot_ref[...])[0:1], cells, 1)
    vec[at : at + 1, 0:n] = dot(jnp.ones((8, gate), BF), sg_ref[...], 1, 1)[0:1]
    vec[at : at + 1, :] = jnp.where(lane < cells, vec[at : at + 1, :], last)
    vec[at + 1 : at + 2, :] = jnp.where(lane < cells, last, 0.0)


def put_vec(ref, at, v):
    ref[at : at + STEP, :] = v.astype(BF)


def get_vec(ref, at):
    return ref[at : at + STEP, :].astype(F32)


def core_kernel(keep, got, own, s1, s2, s3):
    for e, dst in enumerate((own, s1, s2, s3)):
        dst[...] = (keep[e].astype(F32) + got[e].astype(F32)).astype(dst.dtype)


def core_vec_kernel(keep, got, vec, vec_got, tie, own, s1, s2, s3, vec_own):
    rows = own.shape[0]
    total = vec[...] + vec_got[...]
    put_vec(vec_own, 0, total)
    for e, dst in enumerate((own, s1, s2, s3)):
        dst[0:rows, :] = (keep[e].astype(F32) + got[e].astype(F32)).astype(dst.dtype)
        if e:
            put_vec(dst, rows, total)


def plane_kernel(own, g1, g2, g3, z0, z1, z2, z3):
    rows = z0.shape[0]
    for r, dst in enumerate((z0, z1, z2, z3)):
        at = slice(r * rows, (r + 1) * rows)
        total = (own[at, :] + g1[at, :].astype(F32)) + (g2[at, :].astype(F32) + g3[at, :].astype(F32))
        dst[...] = total.astype(dst.dtype)


def plane_vec_kernel(own, vec_own, g1, g2, g3, tie, z0, z1, z2, z3, vec_out):
    rows, at = z0.shape[0], own.shape[0]
    vec = (get_vec(vec_own, 0) + get_vec(g1, at)) + (get_vec(g2, at) + get_vec(g3, at))
    put_vec(vec_out, 0, vec)
    for r, dst in enumerate((z0, z1, z2, z3)):
        at = slice(r * rows, (r + 1) * rows)
        total = (own[at, :] + g1[at, :].astype(F32)) + (g2[at, :].astype(F32) + g3[at, :].astype(F32))
        dst[0:rows, :] = total.astype(dst.dtype)
        if r:
            put_vec(dst, rows, vec)


def patch_kernel(own, g1, g2, g3, out):
    rows = own.shape[0]
    total = own[...]
    for g in (g1, g2, g3):
        total = total + g[0:rows, :].astype(F32)
    out[...] = total.astype(out.dtype)


def patch_vec_kernel(scal, own, vec_own, g1, g2, g3, tie, tie_home, out, vec_out, held):
    patch_kernel(own, g1, g2, g3, out)
    rows = own.shape[0]
    me = scal[0]
    held[me] = get_vec(vec_own, 0)
    for r, g in enumerate((g1, g2, g3), 1):
        held[lax.rem(me + (4 - r), 4)] = get_vec(g, rows)
    vec_out[...] = (held[0] + held[1]) + (held[2] + held[3])


def home_kernel(scal, h0, h1, h2, h3, out_ref, grad_ref, held):
    for r, h in enumerate((h0, h1, h2, h3)):
        m = lax.rem(scal[0] + (4 - r), 4)
        held[m] = h[0:ROWS, :]
        grad_ref[m, :, 0, :] = h[HALF : HALF + ROWS, :].astype(F32)
    for m in range(4):
        out_ref[:, m, :] = held[m]


def update_kernel(rates, first, second, *rest):
    olds, rest = rest[:9], rest[9:]
    news, rest = rest[:9], rest[9:]
    made, sems = rest[:9], rest[9]
    copies = Copies(sems)
    out_unit = olds[3].shape[0] // 8
    low = out_unit + STEP

    def step(which, rows, cols, grads):
        old, new = olds[3 * which : 3 * which + 3], made[3 * which : 3 * which + 3]
        at = (slice(*rows), slice(*cols))
        fresh = nesterov(old[0][at], grads.astype(F32), old[1][at], old[2][at], rates[which])
        for ref, value in zip(new, fresh):
            ref[at] = value

    def send(which):
        for j in range(3 * which, 3 * which + 3):
            copies.bring(made[j], news[j])

    width = olds[3].shape[1]
    for u in range(8):
        step(1, (u * out_unit, (u + 1) * out_unit), (0, width), first[u, 0:out_unit, :])
    send(1)
    mix_rows, cells = olds[6].shape
    for u in range(-(-mix_rows // STEP)):
        rows = min(STEP, mix_rows - u * STEP)
        step(2, (u * STEP, u * STEP + rows), (0, cells), first[u, out_unit : out_unit + rows, 0:cells])
    send(2)
    tiles = olds[0].shape[1] // LANE
    for u in range(8):
        for k in range(tiles):
            if k < tiles // 2:
                grads = first[u, low + k * STEP : low + (k + 1) * STEP, :]
            else:
                j = k - tiles // 2
                grads = second[u, j * STEP : (j + 1) * STEP, :]
            step(0, (u * STEP, (u + 1) * STEP), (k * LANE, (k + 1) * LANE), grads)
    send(0)
    copies.wait()


VM = pl.BlockSpec(memory_space=pltpu.VMEM)
SM = pl.BlockSpec(memory_space=pltpu.SMEM)
ANY = pl.BlockSpec(memory_space=pl.ANY)


def call(body, ins, outs, scratch=(), specs=None, out_specs=None, flops=100_000_000, limit=16, name=None):
    moved = sum(math.prod(a.shape) * a.dtype.itemsize for a in ins)
    return pl.pallas_call(
        body,
        out_shape=[jax.ShapeDtypeStruct(s, d) for s, d in outs],
        in_specs=specs or [VM] * len(ins),
        out_specs=out_specs or [VM] * len(outs),
        scratch_shapes=list(scratch),
        compiler_params=pltpu.CompilerParams(vmem_limit_bytes=limit * 2**20),
        cost_estimate=pl.CostEstimate(flops=flops, bytes_accessed=moved, transcendentals=0),
        name=name,
    )(*ins)


def rest_of_img(total):
    mask = 8
    while mask < lax.axis_size("img"):
        total = total + swap(total, mask)
        mask *= 2
    return total


def img_gather(arr):
    size = lax.axis_size("img")
    groups = [[g * 8 + k for k in range(8)] for g in range(size // 8)]
    return lax.all_gather(arr, "img", axis_index_groups=groups)


def shards(
    tokens,
    cotangent,
    patch_count,
    crop_index,
    in_weight,
    in_moment,
    in_average,
    out_weight,
    out_moment,
    out_average,
    spatial_weight,
    spatial_moment,
    spatial_average,
    vectors,
    vector_moment,
    vector_average,
):
    p = lax.axis_index("patch")
    unit = lax.axis_index("img") % 8
    micro_count, slot_count, row_count, width = tokens.shape
    hidden = in_weight.shape[1]
    gate = hidden // 2
    mix_rows, cells = spatial_weight.shape
    assert micro_count == lax.axis_size("patch") == 4 and slot_count == 1
    assert width == LANE and in_weight.shape[0] == 128 and row_count == mix_rows == 81
    grid = math.isqrt(cells)
    n = -(-cells // STEP) * STEP
    in_unit = in_weight.shape[0] // 8
    out_unit = out_weight.shape[0] // 8
    low = out_unit + STEP
    side_rows = in_unit * gate // LANE
    scal = jnp.stack([p, unit]).astype(I32)

    def over_plane(base):
        near = swap(base, XBIT)
        return [base, near, swap(base, YBIT), swap(near, YBIT)]

    wi_piece = lax.dynamic_slice_in_dim(in_weight, unit * in_unit, in_unit, 0).astype(BF)

    msg, slot_col, slot_row, pick, pack = call(
        functools.partial(out_kernel, grid),
        [scal, patch_count.reshape(1, 4), crop_index, out_weight, spatial_weight],
        [((low, LANE), BF), ((n, 1), I32), ((1, n), I32), ((n, 512), BF), ((512, n), BF)],
        [pltpu.VMEM((out_unit, width), F32), pltpu.VMEM((128, LANE), BF), pltpu.SemaphoreType.DMA((1,))],
        specs=[SM, VM, VM, ANY, VM],
        limit=8,
        name="prep_out",
    )
    (base_in,) = call(
        stack_tied_kernel,
        [turn(wi_piece, -r) for r in (1, 2, 3)] + [msg],
        [((3, in_unit, hidden), BF)],
        specs=[VM] * 3 + [ANY],
        limit=8,
        name="stack_i",
    )
    plane_in = over_plane(base_in)
    wi = [arr for part in plane_in for arr in (part, swap(part, CORE))]
    (base,) = call(
        stack_tied_kernel,
        [turn(msg, r) for r in (1, 2, 3)] + [base_in],
        [((3, low, LANE), BF)],
        specs=[VM] * 3 + [ANY],
        limit=8,
        name="stack_o",
    )
    got = call(
        rows_kernel,
        [scal, tokens.reshape(4, row_count, width), cotangent.reshape(4, row_count, width), base_in],
        [((HALF + row_count, width), BF)] * 4,
        specs=[SM, VM, VM, ANY],
        limit=8,
        name="prep_rows",
    )
    got = [got[0]] + [turn(m, -r) for r, m in enumerate(got[1:], 1)]
    (held,) = call(hold_kernel, [base, plane_in[2]], [((3, low, LANE), BF)], specs=[VM, ANY], limit=8, name="hold_out")
    planes = [[8 * g + c + 2 * k for k in range(4)] for g in range(lax.axis_size("img") // 8) for c in (0, 1)]
    joined = lax.all_gather(held, "img", axis_index_groups=planes)
    joined_got = swap(joined, CORE)

    bounds = [width, width, hidden, gate, gate, cells, width]
    pieces = []
    offset = 0
    for length in bounds:
        pieces.append(vectors[None, offset : offset + length])
        offset += length
    g_one, s_one, b_in, g_two, s_two, b_mix, b_out = pieces
    b_mix = jnp.pad(b_mix[0], (0, n - cells))[:, None]

    pos, xn = call(
        norm_kernel,
        [slot_col, *got, g_one, s_one],
        [((n, width), BF), ((n, width), BF)],
        name="norm_in",
    )
    sized = lambda kind: ((n, gate), kind)
    win, vhat, rstd, slope_v, vn = call(
        right_kernel,
        [scal, slot_col, xn, b_in, g_two, s_two, in_weight, *wi],
        [((width, hidden), BF), sized(F32), ((n, 1), F32), sized(F32), sized(BF)],
        [pltpu.VMEM((n, gate), F32)],
        specs=[SM] + [VM] * 14,
        flops=1_500_000_000,
        limit=20,
        name="right",
    )
    cot_pos, xt = call(
        side_kernel,
        [scal, slot_col, *got, xn, vn],
        [((n, width), BF), ((width, n), BF)],
        [pltpu.VMEM((width, n), BF)],
        specs=[SM] + [VM] * 6 + [ANY],
        name="place_cot",
    )
    u, slope_u = call(
        left_kernel,
        [xn, b_in, win, joined_got],
        [sized(F32), sized(F32)],
        [pltpu.VMEM((n, gate), F32)],
        specs=[VM] * 3 + [ANY],
        flops=1_000_000_000,
        limit=16,
        name="left",
    )
    packed = ((4, 4 * (low + side_rows), LANE), BF)
    mix, pre_u, sg, gated, wout, keep_a, send_a = call(
        spatial_kernel,
        [scal, pick, pack, xt, cot_pos, u, slope_u, vn, b_mix, spatial_weight, out_weight, joined, joined_got],
        [((n, n), BF), sized(BF), sized(BF), sized(BF), ((gate, width), BF), packed, packed],
        [
            pltpu.VMEM((512, LANE), BF),
            pltpu.VMEM((n, gate), F32),
            pltpu.VMEM((gate, width), BF),
        ],
        specs=[SM] + [VM] * 12,
        flops=4_000_000_000,
        limit=24,
        name="spatial",
    )
    core_a = swap(send_a, CORE)
    half = ((4, 4 * side_rows, LANE), BF)
    pre_v, keep_b, send_b, rows_b = call(
        back_kernel,
        [slot_col, xt, mix, sg, vhat, rstd, slope_v, g_two],
        [sized(BF), half, half, ((6, LANE), F32)],
        [pltpu.VMEM((n, gate), F32), pltpu.VMEM((8, gate), F32), pltpu.VMEM((8, gate), F32)],
        flops=2_000_000_000,
        limit=20,
        name="back",
    )
    core_b = swap(send_b, CORE)
    rows_a, rows_b4 = 4 * (low + side_rows), 4 * side_rows
    own_a, *send_a = call(
        core_kernel, [keep_a, core_a], [((rows_a, LANE), F32)] + [((rows_a, LANE), BF)] * 3, limit=12, name="core_a"
    )
    plane_a = [swap(s, m) for s, m in zip(send_a, (2, 4, 6))]
    *home, vec = call(
        token_kernel,
        [slot_col, slot_row, pos, cot_pos, win, pre_u, pre_v, sg, gated, wout, g_one, b_out, rows_b, send_a[2]],
        [((HALF + row_count, width), BF)] * 4 + [((STEP, LANE), F32)],
        [
            pltpu.VMEM((n, width), F32),
            pltpu.VMEM((n, width), BF),
            pltpu.VMEM((n, width), BF),
            pltpu.VMEM((8, width), F32),
            pltpu.VMEM((8, width), F32),
        ],
        specs=[VM] * 13 + [ANY],
        flops=2_000_000_000,
        limit=20,
        name="token_grad",
    )
    vec_got = swap(vec, CORE)
    own_b, *send_b, vec_own = call(
        core_vec_kernel,
        [keep_b, core_b, vec, vec_got, send_a[0]],
        [((rows_b4, LANE), F32)] + [((rows_b4 + STEP, LANE), BF)] * 3 + [((STEP, LANE), BF)],
        specs=[VM] * 4 + [ANY],
        name="core_b",
    )
    plane_b = [swap(s, m) for s, m in zip(send_b, (2, 4, 6))]
    home = [home[0]] + [turn(h, r) for r, h in enumerate(home[1:], 1)]
    out_tokens, in_grad = call(
        home_kernel,
        [scal, *home],
        [((row_count, 4, width), BF), ((4, row_count, 1, width), F32)],
        [pltpu.VMEM((4, row_count, width), BF)],
        specs=[SM] + [VM] * 4,
        limit=8,
        name="home",
    )
    z_rows = low + side_rows
    own_a, *patch_a = call(
        plane_kernel, [own_a, *plane_a], [((z_rows, LANE), F32)] + [((z_rows, LANE), BF)] * 3, name="plane_a"
    )
    got_a = [turn(z, r) for r, z in enumerate(patch_a, 1)]
    own_b, *patch_b, vec_own = call(
        plane_vec_kernel,
        [own_b, vec_own, *plane_b, patch_a[0]],
        [((side_rows, LANE), F32)] + [((side_rows + STEP, LANE), BF)] * 3 + [((STEP, LANE), BF)],
        specs=[VM] * 5 + [ANY],
        name="plane_b",
    )
    got_b = [turn(z, r) for r, z in enumerate(patch_b, 1)]
    kind = BF if lax.axis_size("img") == 8 else F32
    (first,) = call(patch_kernel, [own_a, *got_a], [((z_rows, LANE), kind)], name="patch_a")
    first = img_gather(rest_of_img(first).astype(BF))
    second, vec_sum = call(
        patch_vec_kernel,
        [scal, own_b, vec_own, *got_b, first, in_grad],
        [((side_rows, LANE), kind), ((STEP, LANE), F32)],
        [pltpu.VMEM((4, STEP, LANE), F32)],
        specs=[SM] + [VM] * 5 + [ANY] * 2,
        name="patch_b",
    )
    second = img_gather(rest_of_img(second).astype(BF))
    vec_sum = rest_of_img(vec_sum).reshape(STEP * LANE)

    vec_sum = vec_sum[: vectors.shape[0]]

    images = micro_count * slot_count * lax.axis_size("img")
    rate_in, rate_out, rate_mix, rate_vec = step_rates(images, width, gate, cells)
    olds = [in_weight, in_moment, in_average, out_weight, out_moment, out_average]
    olds += [spatial_weight, spatial_moment, spatial_average]
    news = call(
        functools.partial(update_kernel, (rate_in, rate_out, rate_mix)),
        [first, second, *olds],
        [(a.shape, F32) for a in olds],
        [pltpu.VMEM(a.shape, F32) for a in olds] + [pltpu.SemaphoreType.DMA((9,))],
        specs=[VM] * 11,
        out_specs=[ANY] * 9,
        limit=20,
        name="update",
    )
    vec_new = nesterov(vectors, vec_sum, vector_moment, vector_average, rate_vec)
    return (out_tokens.transpose(1, 0, 2).reshape(tokens.shape), in_grad.transpose(0, 2, 1, 3), *news, *vec_new)


def solution(mesh):
    rows = P("patch", None)
    act = P(None, "img", "patch", None)
    return jax.shard_map(
        shards,
        mesh=mesh,
        in_specs=(act, act, P(None, "img"), P(None, "img", None), *([rows] * 9), P(), P(), P()),
        out_specs=(act, act, *([rows] * 9), P(), P(), P()),
        check_vma=False,
    )
```
